128 devices in a mesh: tx: 16 (over y, z), ty: 8 (over x, core).
Axes of the slice: x: 4, y: 4, z: 4, core: 2. Of those that a mesh axis runs over, the one named last changes fastest.
Arguments:
- increments: bfloat16 [1536, 1536, 128], P('ty', 'tx'), may hold values from -6 to 6
- lengths: float32 [4, 3], replicated, may hold values from 2 to 768
- lat_class: int32 [1536], replicated, may hold values from 0 to 3
- slab_owner: int32 [128], replicated, may hold values from 0 to 127, as said below
- level_sigma: float32 [128], replicated, may hold values from 0.5 to 4
Outputs:
- smoothed: bfloat16 [1536, 1536, 128], P('ty', 'tx')
- peak_table: float32 [128, 2], P(('tx', 'ty'))
The draws below stay inside these ranges and needn't reach their ends.
Inputs may be any that keep to these rules, and one draw needn't show every extreme that they name: `slab_owner`: no device owns more than 2 slabs; some devices own exactly 2, some none.
All inputs are finite; a program needn't handle non-finite values.
Results may differ from the reference program's by a relative error of at most 0.006.
Values may be sent and summed in bfloat16 or wider, within the bound.
No kernel may reach another device: no remote copies, remote signals or barrier semaphores. Data moves between devices by JAX's collectives and lax.ppermute only.
A program may use at most 192 MiB of HBM per device.

```python
import math
import jax
import jax.numpy as jnp
from jax import lax

NX = 1536
NY = 1536
PANEL = 128
NCLASS = 4
MOST = 2
SLABS = 128


def draw_slab_owner(key, part):
    key = jax.random.fold_in(key, 11)
    first_key, second_key = jax.random.split(key)
    order = jax.random.permutation(first_key, SLABS)
    quarter = SLABS // 4
    listed = jnp.concatenate([order[:quarter], order[:quarter], order[quarter:3 * quarter]])
    mixing = jax.random.permutation(second_key, SLABS)
    return listed[mixing].astype(jnp.int32)


def place_ends(values, key, least, high):
    dims = values.shape
    index_at = [jax.random.randint(jax.random.fold_in(key, axis), (), 0, dims[axis]) for axis in range(len(dims))]
    values = values.at[tuple(index_at)].set(least)
    longest = dims.index(max(dims))
    index_at[longest] = (index_at[longest] + 1) % dims[longest]
    return values.at[tuple(index_at)].set(high)


def shard_levels(stream_key, dims, cuts, least, high):
    factor_of = 1.0
    for dim, parts in cuts:
        draws = jax.random.uniform(jax.random.fold_in(jax.random.fold_in(stream_key, 6), dim), (parts,), jnp.float32, least / len(cuts), high / len(cuts))
        factor_of = factor_of * jnp.repeat(jnp.exp(draws), dims[dim] // parts).reshape((-1,) + (1,) * (len(dims) - 1 - dim))
    return factor_of


def centred(own_key, dims, deviation, limit, cuts=(), kind=jnp.bfloat16):
    drawn = jax.random.normal(own_key, dims, jnp.float32) * deviation
    if len(cuts) > 0:
        drawn = shard_levels(own_key, dims, cuts, -0.22, 0.18) * drawn
    return jnp.clip(drawn, min=-limit, max=limit).astype(kind)


def setup_inputs(seed: int = 0) -> dict:
    key_of = jax.random.split(jax.random.key(seed), 6)
    increments = centred(key_of[0], (NY, NX, SLABS), 1.0, 6.0, ((0, 8), (1, 16)))
    lengths = jnp.clip(jnp.exp(jax.random.uniform(key_of[1], (NCLASS, 3), jnp.float32, math.log(2.0), math.log(768.0))), 2.0, 768.0)
    lat_class = place_ends(jax.random.randint(key_of[2], (NY,), 0, NCLASS), jax.random.fold_in(key_of[2], 1), 0, NCLASS - 1).astype(jnp.int32)
    slab_owner = draw_slab_owner(jax.random.fold_in(key_of[5], 71), 0)
    level_sigma = jnp.clip(jnp.exp(jax.random.uniform(key_of[4], (SLABS,), jnp.float32, math.log(0.5), math.log(4.0))), 0.5, 4.0)
    return {"increments": increments, "lengths": lengths, "lat_class": lat_class, "slab_owner": slab_owner, "level_sigma": level_sigma}


SCALE_WEIGHTS = (0.5, 0.35, 0.25)

def multiply(spec, left, right):
    return jnp.einsum(spec, left.astype(jnp.float32), right.astype(jnp.float32), precision=lax.Precision.HIGHEST)

def slot_ranks(slab_owner):
    slab_total = slab_owner.shape[0]
    equal_owner = slab_owner[:, None] == slab_owner[None, :]
    row_index = lax.broadcasted_iota(jnp.int32, (slab_total, slab_total), 0)
    col_index = lax.broadcasted_iota(jnp.int32, (slab_total, slab_total), 1)
    return lax.optimization_barrier(jnp.sum(jnp.where(equal_owner & (col_index < row_index), 1, 0), axis=1)).astype(jnp.int32)

def gains(log_rate, forward):
    rate = jnp.exp(log_rate)
    return jnp.sqrt(1.0 - rate * rate) if forward else 1.0 - rate

def scale_tables(log_rate, gain_value, forward):
    panel = log_rate.shape[-1]
    weights = jnp.array(SCALE_WEIGHTS, jnp.float32)
    if forward:
        level_sum = jnp.cumsum(log_rate, axis=-1)
        edge_level = level_sum[..., -1]
    else:
        level_sum = jnp.flip(jnp.cumsum(jnp.flip(log_rate, -1), axis=-1), -1)
        edge_level = level_sum[..., 0]
    in_index = lax.broadcasted_iota(jnp.int32, (panel, panel), 0)
    out_index = lax.broadcasted_iota(jnp.int32, (panel, panel), 1)
    allowed = in_index <= out_index if forward else in_index >= out_index
    level_gap = level_sum[..., None, :] - level_sum[..., :, None]
    term_table = jnp.where(allowed, jnp.exp(jnp.where(allowed, level_gap, 0.0)), 0.0) * gain_value[..., :, None]
    inner_map = lax.optimization_barrier(jnp.sum(term_table * weights[:, None, None], axis=-3))
    end_map = gain_value * jnp.exp(edge_level[..., None] - level_sum)
    carry_map = weights[:, None] * jnp.exp(level_sum)
    decay_rate = jnp.exp(edge_level)
    return (inner_map, end_map, carry_map, decay_rate)

def chain_states(end_terms, decay_rate, reverse):

    def advance(carried, pair_item):
        return (pair_item[1] * carried + pair_item[0], carried)
    start = jnp.zeros(end_terms.shape[1:], end_terms.dtype)
    _, before = lax.scan(advance, start, (end_terms, decay_rate), reverse=reverse)
    return before

def x_tables(log_table, forward):
    classes = log_table.shape[0]
    log_rate = jnp.broadcast_to(log_table[:, :, None], (classes, 3, PANEL))
    inner_map, end_map, carry_map, decay_rate = scale_tables(log_rate, gains(log_rate, forward), forward)
    table_stack = jnp.concatenate([inner_map, jnp.swapaxes(end_map, -1, -2)], axis=-1)
    table_stack = table_stack.reshape(classes * PANEL, PANEL + 3).astype(jnp.bfloat16)
    return (table_stack, carry_map.reshape(classes * 3, PANEL), decay_rate)

def filter_x(row_data, onehot, tables, forward):
    table_stack, carry_flat, decay_rate = tables
    classes = onehot.shape[1]
    row_total, width = row_data.shape
    panels = width // PANEL
    pieces = row_data.reshape(row_total, panels, PANEL)
    masked = (pieces[:, :, None, :] * onehot.astype(jnp.bfloat16)[:, None, :, None]).reshape(row_total, panels, classes * PANEL)
    product = multiply('bnj,jm->bnm', masked, table_stack)
    within = product[:, :, :PANEL]
    end_terms = jnp.moveaxis(product[:, :, PANEL:], 1, 0)
    row_decay = lax.optimization_barrier(jnp.sum(onehot[:, :, None] * decay_rate[None], axis=1))
    before = chain_states(end_terms, jnp.broadcast_to(row_decay, end_terms.shape), not forward)
    spread = (jnp.moveaxis(before, 0, 1)[:, :, None, :] * onehot[:, None, :, None]).reshape(row_total, panels, classes * 3)
    correction = jnp.einsum('bnq,qi->bni', spread, carry_flat, precision=lax.Precision.HIGHEST)
    return (within + correction).reshape(row_total, width)

def filter_y(slab_data, lat_onehot, log_table, forward):
    height, width = slab_data.shape
    panels = height // PANEL
    log_lat = lax.optimization_barrier(jnp.sum(lat_onehot[:, :, None] * log_table[None], axis=1))
    log_rate = jnp.swapaxes(log_lat.reshape(panels, PANEL, 3), 1, 2)
    inner_map, end_map, carry_map, decay_rate = scale_tables(log_rate, gains(log_rate, forward), forward)
    table_stack = jnp.concatenate([jnp.swapaxes(inner_map, -1, -2), end_map], axis=-2).astype(jnp.bfloat16)
    pieces = slab_data.reshape(panels, PANEL, width)
    product = multiply('pmj,pjx->pmx', table_stack, pieces)
    within = product[:, :PANEL]
    before = chain_states(product[:, PANEL:], jnp.broadcast_to(decay_rate[:, :, None], (panels, 3, width)), not forward)
    correction = jnp.einsum('pki,pkx->pix', carry_map, before, precision=lax.Precision.HIGHEST)
    return (within + correction).reshape(height, width)

def smooth_slab(slab_data, slab_scale, lat_onehot, log_table):
    height, width = slab_data.shape
    block = math.gcd(height, 512)
    onehot_blocks = lat_onehot.reshape(height // block, block, lat_onehot.shape[1])

    def along_x(data, forward):
        tables = x_tables(log_table, forward)
        blocks = data.reshape(height // block, block, width)
        done = lax.map(lambda pair_item: filter_x(pair_item[0], pair_item[1], tables, forward), (blocks, onehot_blocks))
        return done.reshape(height, width)
    pass_one = along_x(slab_data, True).astype(jnp.bfloat16)
    pass_two = along_x(pass_one, False).astype(jnp.bfloat16)
    pass_three = filter_y(pass_two, lat_onehot, log_table, True).astype(jnp.bfloat16)
    pass_four = filter_y(pass_three, lat_onehot, log_table, False)
    scaled = slab_scale * pass_four
    return (scaled.astype(jnp.bfloat16), jnp.max(jnp.abs(scaled)))

def reference(increments, lengths, lat_class, slab_owner, level_sigma):
    log_table = -1.0 / lengths
    lat_onehot = (lat_class[:, None] == jnp.arange(NCLASS, dtype=jnp.int32)[None, :]).astype(jnp.float32)
    slabs_first = jnp.moveaxis(increments, 2, 0)
    smoothed, peaks = lax.map(lambda pair_item: smooth_slab(pair_item[0], pair_item[1], lat_onehot, log_table), (slabs_first, level_sigma))
    slot_rank = slot_ranks(slab_owner)
    peak_table = jnp.zeros((SLABS, MOST), jnp.float32).at[slab_owner, slot_rank].set(peaks)
    return (jnp.moveaxis(smoothed, 0, 2), peak_table)
```

```python
import functools

import jax
import jax.numpy as jnp
from jax import lax
from jax.experimental import pallas as pl
from jax.experimental.pallas import tpu as pltpu
from jax.sharding import PartitionSpec as P

NCLASS = 4
MOST = 2
SCALE_WEIGHTS = (0.5, 0.35, 0.25)
LOG, RATE, FWD, BWD, INV, ROW = 0, 3, 6, 9, 12, 32
GROUP = 8
BLOCK = 16
CHUNK = 48
F32, BF16 = jnp.float32, jnp.bfloat16


def iota(shape, axis):
    return lax.broadcasted_iota(jnp.int32, shape, axis)


def class_scalars(lengths):
    log_rate = -1.0 / lengths
    rate = jnp.exp(log_rate)
    weights = jnp.array(SCALE_WEIGHTS, F32)[None, :]
    forward = weights * jnp.sqrt(1.0 - rate * rate)
    backward = weights * (1.0 - rate)
    inverse = -1.0 / jnp.expm1(log_rate[:, :, None] + log_rate[:, None, :])
    row = jnp.concatenate(
        [log_rate, rate, forward, backward, inverse.reshape(NCLASS, 9)], axis=1
    )
    return jnp.pad(row, ((0, 0), (0, ROW - row.shape[1]))).reshape(-1)


def class_reader(tab_ref, c):
    return lambda at: tab_ref[c * ROW + at]


def ends_kernel(lat_ref, tab_ref, v_ref, e_ref, w_ref):
    block, width, _ = v_ref.shape
    step = pl.program_id(0)
    first = (lax.axis_index("ty") * pl.num_programs(0) + step) * block

    @pl.when(step == 0)
    def _():
        row = iota((GROUP, width), 0)
        at = iota((GROUP, width), 1).astype(F32)
        for c in range(NCLASS):
            get = class_reader(tab_ref, c)
            total = jnp.zeros((GROUP, width), F32)
            for k in range(3):
                fwd_end = get(FWD + k) * jnp.exp(get(LOG + k) * (width - 1 - at))
                total = jnp.where(row == k, fwd_end, total)
            for q in range(3):
                back = jnp.zeros((GROUP, width), F32)
                for k in range(3):
                    both = get(LOG + k) + get(LOG + q)
                    back += (get(FWD + k) * get(INV + 3 * q + k)) * (
                        1.0 - jnp.exp(both * (width - at))
                    )
                back = back * get(BWD + q) * jnp.exp(get(LOG + q) * at)
                total = jnp.where(row == 3 + q, back, total)
            w_ref[c] = jnp.concatenate([total, jnp.zeros_like(total)], axis=0).astype(BF16)

    for r in range(0, block, 2):
        pair = [
            jnp.dot(w_ref[lat_ref[first + r + s]], v_ref[r + s], preferred_element_type=F32)[:GROUP]
            for s in range(2)
        ]
        e_ref[pl.ds(r * GROUP, 2 * GROUP), :] = jnp.concatenate(pair, axis=0).astype(BF16)


def scan_kernel(width, height, lat_ref, tab_ref, e_ref, c_ref, decay_ref, cross_ref, f_ref):
    devices, lines, lanes = e_ref.shape
    rows = lines // GROUP
    first = lax.axis_index("ty") * height + lax.axis_index("tx") * rows
    row = iota((GROUP, lanes), 0)
    lane = iota((GROUP, lanes), 1)
    decay, cross = [], []
    for c in range(NCLASS):
        get = class_reader(tab_ref, c)
        log = jnp.zeros((GROUP, lanes), F32)
        mix = jnp.zeros((GROUP, lanes), F32)
        for k in range(3):
            log = jnp.where((row == k) | (row == 3 + k), get(LOG + k), log)
            for q in range(3):
                both = get(LOG + k) + get(LOG + q)
                value = (get(BWD + q) * get(RATE + k) * get(INV + 3 * q + k)) * (
                    1.0 - jnp.exp(jnp.full((GROUP, lanes), both * width, F32))
                )
                mix = jnp.where((row == 3 + q) & (lane % GROUP == k), value, mix)
        decay.append(jnp.exp(log * width))
        cross.append(mix)
    for r in range(rows):
        c = lat_ref[first + r]
        d, m = decay[0], cross[0]
        for other in range(1, NCLASS):
            d = jnp.where(c == other, decay[other], d)
            m = jnp.where(c == other, cross[other], m)
        decay_ref[pl.ds(r * GROUP, GROUP), :] = d
        cross_ref[pl.ds(r * GROUP, GROUP), :] = jnp.where(lane // GROUP == r, m, 0.0)
    decay = decay_ref[...]
    cross = cross_ref[:, :lines].astype(BF16)
    state = jnp.zeros((lines, lanes), F32)
    for t in range(devices):
        f_ref[t] = state
        state = decay * state + e_ref[t].astype(F32)
    kind = iota((lines, lanes), 0) % GROUP
    state = jnp.zeros((lines, lanes), F32)
    for t in range(devices - 1, -1, -1):
        ahead = f_ref[t]
        c_ref[t] = jnp.where(kind < 3, ahead, jnp.where(kind < 6, state, 0.0)).astype(BF16)
        if t > 0:
            turned = jnp.dot(cross, ahead.astype(BF16), preferred_element_type=F32)
            state = decay * state + e_ref[t].astype(F32) + turned


def fill_x_tables(tab_ref, m_ref, width):
    depth = m_ref.shape[2]
    out_at = iota((width, depth), 0).astype(F32)
    lane = iota((width, depth), 1)
    in_at = lane.astype(F32)
    far = jnp.maximum(out_at, in_at)
    later = out_at >= in_at
    gap = jnp.abs(out_at - in_at)
    for c in range(NCLASS):
        get = class_reader(tab_ref, c)
        near_power = [jnp.exp(get(LOG + k) * gap) for k in range(3)]
        rest_power = [jnp.exp(get(LOG + k) * jnp.maximum(width - far, 0.0)) for k in range(3)]
        own_rest = [jnp.exp(get(LOG + k) * (width - out_at)) for k in range(3)]
        inner = jnp.zeros((width, depth), F32)
        carried = [jnp.zeros((width, depth), F32) for _ in range(3)]
        for q in range(3):
            for k in range(3):
                inverse = get(INV + 3 * q + k)
                inner += (get(FWD + k) * get(BWD + q) * inverse) * (
                    jnp.where(later, near_power[k], near_power[q])
                    * (1.0 - rest_power[k] * rest_power[q])
                )
                carried[k] += (get(BWD + q) * inverse) * (1.0 - own_rest[k] * own_rest[q])
        inner = jnp.where(lane < width, inner, 0.0)
        for k in range(3):
            carried[k] = carried[k] * jnp.exp(get(LOG + k) * (out_at + 1.0))
        for parity in range(2):
            at = width + GROUP * parity
            table = inner
            for k in range(3):
                table = jnp.where(lane == at + k, carried[k], table)
                table = jnp.where(lane == at + 3 + k, own_rest[k], table)
            m_ref[2 * c + parity] = table.astype(BF16)


def middle_kernel(lat_ref, tab_ref, v_ref, c_ref, p_ref, e_ref, m_ref, wide_ref, f_ref, h_ref, q_ref):
    block, width, lanes = v_ref.shape
    step = pl.program_id(0)
    first = (lax.axis_index("ty") * pl.num_programs(0) + step) * block

    @pl.when(step == 0)
    def _():
        fill_x_tables(tab_ref, m_ref, width)
        f_ref[...] = jnp.zeros_like(f_ref)
        h_ref[...] = jnp.zeros_like(h_ref)
        q_ref[...] = jnp.ones_like(q_ref)

    for r in range(block):
        c = lat_ref[first + r]
        states = c_ref[pl.ds(r // 2 * 2 * GROUP, 2 * GROUP), :]
        right = jnp.concatenate([v_ref[r], states], axis=0)
        done = jnp.dot(m_ref[2 * c + r % 2], right, preferred_element_type=F32)
        wide_ref[r] = done
        p_ref[r] = done.astype(BF16)

    for at in range(0, width, CHUNK):
        here = pl.ds(at, CHUNK)
        ahead = [f_ref[k, here, :] for k in range(3)]
        back = [h_ref[k, here, :] for k in range(3)]
        before = [q_ref[k] for k in range(3)]
        for r in range(block):
            get = class_reader(tab_ref, lat_ref[first + r])
            data = wide_ref[r, here, :]
            rate = [get(RATE + k) for k in range(3)]
            ahead = [rate[k] * ahead[k] + get(FWD + k) * data for k in range(3)]
            weighted = ahead[0] + ahead[1] + ahead[2]
            for k in range(3):
                gain = (get(BWD + k) * before[k])[:1]
                back[k] = back[k] + gain * weighted
                before[k] = rate[k] * before[k]
        for k in range(3):
            f_ref[k, here, :] = ahead[k]
            h_ref[k, here, :] = back[k]
    for k in range(3):
        q_ref[k] = before[k]

    @pl.when(step == pl.num_programs(0) - 1)
    def _():
        for k in range(3):
            e_ref[k] = f_ref[k].astype(BF16)
            e_ref[3 + k] = h_ref[k].astype(BF16)


def y_carries(tab_ref, lat_tiles_ref, g_ref, d_ref, c_ref, f_ref, b_ref):
    devices, _, width, lanes = g_ref.shape
    height = lat_tiles_ref.shape[1]
    lat = lat_tiles_ref[...]

    def by_class(at):
        value = jnp.full(lat.shape, tab_ref[at], F32)
        for c in range(1, NCLASS):
            value = jnp.where(lat == c, tab_ref[c * ROW + at], value)
        return value

    logs = [by_class(LOG + k) for k in range(3)]
    upto = (iota((height, height), 0) <= iota((height, height), 1)).astype(F32)
    level = jnp.dot(
        jnp.concatenate(logs, axis=0), upto, precision=lax.Precision.HIGHEST, preferred_element_type=F32
    )
    levels = [level[k * devices : (k + 1) * devices] for k in range(3)]
    reach = [jnp.exp(levels[k]) for k in range(3)]
    for k in range(3):
        d_ref[k] = jnp.broadcast_to(reach[k][:, height - 1 :], (devices, lanes))
    for q in range(3):
        gain = by_class(BWD + q) * jnp.exp(levels[q] - logs[q])
        for k in range(3):
            mixed = jnp.sum(gain * reach[k], axis=1, keepdims=True)
            d_ref[3 + 3 * q + k] = jnp.broadcast_to(mixed, (devices, lanes))
    mine = lax.axis_index("ty")
    for at in range(0, width, CHUNK):
        here = pl.ds(at, CHUNK)
        state = [jnp.zeros((CHUNK, lanes), F32) for _ in range(3)]
        for u in range(devices):
            for k in range(3):
                c_ref[u, k] = state[k]
            for k in range(3):
                state[k] = d_ref[k, pl.ds(u, 1), :] * state[k] + g_ref[u, k, here, :].astype(F32)
        for k in range(3):
            f_ref[k, here, :] = c_ref[mine, k]
        state = [jnp.zeros((CHUNK, lanes), F32) for _ in range(3)]
        for u in range(devices - 1, -1, -1):
            for q in range(3):
                c_ref[u, 3 + q] = state[q]
            if u > 0:
                ahead = [c_ref[u, k] for k in range(3)]
                for q in range(3):
                    total = g_ref[u, 3 + q, here, :].astype(F32)
                    for k in range(3):
                        total += d_ref[3 + 3 * q + k, pl.ds(u, 1), :] * ahead[k]
                    state[q] = d_ref[q, pl.ds(u, 1), :] * state[q] + total
        for q in range(3):
            b_ref[q, here, :] = c_ref[mine, 3 + q]


def owner_rows(owner, peaks):
    slabs = owner.shape[1]
    across = jnp.broadcast_to(owner, (slabs, slabs))
    down = across.T
    row, lane = iota((slabs, slabs), 0), iota((slabs, slabs), 1)
    earlier = jnp.where((across == down) & (row < lane), 1.0, 0.0)
    rank = jnp.sum(earlier, axis=0, keepdims=True)
    mine = across == row.astype(F32)
    rows = jnp.zeros((slabs, slabs), F32)
    for slot in range(MOST):
        held = jnp.where(mine & (rank == slot), peaks, 0.0)
        rows = jnp.where(lane == slot, jnp.sum(held, axis=1, keepdims=True), rows)
    return rows


def final_kernel(
    lat_ref, tab_ref, p_ref, g_ref, lat_tiles_ref, owner_ref, sigma_ref,
    out_ref, peak_ref, d_ref, c_ref, f_ref, b_ref, wide_ref, most_ref,
):
    block, width, lanes = p_ref.shape
    phase, step = pl.program_id(0), pl.program_id(1)
    steps = pl.num_programs(1)
    tile = lax.axis_index("ty") * steps

    @pl.when((phase == 0) & (step == 0))
    def _():
        y_carries(tab_ref, lat_tiles_ref, g_ref, d_ref, c_ref, f_ref, b_ref)
        most_ref[...] = jnp.zeros_like(most_ref)

    @pl.when(phase == 0)
    def _():
        first = (tile + step) * block
        for at in range(0, width, CHUNK):
            here = pl.ds(at, CHUNK)
            ahead = [f_ref[k, here, :] for k in range(3)]
            for r in range(block):
                get = class_reader(tab_ref, lat_ref[first + r])
                data = p_ref[r, here, :].astype(F32)
                ahead = [get(RATE + k) * ahead[k] + get(FWD + k) * data for k in range(3)]
                wide_ref[step * block + r, here, :] = ahead[0] + ahead[1] + ahead[2]
            for k in range(3):
                f_ref[k, here, :] = ahead[k]

    @pl.when(phase == 1)
    def _():
        place = (steps - 1 - step) * block
        first = tile * block + place
        sigma = sigma_ref[...]
        for at in range(0, width, CHUNK):
            here = pl.ds(at, CHUNK)
            back = [b_ref[k, here, :] for k in range(3)]
            most = most_ref[here, :]
            for r in range(block - 1, -1, -1):
                get = class_reader(tab_ref, lat_ref[first + r])
                data = wide_ref[place + r, here, :]
                back = [get(RATE + k) * back[k] + get(BWD + k) * data for k in range(3)]
                scaled = (back[0] + back[1] + back[2]) * sigma
                most = jnp.maximum(most, jnp.abs(scaled))
                out_ref[r, here, :] = scaled.astype(BF16)
            for k in range(3):
                b_ref[k, here, :] = back[k]
            most_ref[here, :] = most

    @pl.when((phase == 1) & (step == steps - 1))
    def _():
        peaks = jnp.max(most_ref[...], axis=0, keepdims=True)
        peak_ref[...] = owner_rows(owner_ref[...], peaks)


SMEM = pl.BlockSpec(memory_space=pltpu.SMEM)
LIMIT = 48 * 1024 * 1024


def params(*semantics):
    return pltpu.CompilerParams(vmem_limit_bytes=LIMIT, dimension_semantics=semantics)


def local(increments, lengths, lat_class, slab_owner, level_sigma):
    count_x = lax.axis_size("tx")
    count_y = lax.axis_size("ty")
    height, width, lanes = increments.shape
    steps = height // BLOCK
    rows = height // count_x
    lines = rows * GROUP
    tab = class_scalars(lengths)
    data_spec = pl.BlockSpec((BLOCK, width, lanes), lambda i: (i, 0, 0))
    state_spec = pl.BlockSpec((BLOCK * GROUP, lanes), lambda i: (i, 0))

    ends = pl.pallas_call(
        ends_kernel,
        grid=(steps,),
        in_specs=[SMEM, SMEM, data_spec],
        out_specs=state_spec,
        out_shape=jax.ShapeDtypeStruct((height * GROUP, lanes), BF16),
        scratch_shapes=[pltpu.VMEM((NCLASS, 2 * GROUP, width), BF16)],
        compiler_params=params("arbitrary"),
        name="x_ends",
    )(lat_class, tab, increments)

    with jax.named_scope("x_ends_to_scanners"):
        ends = lax.all_to_all(ends.reshape(count_x, lines, lanes), "tx", 0, 0, tiled=True)

    states = pl.pallas_call(
        functools.partial(scan_kernel, width, height),
        in_specs=[SMEM, SMEM, pl.BlockSpec(memory_space=pltpu.VMEM)],
        out_specs=pl.BlockSpec(memory_space=pltpu.VMEM),
        out_shape=jax.ShapeDtypeStruct((count_x, lines, lanes), BF16),
        scratch_shapes=[
            pltpu.VMEM((lines, lanes), F32),
            pltpu.VMEM((lines, lanes), F32),
            pltpu.VMEM((count_x, lines, lanes), F32),
        ],
        compiler_params=params(),
        name="x_scan",
    )(lat_class, tab, ends)

    with jax.named_scope("x_states_to_tiles"):
        states = lax.all_to_all(states, "tx", 0, 0, tiled=True).reshape(height * GROUP, lanes)

    pass_two, y_ends = pl.pallas_call(
        middle_kernel,
        grid=(steps,),
        in_specs=[SMEM, SMEM, data_spec, state_spec],
        out_specs=[data_spec, pl.BlockSpec((6, width, lanes), lambda i: (0, 0, 0))],
        out_shape=[
            jax.ShapeDtypeStruct((height, width, lanes), BF16),
            jax.ShapeDtypeStruct((6, width, lanes), BF16),
        ],
        scratch_shapes=[
            pltpu.VMEM((2 * NCLASS, width, width + 2 * GROUP), BF16),
            pltpu.VMEM((BLOCK, width, lanes), F32),
            pltpu.VMEM((3, width, lanes), F32),
            pltpu.VMEM((3, width, lanes), F32),
            pltpu.VMEM((3, 8, lanes), F32),
        ],
        compiler_params=params("arbitrary"),
        name="x_filter_y_ends",
    )(lat_class, tab, increments, states)

    with jax.named_scope("y_ends_to_column"):
        gathered = lax.all_gather(y_ends, "ty")

    last = steps - 1
    tile_out, peak_rows = pl.pallas_call(
        final_kernel,
        grid=(2, steps),
        in_specs=[
            SMEM,
            SMEM,
            pl.BlockSpec((BLOCK, width, lanes), lambda p, i: (jnp.where(p == 0, i, last), 0, 0)),
            pl.BlockSpec((count_y, 6, width, lanes), lambda p, i: (0, 0, 0, 0)),
            pl.BlockSpec((count_y, height), lambda p, i: (0, 0)),
            pl.BlockSpec((1, lanes), lambda p, i: (0, 0)),
            pl.BlockSpec((1, lanes), lambda p, i: (0, 0)),
        ],
        out_specs=[
            pl.BlockSpec(
                (BLOCK, width, lanes), lambda p, i: (jnp.where(p == 0, last, last - i), 0, 0)
            ),
            pl.BlockSpec((lanes, lanes), lambda p, i: (0, 0)),
        ],
        out_shape=[
            jax.ShapeDtypeStruct((height, width, lanes), BF16),
            jax.ShapeDtypeStruct((lanes, lanes), F32),
        ],
        scratch_shapes=[
            pltpu.VMEM((12, count_y, lanes), F32),
            pltpu.VMEM((count_y, 6, CHUNK, lanes), F32),
            pltpu.VMEM((3, width, lanes), F32),
            pltpu.VMEM((3, width, lanes), F32),
            pltpu.VMEM((height, width, lanes), F32),
            pltpu.VMEM((width, lanes), F32),
        ],
        compiler_params=params("arbitrary", "arbitrary"),
        name="y_filter",
    )(
        lat_class,
        tab,
        pass_two,
        gathered,
        lat_class.reshape(count_y, height),
        slab_owner.astype(F32).reshape(1, lanes),
        level_sigma.reshape(1, lanes),
    )

    with jax.named_scope("peaks_to_owners"):
        arrived = lax.all_to_all(peak_rows, ("tx", "ty"), 0, 0, tiled=True)
    peak_table = jnp.max(arrived, axis=0, keepdims=True)[:, :MOST]
    return (tile_out, peak_table)


def solution(mesh):
    placed = (P("ty", "tx", None), P(), P(), P(), P())
    return jax.shard_map(
        local,
        mesh=mesh,
        in_specs=placed,
        out_specs=(P("ty", "tx", None), P(("tx", "ty"), None)),
        check_vma=False,
    )
```

```python
import functools

import jax
import jax.numpy as jnp
from jax import lax
from jax.experimental import pallas as pl
from jax.experimental.pallas import tpu as pltpu
from jax.sharding import PartitionSpec as P

NCLASS = 4
MOST = 2
SCALE_WEIGHTS = (0.5, 0.35, 0.25)
LOG, RATE, FWD, BWD, INV, ROW = 0, 3, 6, 9, 12, 32
GROUP = 8
BLOCK = 16
CHUNK = 48
F32, BF16 = jnp.float32, jnp.bfloat16


def iota(shape, axis):
    return lax.broadcasted_iota(jnp.int32, shape, axis)


def class_scalars(lengths):
    log_rate = -1.0 / lengths
    rate = jnp.exp(log_rate)
    weights = jnp.array(SCALE_WEIGHTS, F32)[None, :]
    forward = weights * jnp.sqrt(1.0 - rate * rate)
    backward = weights * (1.0 - rate)
    inverse = -1.0 / jnp.expm1(log_rate[:, :, None] + log_rate[:, None, :])
    row = jnp.concatenate(
        [log_rate, rate, forward, backward, inverse.reshape(NCLASS, 9)], axis=1
    )
    return jnp.pad(row, ((0, 0), (0, ROW - row.shape[1]))).reshape(-1)


def class_reader(tab_ref, c):
    return lambda at: tab_ref[c * ROW + at]


def ends_kernel(lat_ref, lengths_ref, v_ref, e_ref, w_ref, here_ref, arrived):
    height, width, _ = v_ref.shape
    steps = height // BLOCK
    tile = lax.axis_index("ty") * height

    def piece(step):
        rows = pl.ds(pl.multiple_of(step * BLOCK, BLOCK), BLOCK)
        return pltpu.make_async_copy(v_ref.at[rows], here_ref.at[rows], arrived.at[step])

    for step in range(steps):
        piece(step).start()

    shape = (GROUP, width)
    row = iota(shape, 0)
    at = iota(shape, 1).astype(F32)
    totals = []
    for c in range(NCLASS):
        log = [-1.0 / jnp.full(shape, lengths_ref[c, k], F32) for k in range(3)]
        rate = [jnp.exp(log[k]) for k in range(3)]
        fwd = [SCALE_WEIGHTS[k] * jnp.sqrt(1.0 - rate[k] * rate[k]) for k in range(3)]
        rest = [jnp.exp(log[k] * (width - at)) for k in range(3)]
        total = jnp.zeros(shape, F32)
        for k in range(3):
            fwd_end = fwd[k] * jnp.exp(log[k] * (width - 1 - at))
            total = jnp.where(row == k, fwd_end, total)
        for q in range(3):
            back = jnp.zeros(shape, F32)
            for k in range(3):
                back += fwd[k] * (1.0 - rest[k] * rest[q]) / (1.0 - rate[k] * rate[q])
            back = back * (SCALE_WEIGHTS[q] * (1.0 - rate[q])) * jnp.exp(log[q] * at)
            total = jnp.where(row == 3 + q, back, total)
        totals.append(total)
    for c in range(NCLASS):
        for d in range(NCLASS):
            w_ref[NCLASS * c + d] = jnp.concatenate([totals[c], totals[d]], axis=0).astype(BF16)

    def run(step, _):
        piece(step).wait()
        base = step * BLOCK
        for r in range(0, BLOCK, 2):
            row = base + r
            pair = NCLASS * lat_ref[tile + row] + lat_ref[tile + row + 1]
            both = jnp.concatenate([here_ref[row], here_ref[row + 1]], axis=1)
            done = jnp.dot(w_ref[pair], both, preferred_element_type=F32)
            lanes = done.shape[1] // 2
            own = jnp.concatenate([done[:GROUP, :lanes], done[GROUP:, lanes:]], axis=0)
            at = pl.multiple_of(row * GROUP, 2 * GROUP)
            e_ref[pl.ds(at, 2 * GROUP), :] = own.astype(BF16)
        return 0

    lax.fori_loop(0, steps, run, 0)


def scan_kernel(width, height, lat_ref, tab_ref, e_ref, c_ref, decay_ref, cross_ref, f_ref):
    devices, lines, lanes = e_ref.shape
    rows = lines // GROUP
    first = lax.axis_index("ty") * height + lax.axis_index("tx") * rows
    row = iota((GROUP, lanes), 0)
    lane = iota((GROUP, lanes), 1)
    decay, cross = [], []
    for c in range(NCLASS):
        get = class_reader(tab_ref, c)
        log = jnp.zeros((GROUP, lanes), F32)
        mix = jnp.zeros((GROUP, lanes), F32)
        for k in range(3):
            log = jnp.where((row == k) | (row == 3 + k), get(LOG + k), log)
            for q in range(3):
                both = get(LOG + k) + get(LOG + q)
                value = (get(BWD + q) * get(RATE + k) * get(INV + 3 * q + k)) * (
                    1.0 - jnp.exp(jnp.full((GROUP, lanes), both * width, F32))
                )
                mix = jnp.where((row == 3 + q) & (lane % GROUP == k), value, mix)
        decay.append(jnp.exp(log * width))
        cross.append(mix)
    for r in range(rows):
        c = lat_ref[first + r]
        d, m = decay[0], cross[0]
        for other in range(1, NCLASS):
            d = jnp.where(c == other, decay[other], d)
            m = jnp.where(c == other, cross[other], m)
        decay_ref[pl.ds(r * GROUP, GROUP), :] = d
        cross_ref[pl.ds(r * GROUP, GROUP), :] = jnp.where(lane // GROUP == r, m, 0.0)
    decay = decay_ref[...]
    cross = cross_ref[:, :lines].astype(BF16)
    state = jnp.zeros((lines, lanes), F32)
    for t in range(devices):
        f_ref[t] = state
        state = decay * state + e_ref[t].astype(F32)
    kind = iota((lines, lanes), 0) % GROUP
    state = jnp.zeros((lines, lanes), F32)
    for t in range(devices - 1, -1, -1):
        ahead = f_ref[t]
        c_ref[t] = jnp.where(kind < 3, ahead, jnp.where(kind < 6, state, 0.0)).astype(BF16)
        if t > 0:
            turned = jnp.dot(cross, ahead.astype(BF16), preferred_element_type=F32)
            state = decay * state + e_ref[t].astype(F32) + turned


def x_table_parts(tab_ref, c, width, depth):
    get = class_reader(tab_ref, c)
    out_at = iota((width, depth), 0).astype(F32)
    lane = iota((width, depth), 1)
    in_at = lane.astype(F32)
    far = jnp.maximum(out_at, in_at)
    later = out_at >= in_at
    gap = jnp.abs(out_at - in_at)
    near_power = [jnp.exp(get(LOG + k) * gap) for k in range(3)]
    rest_power = [jnp.exp(get(LOG + k) * jnp.maximum(width - far, 0.0)) for k in range(3)]
    own_rest = [jnp.exp(get(LOG + k) * (width - out_at)) for k in range(3)]
    inner = jnp.zeros((width, depth), F32)
    carried = [jnp.zeros((width, depth), F32) for _ in range(3)]
    for q in range(3):
        for k in range(3):
            inverse = get(INV + 3 * q + k)
            inner += (get(FWD + k) * get(BWD + q) * inverse) * (
                jnp.where(later, near_power[k], near_power[q])
                * (1.0 - rest_power[k] * rest_power[q])
            )
            carried[k] += (get(BWD + q) * inverse) * (1.0 - own_rest[k] * own_rest[q])
    inner = jnp.where(lane < width, inner, 0.0)
    for k in range(3):
        carried[k] = carried[k] * jnp.exp(get(LOG + k) * (out_at + 1.0))
    return lane, inner, carried + own_rest


def tables_kernel(tab_ref, lat_tiles_ref, m_ref, x_ref, d_ref, corner_ref):
    _, width, depth = m_ref.shape
    lanes = d_ref.shape[2]
    devices, height = lat_tiles_ref.shape
    spread = jnp.zeros((width, depth), F32)
    for c in range(NCLASS):
        lane, inner, states = x_table_parts(tab_ref, c, width, depth)
        for parity in range(2):
            table = inner
            for k in range(6):
                table = jnp.where(lane == width + GROUP * parity + k, states[k], table)
            m_ref[2 * c + parity] = table.astype(BF16)
        for k in range(6):
            spread = jnp.where(lane == c * GROUP + k, states[k], spread)
    x_ref[...] = spread[:, : x_ref.shape[1]].astype(BF16)

    def by_class(lat, at):
        value = jnp.full(lat.shape, tab_ref[at], F32)
        for c in range(1, NCLASS):
            value = jnp.where(lat == c, tab_ref[c * ROW + at], value)
        return value

    exact = dict(precision=lax.Precision.HIGHEST, preferred_element_type=F32)
    row, column = iota((height, height), 0), iota((height, height), 1)
    upto = (row <= column).astype(F32)
    lat = lat_tiles_ref[...]
    logs = [by_class(lat, LOG + k) for k in range(3)]
    level = jnp.dot(jnp.concatenate(logs, axis=0), upto, **exact)
    levels = [level[k * devices : (k + 1) * devices] for k in range(3)]
    reach = [jnp.exp(levels[k]) for k in range(3)]
    for k in range(3):
        d_ref[k] = jnp.broadcast_to(reach[k][:, height - 1 :], (devices, lanes))
    for q in range(3):
        gain = by_class(lat, BWD + q) * jnp.exp(levels[q] - logs[q])
        for k in range(3):
            mixed = jnp.sum(gain * reach[k], axis=1, keepdims=True)
            d_ref[3 + 3 * q + k] = jnp.broadcast_to(mixed, (devices, lanes))

    own = jnp.broadcast_to(lat_tiles_ref[pl.ds(lax.axis_index("ty"), 1), :], (GROUP, height))
    kind = iota((GROUP, height), 0)
    log = [by_class(own, LOG + k) for k in range(3)]
    stacked = jnp.zeros((GROUP, height), F32)
    for k in range(3):
        stacked = jnp.where(kind == k, log[k], stacked)
    across = jnp.dot(stacked, upto, **exact)
    down = lax.dot_general(
        (column <= row).astype(F32), stacked, (((1,), (1,)), ((), ())), **exact
    )
    total = jnp.zeros((GROUP, height), F32)
    gains = jnp.zeros((GROUP, height), F32)
    filtered = jnp.zeros((height, height), F32)
    for k in range(3):
        mine = across[k : k + 1]
        forward = by_class(own, FWD + k)
        gap = jnp.minimum(down[:, k : k + 1] - mine, 0.0)
        filtered += jnp.where(row >= column, jnp.exp(gap), 0.0) * forward[:1]
        total = jnp.where(kind == k, forward * jnp.exp(mine[:, height - 1 :] - mine), total)
        gains = jnp.where(
            kind == 3 + k, by_class(own, BWD + k) * jnp.exp(mine - log[k]), gains
        )
    total = jnp.where((kind >= 3) & (kind < 6), jnp.dot(gains, filtered, **exact), total)
    total = jnp.where(kind == 6, own.astype(F32), total).astype(BF16)
    long = height * GROUP
    wider = (iota((height, long), 1) // GROUP == iota((height, long), 0)).astype(BF16)
    total = jnp.dot(total, wider, preferred_element_type=F32)
    group = NCLASS * GROUP
    pick = iota((group, long), 0)
    chosen = (total[6:7] == (pick // GROUP).astype(F32)) & (
        iota((group, long), 1) % GROUP == pick % GROUP
    )
    for q in range(6):
        corner_ref[pl.ds(q * group, group), :] = jnp.where(chosen, total[q : q + 1], 0.0).astype(BF16)


def own_ends_kernel(lat_ref, tab_ref, v_ref, m_ref, e_ref, even_ref, odd_ref, f_ref, h_ref, q_ref):
    height, width, lanes = v_ref.shape
    steps = height // BLOCK
    tile = lax.axis_index("ty") * height
    f_ref[...] = jnp.zeros_like(f_ref)
    h_ref[...] = jnp.zeros_like(h_ref)
    q_ref[...] = jnp.ones_like(q_ref)

    def along_x(step, wide_ref):
        for r in range(BLOCK):
            row = step * BLOCK + r
            table = m_ref[2 * lat_ref[tile + row]][:, :width]
            wide_ref[r] = jnp.dot(table, v_ref[row], preferred_element_type=F32)

    def along_y(step, wide_ref):
        for at in range(0, width, CHUNK):
            here = pl.ds(at, CHUNK)
            ahead = [f_ref[k, here, :] for k in range(3)]
            back = [h_ref[k, here, :] for k in range(3)]
            before = [q_ref[k] for k in range(3)]
            for r in range(BLOCK):
                get = class_reader(tab_ref, lat_ref[tile + step * BLOCK + r])
                data = wide_ref[r, here, :]
                rate = [get(RATE + k) for k in range(3)]
                ahead = [rate[k] * ahead[k] + get(FWD + k) * data for k in range(3)]
                weighted = ahead[0] + ahead[1] + ahead[2]
                for k in range(3):
                    gain = (get(BWD + k) * before[k])[:1]
                    back[k] = back[k] + gain * weighted
                    before[k] = rate[k] * before[k]
            for k in range(3):
                f_ref[k, here, :] = ahead[k]
                h_ref[k, here, :] = back[k]
        for k in range(3):
            q_ref[k] = before[k]

    in_turn(steps, along_x, along_y, even_ref, odd_ref)
    for k in range(3):
        e_ref[k] = f_ref[k]
        e_ref[3 + k] = h_ref[k]


def corner_kernel(corner_ref, c_ref, x_ref, own_ref, e_ref):
    group = x_ref.shape[1]
    sums = jnp.dot(corner_ref[...], c_ref[...], preferred_element_type=F32).astype(BF16)
    for q in range(6):
        part = sums[q * group : (q + 1) * group]
        e_ref[q] = (own_ref[q] + jnp.dot(x_ref[...], part, preferred_element_type=F32)).astype(BF16)


def in_turn(steps, produce, use, even_ref, odd_ref):
    produce(0, even_ref)

    def pair(i, _):
        produce(2 * i + 1, odd_ref)
        use(2 * i, even_ref)
        produce(jnp.minimum(2 * i + 2, steps - 1), even_ref)
        use(2 * i + 1, odd_ref)
        return 0

    lax.fori_loop(0, steps // 2, pair, 0)


def inner_kernel(
    lat_ref, tab_ref, v_ref, c_ref, m_ref, sigma_ref, after_ref,
    out_ref, coef_ref, even_ref, odd_ref, f_ref, wide_ref, unit_ref,
):
    del after_ref
    height, width, lanes = v_ref.shape
    steps = height // BLOCK
    tile = lax.axis_index("ty") * height
    lane = iota((GROUP, lanes), 1)
    diagonal = lane == iota((GROUP, lanes), 0)

    def along_x(step, block_ref):
        for r in range(BLOCK):
            row = step * BLOCK + r
            at = pl.multiple_of(step * (BLOCK * GROUP) + r // 2 * 2 * GROUP, 2 * GROUP)
            right = jnp.concatenate([v_ref[row], c_ref[pl.ds(at, 2 * GROUP), :]], axis=0)
            table = m_ref[2 * lat_ref[tile + row] + r % 2]
            block_ref[r] = jnp.dot(table, right, preferred_element_type=F32)

    def forward(step, block_ref):
        for at in range(0, width, CHUNK):
            here = pl.ds(at, CHUNK)
            ahead = [f_ref[k, here, :] for k in range(3)]
            for r in range(BLOCK):
                row = step * BLOCK + r
                get = class_reader(tab_ref, lat_ref[tile + row])
                data = block_ref[r, here, :]
                ahead = [get(RATE + k) * ahead[k] + get(FWD + k) * data for k in range(3)]
                wide_ref[row, here, :] = ahead[0] + ahead[1] + ahead[2]
            for k in range(3):
                f_ref[k, here, :] = ahead[k]
        ahead = [f_ref[k, pl.ds(width, GROUP), :] for k in range(3)]
        for r in range(BLOCK):
            row = step * BLOCK + r
            get = class_reader(tab_ref, lat_ref[tile + row])
            ahead = [get(RATE + k) * ahead[k] for k in range(3)]
            unit_ref[row] = ahead[0] + ahead[1] + ahead[2]
        for k in range(3):
            f_ref[k, pl.ds(width, GROUP), :] = ahead[k]

    def backward(i, _):
        step = steps - 1 - i
        sigma = sigma_ref[...]
        for at in range(0, width, CHUNK):
            here = pl.ds(at, CHUNK)
            back = [f_ref[k, here, :] for k in range(3)]
            for r in range(BLOCK - 1, -1, -1):
                row = step * BLOCK + r
                get = class_reader(tab_ref, lat_ref[tile + row])
                data = wide_ref[row, here, :]
                back = [get(RATE + k) * back[k] + get(BWD + k) * data for k in range(3)]
                out_ref[row, here, :] = (back[0] + back[1] + back[2]) * sigma
            for k in range(3):
                f_ref[k, here, :] = back[k]
        back = [f_ref[k, pl.ds(width, GROUP), :] for k in range(3)]
        for r in range(BLOCK - 1, -1, -1):
            row = step * BLOCK + r
            get = class_reader(tab_ref, lat_ref[tile + row])
            data = unit_ref[row]
            back = [get(RATE + k) * back[k] + get(BWD + k) * data for k in range(3)]
            own = jnp.where(diagonal, back[0] + back[1] + back[2], 0.0)
            coef_ref[row] = jnp.broadcast_to(jnp.sum(own, axis=1, keepdims=True), (GROUP, lanes))
        for k in range(3):
            f_ref[k, pl.ds(width, GROUP), :] = back[k]
        return 0

    f_ref[...] = jnp.zeros_like(f_ref)
    for k in range(3):
        f_ref[k, pl.ds(width, GROUP), :] = (lane == k).astype(F32)
    in_turn(steps, along_x, forward, even_ref, odd_ref)
    f_ref[...] = jnp.zeros_like(f_ref)
    for k in range(3):
        f_ref[k, pl.ds(width, GROUP), :] = (lane == 3 + k).astype(F32)
    lax.fori_loop(0, steps, backward, 0)


def y_carries(d_ref, end_refs, sigma, c_ref, s_ref):
    devices = len(end_refs)
    _, width, lanes = s_ref.shape
    mine = lax.axis_index("ty")
    for near in range(2):
        for k in range(devices // 2):
            chip = lax.rem(mine // 2 - k + devices // 2, devices // 2)
            core = lax.rem(mine, 2) if near == 0 else 1 - lax.rem(mine, 2)
            c_ref[2 * chip + core] = end_refs[near * (devices // 2) + k][...]
    for at in range(0, width, CHUNK):
        here = pl.ds(at, CHUNK)
        aheads = []
        state = [jnp.zeros((CHUNK, lanes), F32) for _ in range(3)]
        own = state
        for u in range(devices):
            own = [jnp.where(mine == u, state[k], own[k]) for k in range(3)]
            aheads.append(state)
            state = [
                d_ref[k, pl.ds(u, 1), :] * state[k] + c_ref[u, k, here, :].astype(F32)
                for k in range(3)
            ]
        for k in range(3):
            s_ref[k, here, :] = own[k] * sigma
        state = [jnp.zeros((CHUNK, lanes), F32) for _ in range(3)]
        own = state
        for u in range(devices - 1, -1, -1):
            own = [jnp.where(mine == u, state[k], own[k]) for k in range(3)]
            following = []
            for q in range(3):
                total = d_ref[q, pl.ds(u, 1), :] * state[q] + c_ref[u, 3 + q, here, :].astype(F32)
                for k in range(3):
                    total += d_ref[3 + 3 * q + k, pl.ds(u, 1), :] * aheads[u][k]
                following.append(total)
            state = following
        for q in range(3):
            s_ref[3 + q, here, :] = own[q] * sigma


def owner_rows(owner, peaks):
    slabs = owner.shape[1]
    across = jnp.broadcast_to(owner, (slabs, slabs))
    down = across.T
    row, lane = iota((slabs, slabs), 0), iota((slabs, slabs), 1)
    earlier = jnp.where((across == down) & (row < lane), 1.0, 0.0)
    rank = jnp.sum(earlier, axis=0, keepdims=True)
    mine = across == row.astype(F32)
    rows = jnp.zeros((slabs, slabs), F32)
    for slot in range(MOST):
        held = jnp.where(mine & (rank == slot), peaks, 0.0)
        rows = jnp.where(lane == slot, jnp.sum(held, axis=1, keepdims=True), rows)
    return rows


def final_kernel(*refs):
    d_ref, inner_ref, coef_ref, owner_ref, sigma_ref = refs[:5]
    end_refs, (out_ref, peak_ref, c_ref, s_ref, most_ref) = refs[5:-5], refs[-5:]
    height, width, lanes = inner_ref.shape
    y_carries(d_ref, end_refs, sigma_ref[...], c_ref, s_ref)
    most_ref[...] = jnp.zeros_like(most_ref)

    def run(step, _):
        for at in range(0, width, CHUNK):
            here = pl.ds(at, CHUNK)
            states = [s_ref[k, here, :] for k in range(6)]
            most = most_ref[here, :]
            for r in range(BLOCK):
                row = step * BLOCK + r
                scaled = inner_ref[row, here, :]
                for k in range(6):
                    scaled += coef_ref[row, pl.ds(k, 1), :] * states[k]
                most = jnp.maximum(most, jnp.abs(scaled))
                out_ref[row, here, :] = scaled.astype(BF16)
            most_ref[here, :] = most
        return 0

    lax.fori_loop(0, height // BLOCK, run, 0)
    peaks = jnp.max(most_ref[...], axis=0, keepdims=True)
    peak_ref[...] = owner_rows(owner_ref[...], peaks)


SMEM = pl.BlockSpec(memory_space=pltpu.SMEM)
VMEM = pl.BlockSpec(memory_space=pltpu.VMEM)
MIB = 1024 * 1024


def params(mib):
    return pltpu.CompilerParams(vmem_limit_bytes=mib * MIB)


def cost(us):
    return pl.CostEstimate(flops=0, bytes_accessed=int(us * 3.0e6), transcendentals=0)


def shape(*dims, kind=BF16):
    return jax.ShapeDtypeStruct(dims, kind)


def along_column(own):
    count = lax.axis_size("ty")
    sibling = [(i, i ^ 1) for i in range(count)]
    same = [own] + [
        lax.ppermute(own, "ty", [(i, (i + 2 * k) % count) for i in range(count)])
        for k in range(1, count // 2)
    ]
    return same + [lax.ppermute(array, "ty", sibling) for array in same]


def local(increments, lengths, lat_class, slab_owner, level_sigma):
    count_x = lax.axis_size("tx")
    count_y = lax.axis_size("ty")
    height, width, lanes = increments.shape
    steps = height // BLOCK
    rows = height // count_x
    lines = rows * GROUP
    deep = width + 2 * GROUP

    ends = pl.pallas_call(
        ends_kernel,
        in_specs=[SMEM, SMEM, pl.BlockSpec(memory_space=pltpu.HBM)],
        out_specs=VMEM,
        out_shape=shape(height * GROUP, lanes),
        scratch_shapes=[
            pltpu.VMEM((NCLASS * NCLASS, 2 * GROUP, width), BF16),
            pltpu.VMEM((height, width, lanes), BF16),
            pltpu.SemaphoreType.DMA((steps,)),
        ],
        compiler_params=params(8),
        cost_estimate=cost(4),
        name="x_ends",
    )(lat_class, lengths, increments)

    ends, lengths, lat_class, increments = lax.optimization_barrier(
        (ends, lengths, lat_class, increments)
    )
    with jax.named_scope("x_ends_to_scanners"):
        ends = lax.all_to_all(ends.reshape(count_x, lines, lanes), "tx", 0, 0, tiled=True)

    tab = class_scalars(lengths)
    sigma = level_sigma.reshape(1, lanes)
    m_table, x_table, d_table, corner = pl.pallas_call(
        tables_kernel,
        in_specs=[SMEM, VMEM],
        out_specs=[VMEM] * 4,
        out_shape=[
            shape(2 * NCLASS, width, deep),
            shape(width, NCLASS * GROUP),
            shape(12, count_y, lanes, kind=F32),
            shape(6 * NCLASS * GROUP, height * GROUP),
        ],
        compiler_params=params(12),
        cost_estimate=cost(3),
        name="tables",
    )(tab, lat_class.reshape(count_y, height))

    own_ends = pl.pallas_call(
        own_ends_kernel,
        in_specs=[SMEM, SMEM, VMEM, VMEM],
        out_specs=VMEM,
        out_shape=shape(6, width, lanes, kind=F32),
        scratch_shapes=[
            pltpu.VMEM((BLOCK, width, lanes), F32),
            pltpu.VMEM((BLOCK, width, lanes), F32),
            pltpu.VMEM((3, width, lanes), F32),
            pltpu.VMEM((3, width, lanes), F32),
            pltpu.VMEM((3, 8, lanes), F32),
        ],
        compiler_params=params(12),
        cost_estimate=cost(7),
        name="own_y_ends",
    )(lat_class, tab, increments, m_table)

    states = pl.pallas_call(
        functools.partial(scan_kernel, width, height),
        in_specs=[SMEM, SMEM, VMEM],
        out_specs=VMEM,
        out_shape=shape(count_x, lines, lanes),
        scratch_shapes=[
            pltpu.VMEM((lines, lanes), F32),
            pltpu.VMEM((lines, lanes), F32),
            pltpu.VMEM((count_x, lines, lanes), F32),
        ],
        compiler_params=params(8),
        cost_estimate=cost(1),
        name="x_scan",
    )(lat_class, tab, ends)

    with jax.named_scope("x_states_to_tiles"):
        states = lax.all_to_all(states, "tx", 0, 0, tiled=True).reshape(height * GROUP, lanes)

    y_ends = pl.pallas_call(
        corner_kernel,
        in_specs=[VMEM] * 4,
        out_specs=VMEM,
        out_shape=shape(6, width, lanes),
        compiler_params=params(8),
        cost_estimate=cost(1),
        name="y_ends",
    )(corner, states, x_table, own_ends)

    with jax.named_scope("y_ends_to_column"):
        gathered = along_column(y_ends)

    inner, coefs = pl.pallas_call(
        inner_kernel,
        in_specs=[SMEM, SMEM, VMEM, VMEM, VMEM, VMEM, pl.BlockSpec(memory_space=pl.ANY)],
        out_specs=[VMEM, VMEM],
        out_shape=[
            shape(height, width, lanes, kind=F32),
            shape(height, GROUP, lanes, kind=F32),
        ],
        scratch_shapes=[
            pltpu.VMEM((BLOCK, width, lanes), F32),
            pltpu.VMEM((BLOCK, width, lanes), F32),
            pltpu.VMEM((3, width + GROUP, lanes), F32),
            pltpu.VMEM((height, width, lanes), F32),
            pltpu.VMEM((height, GROUP, lanes), F32),
        ],
        compiler_params=params(32),
        cost_estimate=cost(10),
        name="inner",
    )(lat_class, tab, increments, states, m_table, sigma, y_ends)

    tile_out, peak_rows = pl.pallas_call(
        final_kernel,
        in_specs=[VMEM] * (5 + count_y),
        out_specs=[VMEM, VMEM],
        out_shape=[shape(height, width, lanes), shape(lanes, lanes, kind=F32)],
        scratch_shapes=[
            pltpu.VMEM((count_y, 6, width, lanes), BF16),
            pltpu.VMEM((6, width, lanes), F32),
            pltpu.VMEM((width, lanes), F32),
        ],
        compiler_params=params(22),
        cost_estimate=cost(5),
        name="final",
    )(d_table, inner, coefs, slab_owner.astype(F32).reshape(1, lanes), sigma, *gathered)

    with jax.named_scope("peaks_to_owners"):
        arrived = lax.all_to_all(peak_rows, ("tx", "ty"), 0, 0, tiled=True)
    peak_table = jnp.max(arrived, axis=0, keepdims=True)[:, :MOST]
    return (tile_out, peak_table)


def solution(mesh):
    placed = (P("ty", "tx", None), P(), P(), P(), P())
    return jax.shard_map(
        local,
        mesh=mesh,
        in_specs=placed,
        out_specs=(P("ty", "tx", None), P(("tx", "ty"), None)),
        check_vma=False,
    )
```

```python
import jax
import jax.numpy as jnp
from jax import lax
from jax.experimental import pallas as pl
from jax.experimental.pallas import tpu as pltpu
from jax.sharding import PartitionSpec as P

NCLASS = 4
MOST = 2
SCALE_WEIGHTS = (0.5, 0.35, 0.25)
LOG, RATE, FWD, BWD, INV, ROW = 0, 3, 6, 9, 12, 32
GROUP = 8
BLOCK = 16
LONG = 48
CHUNK = 48
F32, BF16 = jnp.float32, jnp.bfloat16


def iota(shape, axis):
    return lax.broadcasted_iota(jnp.int32, shape, axis)


def class_scalars(lengths):
    log_rate = -1.0 / lengths
    rate = jnp.exp(log_rate)
    weights = jnp.array(SCALE_WEIGHTS, F32)[None, :]
    forward = weights * jnp.sqrt(1.0 - rate * rate)
    backward = weights * (1.0 - rate)
    inverse = -1.0 / jnp.expm1(log_rate[:, :, None] + log_rate[:, None, :])
    row = jnp.concatenate(
        [log_rate, rate, forward, backward, inverse.reshape(NCLASS, 9)], axis=1
    )
    return jnp.pad(row, ((0, 0), (0, ROW - row.shape[1]))).reshape(-1)


class Pieces:
    def __init__(self, source, target, done, rows):
        self.source, self.target, self.done, self.rows = source, target, done, rows
        self.count = source.shape[0] // rows

    def copy(self, piece):
        rows = pl.ds(pl.multiple_of(piece * self.rows, self.rows), self.rows)
        return pltpu.make_async_copy(self.source.at[rows], self.target.at[rows], self.done.at[piece])

    def start(self, order=None):
        for piece in range(self.count) if order is None else order:
            self.copy(piece).start()

    def wait(self):
        for piece in range(self.count):
            self.copy(piece).wait()


def class_reader(tab_ref, c):
    return lambda at: tab_ref[c * ROW + at]


def ends_kernel(lat_ref, lengths_ref, v_ref, e_ref, w_ref, here_ref, arrived):
    height, width, lanes = v_ref.shape
    tile = lax.axis_index("ty") * height
    pieces = Pieces(v_ref, here_ref, arrived, LONG)
    pieces.start()
    shape = (GROUP, width)
    row = iota(shape, 0)
    at = iota(shape, 1).astype(F32)
    totals = []
    for c in range(NCLASS):
        log = [-1.0 / jnp.full(shape, lengths_ref[c, k], F32) for k in range(3)]
        rate = [jnp.exp(log[k]) for k in range(3)]
        fwd = [SCALE_WEIGHTS[k] * jnp.sqrt(1.0 - rate[k] * rate[k]) for k in range(3)]
        rest = [jnp.exp(log[k] * (width - at)) for k in range(3)]
        total = jnp.zeros(shape, F32)
        for k in range(3):
            fwd_end = fwd[k] * jnp.exp(log[k] * (width - 1 - at))
            total = jnp.where(row == k, fwd_end, total)
        for q in range(3):
            back = jnp.zeros(shape, F32)
            for k in range(3):
                back += fwd[k] * (1.0 - rest[k] * rest[q]) / (1.0 - rate[k] * rate[q])
            back = back * (SCALE_WEIGHTS[q] * (1.0 - rate[q])) * jnp.exp(log[q] * at)
            total = jnp.where(row == 3 + q, back, total)
        totals.append(total)
    for c in range(NCLASS):
        for d in range(NCLASS):
            w_ref[NCLASS * c + d] = jnp.concatenate([totals[c], totals[d]], axis=0).astype(BF16)

    def run(step, _):
        pieces.copy(step).wait()
        for r in range(0, LONG, 2):
            row = step * LONG + r
            pair = NCLASS * lat_ref[tile + row] + lat_ref[tile + row + 1]
            both = jnp.concatenate([here_ref[row], here_ref[row + 1]], axis=1)
            done = jnp.dot(w_ref[pair], both, preferred_element_type=F32)
            own = jnp.concatenate([done[:GROUP, :lanes], done[GROUP:, lanes:]], axis=0)
            at = pl.multiple_of(row * GROUP, 2 * GROUP)
            e_ref[pl.ds(at, 2 * GROUP), :] = own.astype(BF16)
        return 0

    lax.fori_loop(0, pieces.count, run, 0)


def scan_kernel(decay_ref, cross_ref, e_ref, c_ref, f_ref):
    devices, lines, lanes = e_ref.shape
    decay = decay_ref[...]
    cross = cross_ref[:, :lines]
    state = jnp.zeros((lines, lanes), F32)
    for t in range(devices):
        f_ref[t] = state
        state = decay * state + e_ref[t].astype(F32)
    kind = iota((lines, lanes), 0) % GROUP
    state = jnp.zeros((lines, lanes), F32)
    for t in range(devices - 1, -1, -1):
        ahead = f_ref[t]
        c_ref[t] = jnp.where(kind < 3, ahead, jnp.where(kind < 6, state, 0.0)).astype(BF16)
        if t > 0:
            turned = jnp.dot(cross, ahead.astype(BF16), preferred_element_type=F32)
            state = decay * state + e_ref[t].astype(F32) + turned


def fill_scan_tables(lat_ref, tab_ref, width, height, decay_ref, cross_ref):
    lines, lanes = decay_ref.shape
    rows = lines // GROUP
    first = lax.axis_index("ty") * height + lax.axis_index("tx") * rows
    row = iota((GROUP, lanes), 0)
    lane = iota((GROUP, lanes), 1)
    decay, cross = [], []
    for c in range(NCLASS):
        get = class_reader(tab_ref, c)
        log = jnp.zeros((GROUP, lanes), F32)
        mix = jnp.zeros((GROUP, lanes), F32)
        for k in range(3):
            log = jnp.where((row == k) | (row == 3 + k), get(LOG + k), log)
            for q in range(3):
                both = get(LOG + k) + get(LOG + q)
                value = (get(BWD + q) * get(RATE + k) * get(INV + 3 * q + k)) * (
                    1.0 - jnp.exp(jnp.full((GROUP, lanes), both * width, F32))
                )
                mix = jnp.where((row == 3 + q) & (lane % GROUP == k), value, mix)
        decay.append(jnp.exp(log * width))
        cross.append(mix)
    for r in range(0, rows, 2):
        mixes = []
        for at in (r, r + 1):
            c = lat_ref[first + at]
            d, m = decay[0], cross[0]
            for other in range(1, NCLASS):
                d = jnp.where(c == other, decay[other], d)
                m = jnp.where(c == other, cross[other], m)
            decay_ref[pl.ds(at * GROUP, GROUP), :] = d
            mixes.append(jnp.where(lane // GROUP == at, m, 0.0))
        cross_ref[pl.ds(r * GROUP, 2 * GROUP), :] = jnp.concatenate(mixes, axis=0).astype(BF16)


def x_table_parts(tab_ref, c, width, depth):
    get = class_reader(tab_ref, c)
    out_at = iota((width, depth), 0).astype(F32)
    lane = iota((width, depth), 1)
    in_at = lane.astype(F32)
    far = jnp.maximum(out_at, in_at)
    later = out_at >= in_at
    gap = jnp.abs(out_at - in_at)
    near_power = [jnp.exp(get(LOG + k) * gap) for k in range(3)]
    rest_power = [jnp.exp(get(LOG + k) * jnp.maximum(width - far, 0.0)) for k in range(3)]
    own_rest = [jnp.exp(get(LOG + k) * (width - out_at)) for k in range(3)]
    inner = jnp.zeros((width, depth), F32)
    carried = [jnp.zeros((width, depth), F32) for _ in range(3)]
    for q in range(3):
        for k in range(3):
            inverse = get(INV + 3 * q + k)
            inner += (get(FWD + k) * get(BWD + q) * inverse) * (
                jnp.where(later, near_power[k], near_power[q])
                * (1.0 - rest_power[k] * rest_power[q])
            )
            carried[k] += (get(BWD + q) * inverse) * (1.0 - own_rest[k] * own_rest[q])
    inner = jnp.where(lane < width, inner, 0.0)
    for k in range(3):
        carried[k] = carried[k] * jnp.exp(get(LOG + k) * (out_at + 1.0))
    return lane, inner, carried + own_rest


def tables_kernel(
    lat_ref, tab_ref, lat_tiles_ref, m_ref, x_ref, y_ref, corner_ref, decay_ref, cross_ref
):
    _, width, depth = m_ref.shape
    lanes = y_ref.shape[2]
    devices, height = lat_tiles_ref.shape
    fill_scan_tables(lat_ref, tab_ref, width, height, decay_ref, cross_ref)
    spread = jnp.zeros((width, depth), F32)
    for c in range(NCLASS):
        lane, inner, states = x_table_parts(tab_ref, c, width, depth)
        for parity in range(2):
            table = inner
            for k in range(6):
                table = jnp.where(lane == width + GROUP * parity + k, states[k], table)
            m_ref[2 * c + parity] = table.astype(BF16)
        for k in range(6):
            spread = jnp.where(lane == c * GROUP + k, states[k], spread)
    x_ref[...] = spread[:, : x_ref.shape[1]].astype(BF16)

    def by_class(lat, at):
        value = jnp.full(lat.shape, tab_ref[at], F32)
        for c in range(1, NCLASS):
            value = jnp.where(lat == c, tab_ref[c * ROW + at], value)
        return value

    exact = dict(precision=lax.Precision.HIGHEST, preferred_element_type=F32)
    row, column = iota((height, height), 0), iota((height, height), 1)
    upto = (row <= column).astype(F32)
    lat = lat_tiles_ref[...]
    logs = [by_class(lat, LOG + k) for k in range(3)]
    level = jnp.dot(jnp.concatenate(logs, axis=0), upto, **exact)
    levels = [level[k * devices : (k + 1) * devices] for k in range(3)]
    reach = [jnp.exp(levels[k]) for k in range(3)]
    cross = []
    for q in range(3):
        gain = by_class(lat, BWD + q) * jnp.exp(levels[q] - logs[q])
        for k in range(3):
            mixed = jnp.sum(gain * reach[k], axis=1, keepdims=True)
            cross.append(jnp.broadcast_to(mixed, (devices, lanes)))
    fill_y_tables(levels, cross, y_ref)

    own = jnp.broadcast_to(lat_tiles_ref[pl.ds(lax.axis_index("ty"), 1), :], (GROUP, height))
    kind = iota((GROUP, height), 0)
    log = [by_class(own, LOG + k) for k in range(3)]
    stacked = jnp.zeros((GROUP, height), F32)
    for k in range(3):
        stacked = jnp.where(kind == k, log[k], stacked)
    across = jnp.dot(stacked, upto, **exact)
    down = lax.dot_general(
        (column <= row).astype(F32), stacked, (((1,), (1,)), ((), ())), **exact
    )
    total = jnp.zeros((GROUP, height), F32)
    gains = jnp.zeros((GROUP, height), F32)
    filtered = jnp.zeros((height, height), F32)
    for k in range(3):
        mine = across[k : k + 1]
        forward = by_class(own, FWD + k)
        gap = jnp.minimum(down[:, k : k + 1] - mine, 0.0)
        filtered += jnp.where(row >= column, jnp.exp(gap), 0.0) * forward[:1]
        total = jnp.where(kind == k, forward * jnp.exp(mine[:, height - 1 :] - mine), total)
        gains = jnp.where(
            kind == 3 + k, by_class(own, BWD + k) * jnp.exp(mine - log[k]), gains
        )
    total = jnp.where((kind >= 3) & (kind < 6), jnp.dot(gains, filtered, **exact), total)
    total = jnp.where(kind == 6, own.astype(F32), total).astype(BF16)
    long = height * GROUP
    wider = (iota((height, long), 1) // GROUP == iota((height, long), 0)).astype(BF16)
    total = jnp.dot(total, wider, preferred_element_type=F32)
    group = NCLASS * GROUP
    pick = iota((group, long), 0)
    chosen = (total[6:7] == (pick // GROUP).astype(F32)) & (
        iota((group, long), 1) % GROUP == pick % GROUP
    )
    for q in range(6):
        corner_ref[pl.ds(q * group, group), :] = jnp.where(chosen, total[q : q + 1], 0.0).astype(BF16)


def fill_y_tables(levels, cross, y_ref):
    _, devices, lanes = y_ref.shape
    mine = lax.axis_index("ty")
    row = iota((devices, lanes), 0)
    before, upto, my_before, my_upto = [], [], [], []
    for k in range(3):
        level = jnp.broadcast_to(levels[k][:, -1:], (devices, lanes))
        total = jnp.zeros((devices, lanes), F32)
        for u in range(devices - 1):
            total += jnp.where(row > u, level[u : u + 1], 0.0)
        before.append(total)
        upto.append(total + level)
        my_before.append(jnp.sum(jnp.where(row == mine, total, 0.0), axis=0, keepdims=True))
        my_upto.append(jnp.sum(jnp.where(row == mine, total + level, 0.0), axis=0, keepdims=True))
        y_ref[12 + k] = jnp.broadcast_to(jnp.exp(my_upto[k] - my_before[k]), (devices, lanes))

    def decay(gap):
        return jnp.exp(jnp.minimum(gap, 0.0))

    for q in range(3):
        y_ref[q] = jnp.where(row < mine, decay(my_before[q] - upto[q]), 0.0)
        back = [decay(before[q][u : u + 1] - upto[q]) for u in range(devices)]
        for k in range(3):
            turned = jnp.zeros((devices, lanes), F32)
            for u in range(1, devices):
                ahead = decay(before[k][u : u + 1] - my_upto[k]) * cross[3 * q + k][u : u + 1]
                turned += jnp.where(mine < u, back[u] * ahead, 0.0)
            straight = decay(before[k] - my_upto[k]) if q == k else 0.0
            y_ref[3 + 3 * q + k] = jnp.where(row > mine, straight, turned)


def own_ends_kernel(
    lat_ref, tab_ref, v_ref, m_ref, e_ref, even_ref, odd_ref, f_ref, h_ref, q_ref, here_ref, arrived
):
    height, width, lanes = v_ref.shape
    pieces = Pieces(v_ref, here_ref, arrived, BLOCK)
    pieces.start()
    steps = height // BLOCK
    tile = lax.axis_index("ty") * height
    f_ref[...] = jnp.zeros_like(f_ref)
    h_ref[...] = jnp.zeros_like(h_ref)
    q_ref[...] = jnp.ones_like(q_ref)

    def along_x(step, wide_ref):
        pieces.copy(step).wait()
        for r in range(BLOCK):
            row = step * BLOCK + r
            table = m_ref[2 * lat_ref[tile + row]][:, :width]
            wide_ref[r] = jnp.dot(table, here_ref[row], preferred_element_type=F32)

    def along_y(step, wide_ref):
        for at in range(0, width, CHUNK):
            here = pl.ds(at, CHUNK)
            ahead = [f_ref[k, here, :] for k in range(3)]
            back = [h_ref[k, here, :] for k in range(3)]
            before = [q_ref[k] for k in range(3)]
            for r in range(BLOCK):
                get = class_reader(tab_ref, lat_ref[tile + step * BLOCK + r])
                data = wide_ref[r, here, :]
                rate = [get(RATE + k) for k in range(3)]
                ahead = [rate[k] * ahead[k] + get(FWD + k) * data for k in range(3)]
                weighted = ahead[0] + ahead[1] + ahead[2]
                for k in range(3):
                    gain = (get(BWD + k) * before[k])[:1]
                    back[k] = back[k] + gain * weighted
                    before[k] = rate[k] * before[k]
            for k in range(3):
                f_ref[k, here, :] = ahead[k]
                h_ref[k, here, :] = back[k]
        for k in range(3):
            q_ref[k] = before[k]

    in_turn(steps, along_x, along_y, even_ref, odd_ref)
    for k in range(3):
        e_ref[k] = f_ref[k]
        e_ref[3 + k] = h_ref[k]


def corner_kernel(corner_ref, c_ref, x_ref, own_ref, y_ref, send_ref, e_ref):
    group = x_ref.shape[1]
    devices = send_ref.shape[0]
    _, width, _ = own_ref.shape
    sums = jnp.dot(corner_ref[...], c_ref[...], preferred_element_type=F32).astype(BF16)
    for q in range(6):
        part = sums[q * group : (q + 1) * group]
        e_ref[q] = own_ref[q] + jnp.dot(x_ref[...], part, preferred_element_type=F32)
    for at in range(0, width, CHUNK):
        ends = [e_ref[q, pl.ds(at, CHUNK), :] for q in range(6)]
        for u in range(devices):
            for q in range(3):
                total = y_ref[q, pl.ds(u, 1), :] * ends[3 + q]
                for k in range(3):
                    total += y_ref[3 + 3 * q + k, pl.ds(u, 1), :] * ends[k]
                send_ref[u, pl.ds(q * width + at, CHUNK), :] = total.astype(BF16)


def in_turn(steps, produce, use, even_ref, odd_ref):
    produce(0, even_ref)

    def pair(i, _):
        produce(2 * i + 1, odd_ref)
        use(2 * i, even_ref)
        produce(2 * i + 2, even_ref)
        use(2 * i + 1, odd_ref)
        return 0

    lax.fori_loop(0, steps // 2 - 1, pair, 0)
    produce(steps - 1, odd_ref)
    use(steps - 2, even_ref)
    use(steps - 1, odd_ref)


def inner_kernel(
    lat_ref, tab_ref, v_ref, c_ref, m_ref, sigma_ref, after_ref,
    out_ref, coef_ref, even_ref, odd_ref, f_ref, wide_ref, unit_ref, here_ref, done_ref, arrived, sent,
):
    del after_ref
    height, width, lanes = v_ref.shape
    pieces = Pieces(v_ref, here_ref, arrived, BLOCK)
    results = Pieces(done_ref, out_ref, sent, BLOCK)
    pieces.start()
    steps = height // BLOCK
    tile = lax.axis_index("ty") * height
    lane = iota((GROUP, lanes), 1)
    used = 6 * GROUP
    diagonal = (lane % GROUP == iota((GROUP, lanes), 0)) & (lane < 2 * used)

    def along_x(step, block_ref):
        pieces.copy(step).wait()
        for r in range(BLOCK):
            row = step * BLOCK + r
            at = pl.multiple_of(step * (BLOCK * GROUP) + r // 2 * 2 * GROUP, 2 * GROUP)
            right = jnp.concatenate([here_ref[row], c_ref[pl.ds(at, 2 * GROUP), :]], axis=0)
            table = m_ref[2 * lat_ref[tile + row] + r % 2]
            block_ref[r] = jnp.dot(table, right, preferred_element_type=F32)

    def forward(step, block_ref):
        for at in range(0, width, CHUNK):
            here = pl.ds(at, CHUNK)
            ahead = [f_ref[k, here, :] for k in range(3)]
            for r in range(BLOCK):
                row = step * BLOCK + r
                get = class_reader(tab_ref, lat_ref[tile + row])
                data = block_ref[r, here, :]
                ahead = [get(RATE + k) * ahead[k] + get(FWD + k) * data for k in range(3)]
                wide_ref[row, here, :] = ahead[0] + ahead[1] + ahead[2]
            for k in range(3):
                f_ref[k, here, :] = ahead[k]
        ahead = [f_ref[k, pl.ds(width, GROUP), :] for k in range(3)]
        for r in range(BLOCK):
            row = step * BLOCK + r
            get = class_reader(tab_ref, lat_ref[tile + row])
            ahead = [get(RATE + k) * ahead[k] for k in range(3)]
            unit_ref[row] = ahead[0] + ahead[1] + ahead[2]
        for k in range(3):
            f_ref[k, pl.ds(width, GROUP), :] = ahead[k]

    def backward(i, _):
        step = steps - 1 - i
        sigma = sigma_ref[...]
        for at in range(0, width, CHUNK):
            here = pl.ds(at, CHUNK)
            back = [f_ref[k, here, :] for k in range(3)]
            for r in range(BLOCK - 1, -1, -1):
                row = step * BLOCK + r
                get = class_reader(tab_ref, lat_ref[tile + row])
                data = wide_ref[row, here, :]
                back = [get(RATE + k) * back[k] + get(BWD + k) * data for k in range(3)]
                done_ref[row, here, :] = ((back[0] + back[1] + back[2]) * sigma).astype(BF16)
            for k in range(3):
                f_ref[k, here, :] = back[k]
        back = [f_ref[k, pl.ds(width, GROUP), :] for k in range(3)]
        spread = [None] * BLOCK
        for r in range(BLOCK - 1, -1, -1):
            row = step * BLOCK + r
            get = class_reader(tab_ref, lat_ref[tile + row])
            data = unit_ref[row]
            back = [get(RATE + k) * back[k] + get(BWD + k) * data for k in range(3)]
            own = jnp.where(diagonal, back[0] + back[1] + back[2], 0.0)
            spread[r] = jnp.where(lane < used, own, own - own.astype(BF16).astype(F32))
        for r in range(0, BLOCK, 2):
            at = pl.multiple_of((step * BLOCK + r) * GROUP, 2 * GROUP)
            pair = jnp.concatenate([spread[r], spread[r + 1]], axis=0)
            coef_ref[pl.ds(at, 2 * GROUP), :] = pair.astype(BF16)
        for k in range(3):
            f_ref[k, pl.ds(width, GROUP), :] = back[k]
        results.copy(step).start()
        return 0

    f_ref[...] = jnp.zeros_like(f_ref)
    for k in range(3):
        f_ref[k, pl.ds(width, GROUP), :] = (lane % used // GROUP == k).astype(F32)
    in_turn(steps, along_x, forward, even_ref, odd_ref)
    f_ref[...] = jnp.zeros_like(f_ref)
    for k in range(3):
        f_ref[k, pl.ds(width, GROUP), :] = (lane % used // GROUP == 3 + k).astype(F32)
    lax.fori_loop(0, steps, backward, 0)
    results.wait()


def y_carries(y_ref, arrived_ref, sigma, s_ref):
    devices = arrived_ref.shape[0]
    lanes = arrived_ref.shape[2]
    width = arrived_ref.shape[1] // 3
    mine = lax.axis_index("ty")
    mixed = [
        [
            y_ref[3 + 3 * q + k, pl.ds(mine, 1), :] * y_ref[12 + k, pl.ds(0, 1), :] * sigma
            for k in range(3)
        ]
        for q in range(3)
    ]
    for at in range(0, width, 2 * GROUP):
        ahead = [jnp.zeros((2 * GROUP, lanes), F32) for _ in range(3)]
        back = list(ahead)
        for u in range(devices):
            for q in range(3):
                came = arrived_ref[u, pl.ds(q * width + at, 2 * GROUP), :].astype(F32)
                ahead[q] += jnp.where(u < mine, came, 0.0)
                back[q] += jnp.where(u < mine, 0.0, came)
        states = [ahead[k] * sigma for k in range(3)]
        for q in range(3):
            total = back[q] * sigma
            for k in range(3):
                total += mixed[q][k] * ahead[k]
            states.append(total)
        for half in range(2):
            rows = slice(half * GROUP, (half + 1) * GROUP)
            for k in range(0, 6, 2):
                pair = jnp.concatenate([states[k][rows], states[k + 1][rows]], axis=0).astype(BF16)
                for copy in range(2):
                    place = pl.ds(copy * 6 * GROUP + k * GROUP, 2 * GROUP)
                    s_ref[at // (2 * GROUP), place, half * lanes : (half + 1) * lanes] = pair


def owner_rows(owner, peaks):
    slabs = owner.shape[1]
    across = jnp.broadcast_to(owner, (slabs, slabs))
    down = across.T
    row, lane = iota((slabs, slabs), 0), iota((slabs, slabs), 1)
    earlier = jnp.where((across == down) & (row < lane), 1.0, 0.0)
    rank = jnp.sum(earlier, axis=0, keepdims=True)
    mine = across == row.astype(F32)
    rows = jnp.zeros((slabs, slabs), F32)
    for slot in range(MOST):
        held = jnp.where(mine & (rank == slot), peaks, 0.0)
        rows = jnp.where(lane == slot, jnp.sum(held, axis=1, keepdims=True), rows)
    return rows


def final_kernel(
    y_ref, inner_ref, coef_ref, owner_ref, sigma_ref, arrived_ref,
    out_ref, peak_ref, s_ref, here_ref, done_ref, arrived, sent,
):
    height, width, lanes = inner_ref.shape
    rows = 2 * BLOCK
    pieces = Pieces(inner_ref, here_ref, arrived, rows)
    results = Pieces(done_ref, out_ref, sent, rows)
    pieces.start()
    y_carries(y_ref, arrived_ref, sigma_ref[...], s_ref)
    deep = s_ref.shape[1]

    def run(step, most):
        most = list(most)
        pieces.copy(step).wait()
        at = pl.multiple_of(step * (rows * GROUP), rows * GROUP)
        left = coef_ref[pl.ds(at, rows * GROUP), :][:, :deep]
        for piece in range(width // (2 * GROUP)):
            brought = jnp.dot(left, s_ref[piece], preferred_element_type=F32)
            for r in range(rows):
                row = step * rows + r
                here = pl.ds(piece * 2 * GROUP, 2 * GROUP)
                tile = brought[r * GROUP : (r + 1) * GROUP]
                tile = jnp.concatenate([tile[:, :lanes], tile[:, lanes:]], axis=0)
                scaled = here_ref[row, here, :].astype(F32) + tile
                most[r % 2] = jnp.maximum(most[r % 2], jnp.abs(scaled))
                done_ref[row, here, :] = scaled.astype(BF16)
        results.copy(step).start()
        return tuple(most)

    start = tuple(jnp.zeros((2 * GROUP, lanes), F32) for _ in range(2))
    most = lax.fori_loop(0, pieces.count, run, start)
    peaks = jnp.max(jnp.maximum(*most), axis=0, keepdims=True)
    peak_ref[...] = owner_rows(owner_ref[...], peaks)
    results.wait()


SMEM = pl.BlockSpec(memory_space=pltpu.SMEM)
VMEM = pl.BlockSpec(memory_space=pltpu.VMEM)
HBM = pl.BlockSpec(memory_space=pltpu.HBM)
MIB = 1024 * 1024


def params(mib):
    return pltpu.CompilerParams(vmem_limit_bytes=mib * MIB)


def cost(us):
    return pl.CostEstimate(flops=0, bytes_accessed=int(us * 3.0e6), transcendentals=0)


def shape(*dims, kind=BF16):
    return jax.ShapeDtypeStruct(dims, kind)


def local(increments, lengths, lat_class, slab_owner, level_sigma):
    count_x = lax.axis_size("tx")
    count_y = lax.axis_size("ty")
    height, width, lanes = increments.shape
    steps = height // BLOCK
    rows = height // count_x
    lines = rows * GROUP
    deep = width + 2 * GROUP

    ends = pl.pallas_call(
        ends_kernel,
        in_specs=[SMEM, SMEM, HBM],
        out_specs=VMEM,
        out_shape=shape(height * GROUP, lanes),
        scratch_shapes=[
            pltpu.VMEM((NCLASS * NCLASS, 2 * GROUP, width), BF16),
            pltpu.VMEM((height, width, lanes), BF16),
            pltpu.SemaphoreType.DMA((height // LONG,)),
        ],
        compiler_params=params(60),
        cost_estimate=cost(4),
        name="x_ends",
    )(lat_class, lengths, increments)

    ends, lengths, lat_class = lax.optimization_barrier((ends, lengths, lat_class))
    with jax.named_scope("x_ends_to_scanners"):
        ends = lax.all_to_all(ends.reshape(count_x, lines, lanes), "tx", 0, 0, tiled=True)

    tab = class_scalars(lengths)
    sigma = level_sigma.reshape(1, lanes)
    m_table, x_table, y_table, corner, decay, cross = pl.pallas_call(
        tables_kernel,
        in_specs=[SMEM, SMEM, VMEM],
        out_specs=[VMEM] * 6,
        out_shape=[
            shape(2 * NCLASS, width, deep),
            shape(width, NCLASS * GROUP),
            shape(15, count_y, lanes, kind=F32),
            shape(6 * NCLASS * GROUP, height * GROUP),
            shape(lines, lanes, kind=F32),
            shape(lines, lanes),
        ],
        compiler_params=params(12),
        cost_estimate=cost(3),
        name="tables",
    )(lat_class, tab, lat_class.reshape(count_y, height))

    own_ends = pl.pallas_call(
        own_ends_kernel,
        in_specs=[SMEM, SMEM, HBM, VMEM],
        out_specs=VMEM,
        out_shape=shape(6, width, lanes, kind=F32),
        scratch_shapes=[
            pltpu.VMEM((BLOCK, width, lanes), F32),
            pltpu.VMEM((BLOCK, width, lanes), F32),
            pltpu.VMEM((3, width, lanes), F32),
            pltpu.VMEM((3, width, lanes), F32),
            pltpu.VMEM((3, 8, lanes), F32),
            pltpu.VMEM((height, width, lanes), BF16),
            pltpu.SemaphoreType.DMA((steps,)),
        ],
        compiler_params=params(60),
        cost_estimate=cost(7),
        name="own_y_ends",
    )(lat_class, tab, increments, m_table)

    states = pl.pallas_call(
        scan_kernel,
        in_specs=[VMEM] * 3,
        out_specs=VMEM,
        out_shape=shape(count_x, lines, lanes),
        scratch_shapes=[pltpu.VMEM((count_x, lines, lanes), F32)],
        compiler_params=params(8),
        cost_estimate=cost(1),
        name="x_scan",
    )(decay, cross, ends)

    with jax.named_scope("x_states_to_tiles"):
        states = lax.all_to_all(states, "tx", 0, 0, tiled=True).reshape(height * GROUP, lanes)

    y_ends = pl.pallas_call(
        corner_kernel,
        in_specs=[VMEM] * 5,
        out_specs=VMEM,
        out_shape=shape(count_y, 3 * width, lanes),
        scratch_shapes=[pltpu.VMEM((6, width, lanes), F32)],
        compiler_params=params(8),
        cost_estimate=cost(1),
        name="y_ends",
    )(corner, states, x_table, own_ends, y_table)

    with jax.named_scope("y_ends_to_column"):
        arrived = lax.all_to_all(y_ends, "ty", 0, 0, tiled=True)

    inner, coefs = pl.pallas_call(
        inner_kernel,
        in_specs=[SMEM, SMEM, HBM, VMEM, VMEM, VMEM, pl.BlockSpec(memory_space=pl.ANY)],
        out_specs=[HBM, VMEM],
        out_shape=[
            shape(height, width, lanes),
            shape(height * GROUP, lanes),
        ],
        scratch_shapes=[
            pltpu.VMEM((BLOCK, width, lanes), F32),
            pltpu.VMEM((BLOCK, width, lanes), F32),
            pltpu.VMEM((3, width + GROUP, lanes), F32),
            pltpu.VMEM((height, width, lanes), F32),
            pltpu.VMEM((height, GROUP, lanes), F32),
            pltpu.VMEM((height, width, lanes), BF16),
            pltpu.VMEM((height, width, lanes), BF16),
            pltpu.SemaphoreType.DMA((steps,)),
            pltpu.SemaphoreType.DMA((steps,)),
        ],
        compiler_params=params(60),
        cost_estimate=cost(10),
        name="inner",
    )(lat_class, tab, increments, states, m_table, sigma, y_ends)

    tile_out, peak_rows = pl.pallas_call(
        final_kernel,
        in_specs=[VMEM, HBM] + [VMEM] * 4,
        out_specs=[HBM, VMEM],
        out_shape=[shape(height, width, lanes), shape(lanes, lanes, kind=F32)],
        scratch_shapes=[
            pltpu.VMEM((width // (2 * GROUP), 12 * GROUP, 2 * lanes), BF16),
            pltpu.VMEM((height, width, lanes), BF16),
            pltpu.VMEM((height, width, lanes), BF16),
            pltpu.SemaphoreType.DMA((steps // 2,)),
            pltpu.SemaphoreType.DMA((steps // 2,)),
        ],
        compiler_params=params(60),
        cost_estimate=cost(5),
        name="final",
    )(y_table, inner, coefs, slab_owner.astype(F32).reshape(1, lanes), sigma, arrived)

    with jax.named_scope("peaks_to_owners"):
        peaks = lax.all_to_all(peak_rows, ("tx", "ty"), 0, 0, tiled=True)
    peak_table = jnp.max(peaks, axis=0, keepdims=True)[:, :MOST]
    return (tile_out, peak_table)


def solution(mesh):
    placed = (P("ty", "tx", None), P(), P(), P(), P())
    return jax.shard_map(
        local,
        mesh=mesh,
        in_specs=placed,
        out_specs=(P("ty", "tx", None), P(("tx", "ty"), None)),
        check_vma=False,
    )
```

```python
import functools

import jax
import jax.numpy as jnp
from jax import lax
from jax.experimental import pallas as pl
from jax.experimental.pallas import tpu as pltpu
from jax.sharding import PartitionSpec as P

NCLASS = 4
MOST = 2
SCALE_WEIGHTS = (0.5, 0.35, 0.25)
LOG, RATE, FWD, BWD, INV, ROW = 0, 3, 6, 9, 12, 32
GROUP = 8
BLOCK = 16
LONG = 48
TURNS = 6
CHUNK = 48
F32, BF16 = jnp.float32, jnp.bfloat16


def iota(shape, axis):
    return lax.broadcasted_iota(jnp.int32, shape, axis)


def class_scalars(lengths):
    log_rate = -1.0 / lengths
    rate = jnp.exp(log_rate)
    weights = jnp.array(SCALE_WEIGHTS, F32)[None, :]
    forward = weights * jnp.sqrt(1.0 - rate * rate)
    backward = weights * (1.0 - rate)
    inverse = -1.0 / jnp.expm1(log_rate[:, :, None] + log_rate[:, None, :])
    row = jnp.concatenate(
        [log_rate, rate, forward, backward, inverse.reshape(NCLASS, 9)], axis=1
    )
    return jnp.pad(row, ((0, 0), (0, ROW - row.shape[1]))).reshape(-1)


class Pieces:
    def __init__(self, source, target, done, rows):
        self.source, self.target, self.done, self.rows = source, target, done, rows
        self.count = source.shape[0] // rows

    def copy(self, piece):
        rows = pl.ds(pl.multiple_of(piece * self.rows, self.rows), self.rows)
        return pltpu.make_async_copy(self.source.at[rows], self.target.at[rows], self.done.at[piece])

    def start(self, order=None):
        for piece in range(self.count) if order is None else order:
            self.copy(piece).start()

    def wait(self):
        for piece in range(self.count):
            self.copy(piece).wait()


def start_all(sources, targets, done):
    copies = [
        pltpu.make_async_copy(source, target, done.at[i])
        for i, (source, target) in enumerate(zip(sources, targets))
    ]
    for copy in copies:
        copy.start()

    def wait():
        for copy in copies:
            copy.wait()

    return wait


def class_reader(tab_ref, c):
    return lambda at: tab_ref[c * ROW + at]


def ends_kernel(lat_ref, lengths_ref, v_ref, e_ref, w_ref, here_ref, arrived):
    height, width, lanes = v_ref.shape
    tile = lax.axis_index("ty") * height
    pieces = Pieces(v_ref, here_ref, arrived, LONG)
    pieces.start()
    shape = (GROUP, width)
    row = iota(shape, 0)
    at = iota(shape, 1).astype(F32)
    totals = []
    for c in range(NCLASS):
        log = [-1.0 / jnp.full(shape, lengths_ref[c, k], F32) for k in range(3)]
        rate = [jnp.exp(log[k]) for k in range(3)]
        fwd = [SCALE_WEIGHTS[k] * jnp.sqrt(1.0 - rate[k] * rate[k]) for k in range(3)]
        rest = [jnp.exp(log[k] * (width - at)) for k in range(3)]
        total = jnp.zeros(shape, F32)
        for k in range(3):
            fwd_end = fwd[k] * jnp.exp(log[k] * (width - 1 - at))
            total = jnp.where(row == k, fwd_end, total)
        for q in range(3):
            back = jnp.zeros(shape, F32)
            for k in range(3):
                back += fwd[k] * (1.0 - rest[k] * rest[q]) / (1.0 - rate[k] * rate[q])
            back = back * (SCALE_WEIGHTS[q] * (1.0 - rate[q])) * jnp.exp(log[q] * at)
            total = jnp.where(row == 3 + q, back, total)
        totals.append(total)
    for c in range(NCLASS):
        for d in range(NCLASS):
            w_ref[NCLASS * c + d] = jnp.concatenate([totals[c], totals[d]], axis=0).astype(BF16)

    def run(step, _):
        pieces.copy(step).wait()
        for r in range(0, LONG, 2):
            row = step * LONG + r
            pair = NCLASS * lat_ref[tile + row] + lat_ref[tile + row + 1]
            both = jnp.concatenate([here_ref[row], here_ref[row + 1]], axis=1)
            done = jnp.dot(w_ref[pair], both, preferred_element_type=F32)
            own = jnp.concatenate([done[:GROUP, :lanes], done[GROUP:, lanes:]], axis=0)
            at = pl.multiple_of(row * GROUP, 2 * GROUP)
            e_ref[pl.ds(at, 2 * GROUP), :] = own.astype(BF16)
        return 0

    lax.fori_loop(0, pieces.count, run, 0)


def scan_kernel(width, height, lat_ref, lengths_ref, e_ref, c_ref, decay_ref, cross_ref, f_ref):
    devices, lines, lanes = e_ref.shape
    fill_scan_tables(lat_ref, lengths_ref, width, height, decay_ref, cross_ref)
    decay = decay_ref[...]
    cross = cross_ref[:, :lines]
    state = jnp.zeros((lines, lanes), F32)
    for t in range(devices):
        f_ref[t] = state
        state = decay * state + e_ref[t].astype(F32)
    kind = iota((lines, lanes), 0) % GROUP
    state = jnp.zeros((lines, lanes), F32)
    for t in range(devices - 1, -1, -1):
        ahead = f_ref[t]
        c_ref[t] = jnp.where(kind < 3, ahead, jnp.where(kind < 6, state, 0.0)).astype(BF16)
        if t > 0:
            turned = jnp.dot(cross, ahead.astype(BF16), preferred_element_type=F32)
            state = decay * state + e_ref[t].astype(F32) + turned


def fill_scan_tables(lat_ref, lengths_ref, width, height, decay_ref, cross_ref):
    lines, lanes = decay_ref.shape
    rows = lines // GROUP
    first = lax.axis_index("ty") * height + lax.axis_index("tx") * rows
    row = iota((GROUP, lanes), 0)
    lane = iota((GROUP, lanes), 1)
    decay, cross = [], []
    for c in range(NCLASS):
        logs = [-1.0 / jnp.full((GROUP, lanes), lengths_ref[c, k], F32) for k in range(3)]
        rate = [jnp.exp(logs[k]) for k in range(3)]
        far = [jnp.exp(logs[k] * width) for k in range(3)]
        hold = jnp.zeros((GROUP, lanes), F32)
        mix = jnp.zeros((GROUP, lanes), F32)
        for k in range(3):
            hold = jnp.where((row == k) | (row == 3 + k), far[k], hold)
            for q in range(3):
                value = (SCALE_WEIGHTS[q] * (1.0 - rate[q])) * rate[k] * (
                    (1.0 - far[k] * far[q]) / (1.0 - rate[k] * rate[q])
                )
                mix = jnp.where((row == 3 + q) & (lane % GROUP == k), value, mix)
        decay.append(hold)
        cross.append(mix)
    for r in range(0, rows, 2):
        mixes = []
        for at in (r, r + 1):
            c = lat_ref[first + at]
            d, m = decay[0], cross[0]
            for other in range(1, NCLASS):
                d = jnp.where(c == other, decay[other], d)
                m = jnp.where(c == other, cross[other], m)
            decay_ref[pl.ds(at * GROUP, GROUP), :] = d
            mixes.append(jnp.where(lane // GROUP == at, m, 0.0))
        cross_ref[pl.ds(r * GROUP, 2 * GROUP), :] = jnp.concatenate(mixes, axis=0).astype(BF16)


def x_table_parts(tab_ref, c, width, depth):
    get = class_reader(tab_ref, c)
    out_at = iota((width, depth), 0).astype(F32)
    lane = iota((width, depth), 1)
    in_at = lane.astype(F32)
    far = jnp.maximum(out_at, in_at)
    later = out_at >= in_at
    gap = jnp.abs(out_at - in_at)
    near_power = [jnp.exp(get(LOG + k) * gap) for k in range(3)]
    rest_power = [jnp.exp(get(LOG + k) * jnp.maximum(width - far, 0.0)) for k in range(3)]
    own_rest = [jnp.exp(get(LOG + k) * (width - out_at)) for k in range(3)]
    inner = jnp.zeros((width, depth), F32)
    carried = [jnp.zeros((width, depth), F32) for _ in range(3)]
    for q in range(3):
        for k in range(3):
            inverse = get(INV + 3 * q + k)
            inner += (get(FWD + k) * get(BWD + q) * inverse) * (
                jnp.where(later, near_power[k], near_power[q])
                * (1.0 - rest_power[k] * rest_power[q])
            )
            carried[k] += (get(BWD + q) * inverse) * (1.0 - own_rest[k] * own_rest[q])
    inner = jnp.where(lane < width, inner, 0.0)
    for k in range(3):
        carried[k] = carried[k] * jnp.exp(get(LOG + k) * (out_at + 1.0))
    return lane, inner, carried + own_rest


EXACT = dict(precision=lax.Precision.HIGHEST, preferred_element_type=F32)


def of_class(tab_ref, lat, at):
    value = jnp.full(lat.shape, tab_ref[at], F32)
    for c in range(1, NCLASS):
        value = jnp.where(lat == c, tab_ref[c * ROW + at], value)
    return value


def over_points(rows):
    height = rows.shape[1]
    long = height * GROUP
    wider = (iota((height, long), 1) // GROUP == iota((height, long), 0)).astype(BF16)
    wide = jnp.dot(rows.astype(BF16), wider, preferred_element_type=F32)
    same = iota((GROUP, long), 1) % GROUP == iota((GROUP, long), 0)
    spread = [jnp.where(same, wide[q : q + 1], 0.0) for q in range(6)]
    return wide, jnp.concatenate(spread, axis=0).astype(BF16)


def tables_kernel(
    lat_ref, tab_ref, lat_tiles_ref, m_ref, x_ref, y_ref, corner_ref,
    own_ref, ends_ref, local_ref, scan_ref,
):
    _, width, depth = m_ref.shape
    lanes = y_ref.shape[2]
    devices, height = lat_tiles_ref.shape
    spread = jnp.zeros((width, depth), F32)
    for c in range(NCLASS):
        lane, inner, states = x_table_parts(tab_ref, c, width, depth)
        for parity in range(2):
            table = inner
            for k in range(6):
                table = jnp.where(lane == width + GROUP * parity + k, states[k], table)
            m_ref[2 * c + parity] = table.astype(BF16)
        for k in range(6):
            spread = jnp.where(lane == c * GROUP + k, states[k], spread)
    x_ref[...] = spread[:, : x_ref.shape[1]].astype(BF16)

    def by_class(lat, at):
        return of_class(tab_ref, lat, at)

    row, column = iota((height, height), 0), iota((height, height), 1)
    upto = (row <= column).astype(F32)
    lat = lat_tiles_ref[...]
    logs = [by_class(lat, LOG + k) for k in range(3)]
    level = jnp.dot(jnp.concatenate(logs, axis=0), upto, **EXACT)
    levels = [level[k * devices : (k + 1) * devices] for k in range(3)]
    reach = [jnp.exp(levels[k]) for k in range(3)]
    cross = []
    for q in range(3):
        gain = by_class(lat, BWD + q) * jnp.exp(levels[q] - logs[q])
        for k in range(3):
            mixed = jnp.sum(gain * reach[k], axis=1, keepdims=True)
            cross.append(jnp.broadcast_to(mixed, (devices, lanes)))
    fill_y_tables(levels, cross, y_ref)

    own = jnp.broadcast_to(lat_tiles_ref[pl.ds(lax.axis_index("ty"), 1), :], (GROUP, height))
    fill_block_tables(tab_ref, own, ends_ref, local_ref, scan_ref)
    _, _, ends, _, _, _, _ = two_passes(tab_ref, own, row >= 0)
    total, own_ref[...] = over_points(ends)
    corner_ref[...] = total


def two_passes(tab_ref, lat, same):
    height = lat.shape[1]
    lanes = 128
    kind = iota((GROUP, height), 0)
    row, column = iota((height, height), 0), iota((height, height), 1)
    log = jnp.zeros((GROUP, height), F32)
    forward = jnp.zeros((GROUP, height), F32)
    backward = jnp.zeros((GROUP, height), F32)
    for k in range(3):
        log = jnp.where(kind == k, of_class(tab_ref, lat, LOG + k), log)
        forward = jnp.where(kind == k, of_class(tab_ref, lat, FWD + k), forward)
        backward = jnp.where(kind == k, of_class(tab_ref, lat, BWD + k), backward)
    turn = (((1,), (1,)), ((), ()))
    upto = jnp.dot(log, (same & (row <= column)).astype(F32), **EXACT)
    every = jnp.dot(log, same.astype(F32), **EXACT)
    before = upto - log
    upto_down = lax.dot_general((same & (column <= row)).astype(F32), log, turn, **EXACT)
    before_down = lax.dot_general((same & (column < row)).astype(F32), log, turn, **EXACT)
    every_down = lax.dot_general(same.astype(F32), log, turn, **EXACT)
    ahead = jnp.zeros((height, height), F32)
    back = jnp.zeros((height, height), F32)
    for k in range(3):
        gap = jnp.minimum(upto_down[:, k : k + 1] - upto[k : k + 1], 0.0)
        ahead += jnp.exp(gap) * forward[k : k + 1]
        gap = jnp.minimum(before[k : k + 1] - before_down[:, k : k + 1], 0.0)
        back += jnp.exp(gap) * backward[k : k + 1]
    ahead = jnp.where(same & (row >= column), ahead, 0.0)
    back = jnp.where(same & (row <= column), back, 0.0)

    gain = backward * jnp.exp(before)
    turned = jnp.dot(gain, ahead, **EXACT)
    ends = [(forward * jnp.exp(every - upto))[:3], turned[:3], lat[:1].astype(F32), lat[:1].astype(F32)]
    from_ahead = jnp.dot(back, jnp.exp(upto_down), **EXACT)
    from_back = jnp.exp(every_down - before_down)
    lane = iota((height, lanes), 1)
    entering = jnp.zeros((height, lanes), F32)
    for k in range(3):
        entering = jnp.where(lane % 48 // GROUP == k, from_ahead[:, k : k + 1], entering)
        entering = jnp.where(lane % 48 // GROUP == 3 + k, from_back[:, k : k + 1], entering)
    rest = entering - entering.astype(BF16).astype(F32)
    entering = jnp.where(lane < 48, entering, jnp.where(lane < 96, rest, 0.0)).astype(BF16)
    return ahead, back, jnp.concatenate(ends, axis=0), entering, gain, upto, every


def fill_block_tables(tab_ref, lat, ends_ref, local_ref, scan_ref):
    height = lat.shape[1]
    blocks, _, lanes = scan_ref.shape
    same = iota((height, height), 0) // BLOCK == iota((height, height), 1) // BLOCK
    ahead, back, ends, entering, gain, upto, every = two_passes(tab_ref, lat, same)
    _, ends_ref[...] = over_points(ends)

    reach = jnp.exp(upto)
    steps = [jnp.exp(every)[:3]]
    for q in range(3):
        steps.append(jnp.dot(gain[q : q + 1] * reach, same.astype(F32), **EXACT)[:3])
    steps = jnp.concatenate(steps + [jnp.zeros((4, height), F32)], axis=0)
    pick = (iota((height, lanes), 0) == iota((height, lanes), 1) * BLOCK).astype(F32)
    steps = jnp.dot(steps, pick, **EXACT)
    for block in range(blocks):
        scan_ref[block] = jnp.broadcast_to(steps[:, block : block + 1], steps.shape)

    inner = jnp.dot(back, ahead, **EXACT)
    fold = (iota((height, lanes), 0) % BLOCK == iota((height, lanes), 1) // GROUP).astype(BF16)
    inner = jnp.dot(inner.astype(BF16), fold, preferred_element_type=F32).astype(BF16)
    local_ref[...] = jnp.concatenate([inner, entering], axis=1)


def each_point(rows):
    count = rows.shape[0]
    long = count * GROUP
    taller = (iota((long, count), 0) // GROUP == iota((long, count), 1)).astype(BF16)
    whole = jnp.dot(taller, rows, preferred_element_type=F32)
    same_point = iota(whole.shape, 0) % GROUP == iota(whole.shape, 1) % GROUP
    return jnp.where(same_point, whole, 0.0).astype(BF16)


def fill_y_tables(levels, cross, y_ref):
    _, devices, lanes = y_ref.shape
    mine = lax.axis_index("ty")
    row = iota((devices, lanes), 0)
    before, upto, my_before, my_upto = [], [], [], []
    for k in range(3):
        level = jnp.broadcast_to(levels[k][:, -1:], (devices, lanes))
        total = jnp.zeros((devices, lanes), F32)
        for u in range(devices - 1):
            total += jnp.where(row > u, level[u : u + 1], 0.0)
        before.append(total)
        upto.append(total + level)
        my_before.append(jnp.sum(jnp.where(row == mine, total, 0.0), axis=0, keepdims=True))
        my_upto.append(jnp.sum(jnp.where(row == mine, total + level, 0.0), axis=0, keepdims=True))
        y_ref[12 + k] = jnp.broadcast_to(jnp.exp(my_upto[k] - my_before[k]), (devices, lanes))

    def decay(gap):
        return jnp.exp(jnp.minimum(gap, 0.0))

    for q in range(3):
        y_ref[q] = jnp.where(row < mine, decay(my_before[q] - upto[q]), 0.0)
        back = [decay(before[q][u : u + 1] - upto[q]) for u in range(devices)]
        for k in range(3):
            turned = jnp.zeros((devices, lanes), F32)
            for u in range(1, devices):
                ahead = decay(before[k][u : u + 1] - my_upto[k]) * cross[3 * q + k][u : u + 1]
                turned += jnp.where(mine < u, back[u] * ahead, 0.0)
            straight = decay(before[k] - my_upto[k]) if q == k else 0.0
            y_ref[3 + 3 * q + k] = jnp.where(row > mine, straight, turned)


def block_rows(step):
    lines = BLOCK * GROUP
    return pl.ds(pl.multiple_of(step * lines, lines), lines)


def store_points(wide_ref, row, pair):
    width, lanes = pair[0].shape
    at = pl.multiple_of(row * GROUP, 2 * GROUP)
    for piece in range(width // (2 * GROUP)):
        for half in range(2):
            rows = slice((2 * piece + half) * GROUP, (2 * piece + half + 1) * GROUP)
            both = jnp.concatenate([pair[0][rows], pair[1][rows]], axis=0)
            here = slice(half * lanes, (half + 1) * lanes)
            wide_ref[piece, pl.ds(at, 2 * GROUP), here] = both.astype(BF16)


def own_ends_kernel(
    lat_ref, v_ref, m_far, weight_far,
    e_ref, sum_ref, even_ref, odd_ref, here_ref, arrived, m_ref, weight_ref, fetched,
):
    height, width, lanes = v_ref.shape
    pieces = Pieces(v_ref, here_ref, arrived, 2 * BLOCK)
    wait = start_all([m_far, weight_far], [m_ref, weight_ref], fetched)
    pieces.start()
    tile = lax.axis_index("ty") * height
    sum_ref[...] = jnp.zeros_like(sum_ref)

    def along_x(step, block_ref):
        for r in range(0, BLOCK, 2):
            pair = []
            for at in (r, r + 1):
                row = step * BLOCK + at
                table = m_ref[2 * lat_ref[tile + row]][:, :width]
                pair.append(jnp.dot(table, here_ref[row], preferred_element_type=F32))
            store_points(block_ref, r, pair)

    def along_y(step, block_ref):
        weight = weight_ref[:, block_rows(step)]
        for piece in range(sum_ref.shape[0]):
            sum_ref[piece] += jnp.dot(weight, block_ref[piece], preferred_element_type=F32)

    wait()
    in_turn(pieces, along_x, along_y, even_ref, odd_ref)
    for piece in range(sum_ref.shape[0]):
        for half in range(2):
            for q in range(6):
                here = pl.ds((2 * piece + half) * GROUP, GROUP)
                part = sum_ref[piece, pl.ds(q * GROUP, GROUP), half * lanes : (half + 1) * lanes]
                e_ref[q, here, :] = part


def corner_kernel(corner_ref, c_ref, x_ref, own_ref, y_ref, send_ref, e_ref):
    group = x_ref.shape[1]
    devices = send_ref.shape[0]
    _, width, _ = own_ref.shape
    long = corner_ref.shape[1]
    pick = iota((group, long), 0)
    chosen = (corner_ref[pl.ds(6, 1), :] == (pick // GROUP).astype(F32)) & (
        iota((group, long), 1) % GROUP == pick % GROUP
    )
    corner = [jnp.where(chosen, corner_ref[pl.ds(q, 1), :], 0.0).astype(BF16) for q in range(6)]
    corner = jnp.concatenate(corner, axis=0)
    sums = jnp.dot(corner, c_ref[...], preferred_element_type=F32).astype(BF16)
    for q in range(6):
        part = sums[q * group : (q + 1) * group]
        e_ref[q] = own_ref[q] + jnp.dot(x_ref[...], part, preferred_element_type=F32)
    for at in range(0, width, CHUNK):
        ends = [e_ref[q, pl.ds(at, CHUNK), :] for q in range(6)]
        for u in range(devices):
            for q in range(3):
                total = y_ref[q, pl.ds(u, 1), :] * ends[3 + q]
                for k in range(3):
                    total += y_ref[3 + 3 * q + k, pl.ds(u, 1), :] * ends[k]
                send_ref[u, pl.ds(q * width + at, CHUNK), :] = total.astype(BF16)


def in_turn(pieces, produce, use, even_ref, odd_ref):
    steps = 2 * pieces.count
    pieces.copy(0).wait()
    produce(0, even_ref)

    def pair(i, _):
        pieces.copy(i + 1).wait()
        produce(2 * i + 1, odd_ref)
        use(2 * i, even_ref)
        produce(2 * i + 2, even_ref)
        use(2 * i + 1, odd_ref)
        return 0

    lax.fori_loop(0, pieces.count - 1, pair, 0)
    produce(steps - 1, odd_ref)
    use(steps - 2, even_ref)
    use(steps - 1, odd_ref)


def filter_kernel(
    lat_ref, v_ref, c_far, m_far, ends_far, after_ref,
    wide_far, end_far, c_ref, m_ref, ends_ref, fetched, even_ref, odd_ref, wide_ref, end_ref,
    here_ref, arrived, sent, end_sent,
):
    del after_ref
    height, width, lanes = v_ref.shape
    pieces = Pieces(v_ref, here_ref, arrived, 2 * BLOCK)
    results = Pieces(wide_ref, wide_far, sent, 1)
    end_results = Pieces(end_ref, end_far, end_sent, 1)
    wait = start_all([c_far, m_far, ends_far], [c_ref, m_ref, ends_ref], fetched)
    pieces.start()
    tile = lax.axis_index("ty") * height

    def along_x(step, block_ref):
        for r in range(0, BLOCK, 2):
            pair = []
            at = pl.multiple_of((step * BLOCK + r) * GROUP, 2 * GROUP)
            states = c_ref[pl.ds(at, 2 * GROUP), :]
            for parity in range(2):
                row = step * BLOCK + r + parity
                right = jnp.concatenate([here_ref[row], states], axis=0)
                table = m_ref[2 * lat_ref[tile + row] + parity]
                pair.append(jnp.dot(table, right, preferred_element_type=F32))
            store_points(block_ref, r, pair)

    def ends(step, block_ref):
        weight = ends_ref[:, block_rows(step)]
        for piece in range(wide_ref.shape[1]):
            block = block_ref[piece]
            wide_ref[step, piece] = block
            done = jnp.dot(weight, block, preferred_element_type=F32)
            end_ref[step, piece] = done.astype(BF16)
        results.copy(step).start()
        end_results.copy(step).start()

    wait()
    in_turn(pieces, along_x, ends, even_ref, odd_ref)
    results.wait()
    end_results.wait()


def y_carries(y_ref, arrived_ref, f_ref):
    devices = arrived_ref.shape[0]
    lanes = arrived_ref.shape[2]
    width = arrived_ref.shape[1] // 3
    mine = lax.axis_index("ty")
    mixed = [
        [
            y_ref[3 + 3 * q + k, pl.ds(mine, 1), :] * y_ref[12 + k, pl.ds(0, 1), :]
            for k in range(3)
        ]
        for q in range(3)
    ]
    for at in range(0, width, 2 * GROUP):
        ahead = [jnp.zeros((2 * GROUP, lanes), F32) for _ in range(3)]
        back = list(ahead)
        for u in range(devices):
            for q in range(3):
                came = arrived_ref[u, pl.ds(q * width + at, 2 * GROUP), :].astype(F32)
                ahead[q] += jnp.where(u < mine, came, 0.0)
                back[q] += jnp.where(u < mine, 0.0, came)
        states = list(ahead)
        for q in range(3):
            total = back[q]
            for k in range(3):
                total += mixed[q][k] * ahead[k]
            states.append(total)
        for half in range(2):
            for k in range(6):
                part = states[k][half * GROUP : (half + 1) * GROUP]
                place = pl.ds(k * GROUP, GROUP)
                f_ref[at // (2 * GROUP), place, half * lanes : (half + 1) * lanes] = part


def scan_blocks(scan_ref, end_ref, f_ref, ahead_ref, state_ref):
    steps, count, _, _ = end_ref.shape

    def at(k):
        return pl.ds(k * GROUP, GROUP)

    def factor(step, plane):
        row = scan_ref[step, pl.ds(plane, 1), :]
        return jnp.concatenate([row, row], axis=1)

    def two(step, piece, k):
        pair = end_ref[step, piece, pl.ds(k * GROUP, 2 * GROUP), :].astype(F32)
        return pair[:GROUP], pair[GROUP:]

    def ends_of(step, piece):
        return [part for k in range(0, 6, 2) for part in two(step, piece, k)]

    def forward(step, _):
        for piece in range(count):
            ends = ends_of(step, piece)
            for k in range(3):
                state = f_ref[piece, at(k), :]
                ahead_ref[step, piece, at(k), :] = state
                f_ref[piece, at(k), :] = factor(step, k) * state + ends[k]
        return 0

    def backward(i, _):
        step = steps - 1 - i
        for piece in range(count):
            ends = ends_of(step, piece)
            states = [ahead_ref[step, piece, at(k), :] for k in range(3)]
            for q in range(3):
                state = f_ref[piece, at(3 + q), :]
                states.append(state)
                total = factor(step, q) * state + ends[3 + q]
                for k in range(3):
                    total += factor(step, 3 + 3 * q + k) * states[k]
                f_ref[piece, at(3 + q), :] = total
            for k in range(0, 6, 2):
                pair = jnp.concatenate([states[k], states[k + 1]], axis=0)
                state_ref[step, piece, pl.ds(k * GROUP, 2 * GROUP), :] = pair.astype(BF16)
        return 0

    lax.fori_loop(0, steps, forward, 0)
    lax.fori_loop(0, steps, backward, 0)


def fill_held(owner, held_ref):
    slabs = owner.shape[1]
    across = jnp.broadcast_to(owner, (slabs, slabs))
    down = across.T
    row, lane = iota((slabs, slabs), 0), iota((slabs, slabs), 1)
    earlier = jnp.where((across == down) & (row < lane), 1.0, 0.0)
    rank = jnp.sum(earlier, axis=0, keepdims=True)
    for slot in range(MOST):
        held_ref[slot] = jnp.where((across == row.astype(F32)) & (rank == slot), 1.0, 0.0)


def whole_rows(left_ref, wide_ref, state_ref, step, sigma, take):
    _, count, lines, lanes = wide_ref.shape
    lanes //= 2
    left = left_ref[block_rows(step), :][:, : lines + 12 * GROUP]
    for piece in range(count):
        states = state_ref[step, piece]
        right = jnp.concatenate([wide_ref[step, piece], states, states], axis=0)
        result = jnp.dot(left, right, preferred_element_type=F32)
        here = pl.ds(piece * 2 * GROUP, 2 * GROUP)
        for r in range(BLOCK):
            part = result[r * GROUP : (r + 1) * GROUP]
            part = jnp.concatenate([part[:, :lanes], part[:, lanes:]], axis=0)
            take(step * BLOCK + r, here, part * sigma)


def final_kernel(
    y_far, wide_far, end_far, local_far, scan_far, owner_ref, sigma_ref, arrived_ref,
    out_ref, peak_ref, wide_ref, arrived, end_ref, y_ref, local_ref, scan_ref, fetched, fetched_small,
    held_ref, f_ref, ahead_ref, state_ref, done_ref, sent, left_ref,
):
    steps = wide_far.shape[0]
    lanes = peak_ref.shape[1]
    pieces = Pieces(wide_far, wide_ref, arrived, TURNS)
    results = Pieces(done_ref, out_ref, sent, TURNS * BLOCK)
    wait_small = start_all([local_far, y_far, scan_far], [local_ref, y_ref, scan_ref], fetched_small)
    wait = start_all([end_far], [end_ref], fetched)
    pieces.start()
    fill_held(owner_ref[...], held_ref)
    wait_small()
    lines = BLOCK * GROUP
    for step in range(steps):
        whole = each_point(local_ref[pl.ds(step * BLOCK, BLOCK), :])
        left_ref[pl.ds(step * lines, lines), :] = whole
    y_carries(y_ref, arrived_ref, f_ref)
    wait()
    scan_blocks(scan_ref, end_ref, f_ref, ahead_ref, state_ref)
    sigma = jnp.broadcast_to(sigma_ref[...], (2 * GROUP, lanes))

    def run(i, most):
        most = list(most)

        def take(row, here, scaled):
            at = len(taken) % 2
            taken.append(row)
            most[at] = jnp.maximum(most[at], jnp.abs(scaled))
            done_ref[row, here, :] = scaled.astype(BF16)

        taken = []
        pieces.copy(i).wait()
        for step in range(TURNS):
            whole_rows(left_ref, wide_ref, state_ref, TURNS * i + step, sigma, take)
        results.copy(i).start()
        return tuple(most)

    start = tuple(jnp.zeros((2 * GROUP, lanes), F32) for _ in range(2))
    most = lax.fori_loop(0, steps // TURNS, run, start)
    peaks = jnp.max(jnp.maximum(*most), axis=0, keepdims=True)
    lane = iota(peak_ref.shape, 1)
    rows = jnp.zeros(peak_ref.shape, F32)
    for slot in range(MOST):
        held = jnp.sum(held_ref[slot] * peaks, axis=1, keepdims=True)
        rows = jnp.where(lane == slot, held, rows)
    peak_ref[...] = rows
    results.wait()


SMEM = pl.BlockSpec(memory_space=pltpu.SMEM)
VMEM = pl.BlockSpec(memory_space=pltpu.VMEM)
HBM = pl.BlockSpec(memory_space=pltpu.HBM)
MIB = 1024 * 1024
FULL = 61
LAST = 55


def call(kernel, name, ins, outs, scratch, mib, us):
    return pl.pallas_call(
        kernel,
        in_specs=ins,
        out_specs=[spec for spec, _ in outs],
        out_shape=[array for _, array in outs],
        scratch_shapes=scratch,
        compiler_params=pltpu.CompilerParams(vmem_limit_bytes=mib * MIB),
        cost_estimate=pl.CostEstimate(flops=0, bytes_accessed=int(us * 3e6), transcendentals=0),
        name=name,
    )


def shape(*dims, kind=BF16):
    return jax.ShapeDtypeStruct(dims, kind)


def copies(count):
    return pltpu.SemaphoreType.DMA((count,))


def x_ends(lat_class, lengths, increments):
    height, width, lanes = increments.shape
    return call(
        ends_kernel,
        "x_ends",
        [SMEM, SMEM, HBM],
        [(VMEM, shape(height * GROUP, lanes))],
        [
            pltpu.VMEM((NCLASS * NCLASS, 2 * GROUP, width), BF16),
            pltpu.VMEM((height, width, lanes), BF16),
            copies(height // LONG),
        ],
        FULL,
        4,
    )(lat_class, lengths, increments)[0]


def tables(lat_class, tab, lat_tiles, width, lanes):
    count, height = lat_tiles.shape
    return call(
        tables_kernel,
        "tables",
        [SMEM, SMEM, VMEM],
        [
            (VMEM, shape(2 * NCLASS, width, width + 2 * GROUP)),
            (VMEM, shape(width, NCLASS * GROUP)),
            (VMEM, shape(15, count, lanes, kind=F32)),
            (VMEM, shape(GROUP, height * GROUP, kind=F32)),
            (VMEM, shape(6 * GROUP, height * GROUP)),
            (VMEM, shape(6 * GROUP, height * GROUP)),
            (VMEM, shape(height, 2 * lanes)),
            (VMEM, shape(height // BLOCK, 16, lanes, kind=F32)),
        ],
        [],
        FULL,
        6,
    )(lat_class, tab, lat_tiles)


def own_y_ends(lat_class, increments, m_table, weights):
    height, width, lanes = increments.shape
    pieces = width // (2 * GROUP)
    block = pltpu.VMEM((pieces, BLOCK * GROUP, 2 * lanes), BF16)
    return call(
        own_ends_kernel,
        "own_y_ends",
        [SMEM, HBM, HBM, HBM],
        [(VMEM, shape(6, width, lanes, kind=F32))],
        [
            pltpu.VMEM((pieces, 6 * GROUP, 2 * lanes), F32),
            block,
            block,
            pltpu.VMEM((height, width, lanes), BF16),
            copies(height // (2 * BLOCK)),
            pltpu.VMEM(m_table.shape, m_table.dtype),
            pltpu.VMEM(weights.shape, weights.dtype),
            copies(2),
        ],
        FULL,
        6,
    )(lat_class, increments, m_table, weights)[0]


def x_scan(lat_class, lengths, ends, width, height):
    _, lines, lanes = ends.shape
    return call(
        functools.partial(scan_kernel, width, height),
        "x_scan",
        [SMEM, SMEM, VMEM],
        [(VMEM, shape(*ends.shape))],
        [pltpu.VMEM((lines, lanes), F32), pltpu.VMEM((lines, lanes), BF16), pltpu.VMEM(ends.shape, F32)],
        8,
        1,
    )(lat_class, lengths, ends)[0]


def y_ends(corner, states, x_table, own, y_table):
    _, width, lanes = own.shape
    return call(
        corner_kernel,
        "y_ends",
        [VMEM] * 5,
        [(VMEM, shape(y_table.shape[1], 3 * width, lanes))],
        [pltpu.VMEM((6, width, lanes), F32)],
        8,
        1,
    )(corner, states, x_table, own, y_table)[0]


def x_filter(lat_class, increments, states, m_table, ends, after):
    height, width, lanes = increments.shape
    pieces = width // (2 * GROUP)
    steps = height // BLOCK
    wide = (steps, pieces, BLOCK * GROUP, 2 * lanes)
    end = (steps, pieces, 6 * GROUP, 2 * lanes)
    return call(
        filter_kernel,
        "x_filter",
        [SMEM] + [HBM] * 5,
        [(HBM, shape(*wide)), (HBM, shape(*end))],
        [pltpu.VMEM(array.shape, array.dtype) for array in (states, m_table, ends)]
        + [
            copies(3),
            pltpu.VMEM(wide[1:], BF16),
            pltpu.VMEM(wide[1:], BF16),
            pltpu.VMEM(wide, BF16),
            pltpu.VMEM(end, BF16),
            pltpu.VMEM((height, width, lanes), BF16),
            copies(steps // 2),
            copies(steps),
            copies(steps),
        ],
        FULL,
        8,
    )(lat_class, increments, states, m_table, ends, after)


def tile_output(y_table, wide, ends, local, scan, owner, sigma, arrived, height, width):
    steps, pieces, lines, lanes = ends.shape
    half = lanes // 2
    return call(
        final_kernel,
        "tile_output",
        [HBM] * 5 + [VMEM] * 3,
        [(HBM, shape(height, width, half)), (VMEM, shape(half, half, kind=F32))],
        [
            pltpu.VMEM(wide.shape, wide.dtype),
            copies(steps // TURNS),
            pltpu.VMEM(ends.shape, ends.dtype),
            pltpu.VMEM(y_table.shape, y_table.dtype),
            pltpu.VMEM(local.shape, local.dtype),
            pltpu.VMEM(scan.shape, scan.dtype),
            copies(1),
            copies(3),
            pltpu.VMEM((MOST, half, half), F32),
            pltpu.VMEM((pieces, lines, lanes), F32),
            pltpu.VMEM((steps, pieces, lines // 2, lanes), F32),
            pltpu.VMEM(ends.shape, BF16),
            pltpu.VMEM((height, width, half), BF16),
            copies(steps // TURNS),
            pltpu.VMEM((height * GROUP, lanes), BF16),
        ],
        LAST,
        8,
    )(y_table, wide, ends, local, scan, owner, sigma, arrived)


def local(increments, lengths, lat_class, slab_owner, level_sigma):
    count_x = lax.axis_size("tx")
    count_y = lax.axis_size("ty")
    height, width, lanes = increments.shape
    lines = height // count_x * GROUP

    ends = x_ends(lat_class, lengths, increments)
    ends, lengths, lat_class = lax.optimization_barrier((ends, lengths, lat_class))
    with jax.named_scope("x_ends_to_scanners"):
        ends = lax.all_to_all(ends.reshape(count_x, lines, lanes), "tx", 0, 0, tiled=True)

    tab = class_scalars(lengths)
    sigma = level_sigma.reshape(1, lanes)
    owner = slab_owner.astype(F32).reshape(1, lanes)
    lat_tiles = lat_class.reshape(count_y, height)
    (
        m_table, x_table, y_table, corner,
        weights, block_ends, block_local, block_scan,
    ) = tables(lat_class, tab, lat_tiles, width, lanes)

    ends, m_table = lax.optimization_barrier((ends, m_table))
    states = x_scan(lat_class, lengths, ends, width, height)
    with jax.named_scope("x_states_to_tiles"):
        states = lax.all_to_all(states, "tx", 0, 0, tiled=True).reshape(height * GROUP, lanes)
    own = own_y_ends(lat_class, increments, m_table, weights)

    sent = y_ends(corner, states, x_table, own, y_table)
    with jax.named_scope("y_ends_to_column"):
        arrived = lax.all_to_all(sent, "ty", 0, 0, tiled=True)
    wide, ends = x_filter(lat_class, increments, states, m_table, block_ends, sent)

    tile_out, peak_rows = tile_output(
        y_table, wide, ends, block_local, block_scan, owner, sigma, arrived, height, width
    )
    with jax.named_scope("peaks_to_owners"):
        peaks = lax.all_to_all(peak_rows, ("tx", "ty"), 0, 0, tiled=True)
    peak_table = jnp.max(peaks, axis=0, keepdims=True)[:, :MOST]
    return (tile_out, peak_table)


def solution(mesh):
    placed = (P("ty", "tx", None), P(), P(), P(), P())
    return jax.shard_map(
        local,
        mesh=mesh,
        in_specs=placed,
        out_specs=(P("ty", "tx", None), P(("tx", "ty"), None)),
        check_vma=False,
    )
```

```python
import functools

import jax
import jax.numpy as jnp
from jax import lax
from jax.experimental import pallas as pl
from jax.experimental.pallas import tpu as pltpu
from jax.sharding import PartitionSpec as P

NCLASS = 4
MOST = 2
SCALE_WEIGHTS = (0.5, 0.35, 0.25)
LOG, RATE, FWD, BWD, INV = 0, 3, 6, 9, 12
GROUP = 8
BLOCK = 16
LONG = 48
TURNS = 6
CHUNK = 48
F32, BF16 = jnp.float32, jnp.bfloat16


def iota(shape, axis):
    return lax.broadcasted_iota(jnp.int32, shape, axis)


def class_rows(lengths_ref, lanes):
    rows = []
    for c in range(NCLASS):
        log = [-1.0 / jnp.full((1, lanes), lengths_ref[c, k], F32) for k in range(3)]
        rate = [jnp.exp(log[k]) for k in range(3)]
        forward = [SCALE_WEIGHTS[k] * jnp.sqrt(1.0 - rate[k] * rate[k]) for k in range(3)]
        backward = [SCALE_WEIGHTS[k] * (1.0 - rate[k]) for k in range(3)]
        inverse = [1.0 / (1.0 - rate[k] * rate[q]) for q in range(3) for k in range(3)]
        rows.append(log + rate + forward + backward + inverse)
    return rows


class Pieces:
    def __init__(self, source, target, done, rows):
        self.source, self.target, self.done, self.rows = source, target, done, rows
        self.count = source.shape[0] // rows

    def copy(self, piece):
        rows = pl.ds(pl.multiple_of(piece * self.rows, self.rows), self.rows)
        return pltpu.make_async_copy(self.source.at[rows], self.target.at[rows], self.done.at[piece])

    def start(self, order=None):
        for piece in range(self.count) if order is None else order:
            self.copy(piece).start()

    def wait(self):
        for piece in range(self.count):
            self.copy(piece).wait()


def start_all(sources, targets, done):
    copies = [
        pltpu.make_async_copy(source, target, done.at[i])
        for i, (source, target) in enumerate(zip(sources, targets))
    ]
    for copy in copies:
        copy.start()

    def wait():
        for copy in copies:
            copy.wait()

    return wait


def class_reader(rows, c, lanes):
    return lambda at: rows[c][at][:, :lanes]


def ends_kernel(lat_ref, lengths_ref, v_ref, e_ref, w_ref, here_ref, arrived):
    height, width, lanes = v_ref.shape
    tile = lax.axis_index("ty") * height
    pieces = Pieces(v_ref, here_ref, arrived, LONG)
    pieces.start()
    shape = (GROUP, width)
    row = iota(shape, 0)
    at = iota(shape, 1).astype(F32)
    totals = []
    for c in range(NCLASS):
        log = [-1.0 / jnp.full(shape, lengths_ref[c, k], F32) for k in range(3)]
        rate = [jnp.exp(log[k]) for k in range(3)]
        fwd = [SCALE_WEIGHTS[k] * jnp.sqrt(1.0 - rate[k] * rate[k]) for k in range(3)]
        rest = [jnp.exp(log[k] * (width - at)) for k in range(3)]
        total = jnp.zeros(shape, F32)
        for k in range(3):
            fwd_end = fwd[k] * jnp.exp(log[k] * (width - 1 - at))
            total = jnp.where(row == k, fwd_end, total)
        for q in range(3):
            back = jnp.zeros(shape, F32)
            for k in range(3):
                back += fwd[k] * (1.0 - rest[k] * rest[q]) / (1.0 - rate[k] * rate[q])
            back = back * (SCALE_WEIGHTS[q] * (1.0 - rate[q])) * jnp.exp(log[q] * at)
            total = jnp.where(row == 3 + q, back, total)
        totals.append(total)
    for c in range(NCLASS):
        for d in range(NCLASS):
            w_ref[NCLASS * c + d] = jnp.concatenate([totals[c], totals[d]], axis=0).astype(BF16)

    def run(step, _):
        pieces.copy(step).wait()
        for r in range(0, LONG, 2):
            row = step * LONG + r
            pair = NCLASS * lat_ref[tile + row] + lat_ref[tile + row + 1]
            both = jnp.concatenate([here_ref[row], here_ref[row + 1]], axis=1)
            done = jnp.dot(w_ref[pair], both, preferred_element_type=F32)
            own = jnp.concatenate([done[:GROUP, :lanes], done[GROUP:, lanes:]], axis=0)
            at = pl.multiple_of(row * GROUP, 2 * GROUP)
            e_ref[pl.ds(at, 2 * GROUP), :] = own.astype(BF16)
        return 0

    lax.fori_loop(0, pieces.count, run, 0)


def scan_kernel(width, height, lat_ref, lengths_ref, e_ref, c_ref, decay_ref, cross_ref, f_ref):
    devices, lines, lanes = e_ref.shape
    fill_scan_tables(lat_ref, lengths_ref, width, height, decay_ref, cross_ref)
    decay = decay_ref[...]
    cross = cross_ref[:, :lines]
    state = jnp.zeros((lines, lanes), F32)
    for t in range(devices):
        f_ref[t] = state
        state = decay * state + e_ref[t].astype(F32)
    kind = iota((lines, lanes), 0) % GROUP
    state = jnp.zeros((lines, lanes), F32)
    for t in range(devices - 1, -1, -1):
        ahead = f_ref[t]
        c_ref[t] = jnp.where(kind < 3, ahead, jnp.where(kind < 6, state, 0.0)).astype(BF16)
        if t > 0:
            turned = jnp.dot(cross, ahead.astype(BF16), preferred_element_type=F32)
            state = decay * state + e_ref[t].astype(F32) + turned


def fill_scan_tables(lat_ref, lengths_ref, width, height, decay_ref, cross_ref):
    lines, lanes = decay_ref.shape
    rows = lines // GROUP
    first = lax.axis_index("ty") * height + lax.axis_index("tx") * rows
    row = iota((GROUP, lanes), 0)
    lane = iota((GROUP, lanes), 1)
    decay, cross = [], []
    for c in range(NCLASS):
        logs = [-1.0 / jnp.full((GROUP, lanes), lengths_ref[c, k], F32) for k in range(3)]
        rate = [jnp.exp(logs[k]) for k in range(3)]
        far = [jnp.exp(logs[k] * width) for k in range(3)]
        hold = jnp.zeros((GROUP, lanes), F32)
        mix = jnp.zeros((GROUP, lanes), F32)
        for k in range(3):
            hold = jnp.where((row == k) | (row == 3 + k), far[k], hold)
            for q in range(3):
                value = (SCALE_WEIGHTS[q] * (1.0 - rate[q])) * rate[k] * (
                    (1.0 - far[k] * far[q]) / (1.0 - rate[k] * rate[q])
                )
                mix = jnp.where((row == 3 + q) & (lane % GROUP == k), value, mix)
        decay.append(hold)
        cross.append(mix)
    for r in range(0, rows, 2):
        mixes = []
        for at in (r, r + 1):
            c = lat_ref[first + at]
            d, m = decay[0], cross[0]
            for other in range(1, NCLASS):
                d = jnp.where(c == other, decay[other], d)
                m = jnp.where(c == other, cross[other], m)
            decay_ref[pl.ds(at * GROUP, GROUP), :] = d
            mixes.append(jnp.where(lane // GROUP == at, m, 0.0))
        cross_ref[pl.ds(r * GROUP, 2 * GROUP), :] = jnp.concatenate(mixes, axis=0).astype(BF16)


def x_table_parts(rows, c, width, depth):
    get = class_reader(rows, c, depth)
    out_at = iota((width, depth), 0).astype(F32)
    lane = iota((width, depth), 1)
    in_at = lane.astype(F32)
    far = jnp.maximum(out_at, in_at)
    later = out_at >= in_at
    gap = jnp.abs(out_at - in_at)
    near_power = [jnp.exp(get(LOG + k) * gap) for k in range(3)]
    rest_power = [jnp.exp(get(LOG + k) * jnp.maximum(width - far, 0.0)) for k in range(3)]
    own_rest = [jnp.exp(get(LOG + k) * (width - out_at)) for k in range(3)]
    inner = jnp.zeros((width, depth), F32)
    carried = [jnp.zeros((width, depth), F32) for _ in range(3)]
    for q in range(3):
        for k in range(3):
            inverse = get(INV + 3 * q + k)
            inner += (get(FWD + k) * get(BWD + q) * inverse) * (
                jnp.where(later, near_power[k], near_power[q])
                * (1.0 - rest_power[k] * rest_power[q])
            )
            carried[k] += (get(BWD + q) * inverse) * (1.0 - own_rest[k] * own_rest[q])
    inner = jnp.where(lane < width, inner, 0.0)
    for k in range(3):
        carried[k] = carried[k] * jnp.exp(get(LOG + k) * (out_at + 1.0))
    return lane, inner, carried + own_rest


EXACT = dict(precision=lax.Precision.HIGHEST, preferred_element_type=F32)


def of_class(rows, lat, at):
    lanes = lat.shape[1]
    value = jnp.broadcast_to(rows[0][at][:, :lanes], lat.shape)
    for c in range(1, NCLASS):
        value = jnp.where(lat == c, rows[c][at][:, :lanes], value)
    return value


def over_points(rows):
    height = rows.shape[1]
    long = height * GROUP
    wider = (iota((height, long), 1) // GROUP == iota((height, long), 0)).astype(BF16)
    wide = jnp.dot(rows.astype(BF16), wider, preferred_element_type=F32)
    same = iota((GROUP, long), 1) % GROUP == iota((GROUP, long), 0)
    spread = [jnp.where(same, wide[q : q + 1], 0.0) for q in range(6)]
    return wide, jnp.concatenate(spread, axis=0).astype(BF16)


def tables_kernel(
    lengths_ref, lat_ref, m_ref, x_ref, y_ref, corner_ref,
    own_ref, ends_ref, local_ref, scan_ref,
):
    _, width, depth = m_ref.shape
    lanes = y_ref.shape[2]
    devices = y_ref.shape[1]
    height = lat_ref.shape[0] * lat_ref.shape[1] // devices
    rows = class_rows(lengths_ref, 2 * lanes)
    flat = lat_ref[...].astype(F32)
    flat = jnp.concatenate([flat[i : i + 1] for i in range(lat_ref.shape[0])], axis=1)
    lat = [flat[:, u * height : (u + 1) * height] for u in range(devices)]
    lat = jnp.concatenate(lat, axis=0)
    spread = jnp.zeros((width, depth), F32)
    for c in range(NCLASS):
        lane, inner, states = x_table_parts(rows, c, width, depth)
        for parity in range(2):
            table = inner
            for k in range(6):
                table = jnp.where(lane == width + GROUP * parity + k, states[k], table)
            m_ref[2 * c + parity] = table.astype(BF16)
        for k in range(6):
            spread = jnp.where(lane == c * GROUP + k, states[k], spread)
    x_ref[...] = spread[:, : x_ref.shape[1]].astype(BF16)

    def by_class(lat, at):
        return of_class(rows, lat, at)

    row, column = iota((height, height), 0), iota((height, height), 1)
    upto = (row <= column).astype(F32)
    logs = [by_class(lat, LOG + k) for k in range(3)]
    level = jnp.dot(jnp.concatenate(logs, axis=0), upto, **EXACT)
    levels = [level[k * devices : (k + 1) * devices] for k in range(3)]
    reach = [jnp.exp(levels[k]) for k in range(3)]
    cross = []
    for q in range(3):
        gain = by_class(lat, BWD + q) * jnp.exp(levels[q] - logs[q])
        for k in range(3):
            mixed = jnp.sum(gain * reach[k], axis=1, keepdims=True)
            cross.append(jnp.broadcast_to(mixed, (devices, lanes)))
    fill_y_tables(levels, cross, y_ref)

    mine = iota(lat.shape, 0) == lax.axis_index("ty")
    own = jnp.sum(jnp.where(mine, lat, 0.0), axis=0, keepdims=True)
    own = jnp.broadcast_to(own, (GROUP, height))
    fill_block_tables(rows, own, ends_ref, local_ref, scan_ref)
    _, _, ends, _, _, _, _ = two_passes(rows, own, row >= 0)
    total, own_ref[...] = over_points(ends)
    corner_ref[...] = total


def two_passes(rows, lat, same):
    height = lat.shape[1]
    lanes = 128
    kind = iota((GROUP, height), 0)
    row, column = iota((height, height), 0), iota((height, height), 1)
    log = jnp.zeros((GROUP, height), F32)
    forward = jnp.zeros((GROUP, height), F32)
    backward = jnp.zeros((GROUP, height), F32)
    for k in range(3):
        log = jnp.where(kind == k, of_class(rows, lat, LOG + k), log)
        forward = jnp.where(kind == k, of_class(rows, lat, FWD + k), forward)
        backward = jnp.where(kind == k, of_class(rows, lat, BWD + k), backward)
    turn = (((1,), (1,)), ((), ()))
    upto = jnp.dot(log, (same & (row <= column)).astype(F32), **EXACT)
    every = jnp.dot(log, same.astype(F32), **EXACT)
    before = upto - log
    upto_down = lax.dot_general((same & (column <= row)).astype(F32), log, turn, **EXACT)
    before_down = lax.dot_general((same & (column < row)).astype(F32), log, turn, **EXACT)
    every_down = lax.dot_general(same.astype(F32), log, turn, **EXACT)
    ahead = jnp.zeros((height, height), F32)
    back = jnp.zeros((height, height), F32)
    for k in range(3):
        gap = jnp.minimum(upto_down[:, k : k + 1] - upto[k : k + 1], 0.0)
        ahead += jnp.exp(gap) * forward[k : k + 1]
        gap = jnp.minimum(before[k : k + 1] - before_down[:, k : k + 1], 0.0)
        back += jnp.exp(gap) * backward[k : k + 1]
    ahead = jnp.where(same & (row >= column), ahead, 0.0)
    back = jnp.where(same & (row <= column), back, 0.0)

    gain = backward * jnp.exp(before)
    turned = jnp.dot(gain, ahead, **EXACT)
    ends = [(forward * jnp.exp(every - upto))[:3], turned[:3], lat[:1].astype(F32), lat[:1].astype(F32)]
    from_ahead = jnp.dot(back, jnp.exp(upto_down), **EXACT)
    from_back = jnp.exp(every_down - before_down)
    lane = iota((height, lanes), 1)
    entering = jnp.zeros((height, lanes), F32)
    for k in range(3):
        entering = jnp.where(lane % 48 // GROUP == k, from_ahead[:, k : k + 1], entering)
        entering = jnp.where(lane % 48 // GROUP == 3 + k, from_back[:, k : k + 1], entering)
    rest = entering - entering.astype(BF16).astype(F32)
    entering = jnp.where(lane < 48, entering, jnp.where(lane < 96, rest, 0.0)).astype(BF16)
    return ahead, back, jnp.concatenate(ends, axis=0), entering, gain, upto, every


def fill_block_tables(rows, lat, ends_ref, local_ref, scan_ref):
    height = lat.shape[1]
    blocks, _, lanes = scan_ref.shape
    same = iota((height, height), 0) // BLOCK == iota((height, height), 1) // BLOCK
    ahead, back, ends, entering, gain, upto, every = two_passes(rows, lat, same)
    _, ends_ref[...] = over_points(ends)

    reach = jnp.exp(upto)
    steps = [jnp.exp(every)[:3]]
    for q in range(3):
        steps.append(jnp.dot(gain[q : q + 1] * reach, same.astype(F32), **EXACT)[:3])
    steps = jnp.concatenate(steps + [jnp.zeros((4, height), F32)], axis=0)
    pick = (iota((height, lanes), 0) == iota((height, lanes), 1) * BLOCK).astype(F32)
    steps = jnp.dot(steps, pick, **EXACT)
    for block in range(blocks):
        scan_ref[block] = jnp.broadcast_to(steps[:, block : block + 1], steps.shape)

    inner = jnp.dot(back, ahead, **EXACT)
    fold = (iota((height, lanes), 0) % BLOCK == iota((height, lanes), 1) // GROUP).astype(BF16)
    inner = jnp.dot(inner.astype(BF16), fold, preferred_element_type=F32).astype(BF16)
    local_ref[...] = jnp.concatenate([inner, entering], axis=1)


def each_point(rows):
    count = rows.shape[0]
    long = count * GROUP
    taller = (iota((long, count), 0) // GROUP == iota((long, count), 1)).astype(BF16)
    whole = jnp.dot(taller, rows, preferred_element_type=F32)
    same_point = iota(whole.shape, 0) % GROUP == iota(whole.shape, 1) % GROUP
    return jnp.where(same_point, whole, 0.0).astype(BF16)


def fill_y_tables(levels, cross, y_ref):
    _, devices, lanes = y_ref.shape
    mine = lax.axis_index("ty")
    row = iota((devices, lanes), 0)
    before, upto, my_before, my_upto = [], [], [], []
    for k in range(3):
        level = jnp.broadcast_to(levels[k][:, -1:], (devices, lanes))
        total = jnp.zeros((devices, lanes), F32)
        for u in range(devices - 1):
            total += jnp.where(row > u, level[u : u + 1], 0.0)
        before.append(total)
        upto.append(total + level)
        my_before.append(jnp.sum(jnp.where(row == mine, total, 0.0), axis=0, keepdims=True))
        my_upto.append(jnp.sum(jnp.where(row == mine, total + level, 0.0), axis=0, keepdims=True))
        y_ref[12 + k] = jnp.broadcast_to(jnp.exp(my_upto[k] - my_before[k]), (devices, lanes))

    def decay(gap):
        return jnp.exp(jnp.minimum(gap, 0.0))

    for q in range(3):
        y_ref[q] = jnp.where(row < mine, decay(my_before[q] - upto[q]), 0.0)
        back = [decay(before[q][u : u + 1] - upto[q]) for u in range(devices)]
        for k in range(3):
            turned = jnp.zeros((devices, lanes), F32)
            for u in range(1, devices):
                ahead = decay(before[k][u : u + 1] - my_upto[k]) * cross[3 * q + k][u : u + 1]
                turned += jnp.where(mine < u, back[u] * ahead, 0.0)
            straight = decay(before[k] - my_upto[k]) if q == k else 0.0
            y_ref[3 + 3 * q + k] = jnp.where(row > mine, straight, turned)


def block_rows(step):
    lines = BLOCK * GROUP
    return pl.ds(pl.multiple_of(step * lines, lines), lines)


def store_points(wide_ref, row, pair):
    width, lanes = pair[0].shape
    at = pl.multiple_of(row * GROUP, 2 * GROUP)
    for piece in range(width // (2 * GROUP)):
        for half in range(2):
            rows = slice((2 * piece + half) * GROUP, (2 * piece + half + 1) * GROUP)
            both = jnp.concatenate([pair[0][rows], pair[1][rows]], axis=0)
            here = slice(half * lanes, (half + 1) * lanes)
            wide_ref[piece, pl.ds(at, 2 * GROUP), here] = both.astype(BF16)


def own_ends_kernel(
    lat_ref, v_ref, m_far, weight_far,
    e_ref, sum_ref, even_ref, odd_ref, here_ref, arrived, m_ref, weight_ref, fetched,
):
    height, width, lanes = v_ref.shape
    pieces = Pieces(v_ref, here_ref, arrived, 2 * BLOCK)
    wait = start_all([m_far, weight_far], [m_ref, weight_ref], fetched)
    pieces.start()
    tile = lax.axis_index("ty") * height
    sum_ref[...] = jnp.zeros_like(sum_ref)

    def along_x(step, block_ref):
        for r in range(0, BLOCK, 2):
            pair = []
            for at in (r, r + 1):
                row = step * BLOCK + at
                table = m_ref[2 * lat_ref[tile + row]][:, :width]
                pair.append(jnp.dot(table, here_ref[row], preferred_element_type=F32))
            store_points(block_ref, r, pair)

    def along_y(step, block_ref):
        weight = weight_ref[:, block_rows(step)]
        for piece in range(sum_ref.shape[0]):
            sum_ref[piece] += jnp.dot(weight, block_ref[piece], preferred_element_type=F32)

    wait()
    in_turn(pieces, along_x, along_y, even_ref, odd_ref)
    for piece in range(sum_ref.shape[0]):
        for half in range(2):
            for q in range(6):
                here = pl.ds((2 * piece + half) * GROUP, GROUP)
                part = sum_ref[piece, pl.ds(q * GROUP, GROUP), half * lanes : (half + 1) * lanes]
                e_ref[q, here, :] = part


def corner_kernel(corner_ref, c_ref, x_ref, own_ref, y_ref, send_ref, e_ref):
    group = x_ref.shape[1]
    devices = send_ref.shape[0]
    _, width, _ = own_ref.shape
    long = corner_ref.shape[1]
    pick = iota((group, long), 0)
    chosen = (corner_ref[pl.ds(6, 1), :] == (pick // GROUP).astype(F32)) & (
        iota((group, long), 1) % GROUP == pick % GROUP
    )
    corner = [jnp.where(chosen, corner_ref[pl.ds(q, 1), :], 0.0).astype(BF16) for q in range(6)]
    corner = jnp.concatenate(corner, axis=0)
    sums = jnp.dot(corner, c_ref[...], preferred_element_type=F32).astype(BF16)
    for q in range(6):
        part = sums[q * group : (q + 1) * group]
        e_ref[q] = own_ref[q] + jnp.dot(x_ref[...], part, preferred_element_type=F32)
    for at in range(0, width, CHUNK):
        ends = [e_ref[q, pl.ds(at, CHUNK), :] for q in range(6)]
        for u in range(devices):
            for q in range(3):
                total = y_ref[q, pl.ds(u, 1), :] * ends[3 + q]
                for k in range(3):
                    total += y_ref[3 + 3 * q + k, pl.ds(u, 1), :] * ends[k]
                send_ref[u, pl.ds(q * width + at, CHUNK), :] = total.astype(BF16)


def in_turn(pieces, produce, use, even_ref, odd_ref):
    steps = 2 * pieces.count
    pieces.copy(0).wait()
    produce(0, even_ref)

    def pair(i, _):
        pieces.copy(i + 1).wait()
        produce(2 * i + 1, odd_ref)
        use(2 * i, even_ref)
        produce(2 * i + 2, even_ref)
        use(2 * i + 1, odd_ref)
        return 0

    lax.fori_loop(0, pieces.count - 1, pair, 0)
    produce(steps - 1, odd_ref)
    use(steps - 2, even_ref)
    use(steps - 1, odd_ref)


def filter_kernel(
    lat_ref, v_ref, c_far, m_far, ends_far, after_ref,
    wide_far, end_far, c_ref, m_ref, ends_ref, fetched, even_ref, odd_ref, wide_ref, end_ref,
    here_ref, arrived, sent, end_sent,
):
    del after_ref
    height, width, lanes = v_ref.shape
    pieces = Pieces(v_ref, here_ref, arrived, 2 * BLOCK)
    results = Pieces(wide_ref, wide_far, sent, 1)
    end_results = Pieces(end_ref, end_far, end_sent, 1)
    wait = start_all([c_far, m_far, ends_far], [c_ref, m_ref, ends_ref], fetched)
    pieces.start()
    tile = lax.axis_index("ty") * height

    def along_x(step, block_ref):
        for r in range(0, BLOCK, 2):
            pair = []
            at = pl.multiple_of((step * BLOCK + r) * GROUP, 2 * GROUP)
            states = c_ref[pl.ds(at, 2 * GROUP), :]
            for parity in range(2):
                row = step * BLOCK + r + parity
                right = jnp.concatenate([here_ref[row], states], axis=0)
                table = m_ref[2 * lat_ref[tile + row] + parity]
                pair.append(jnp.dot(table, right, preferred_element_type=F32))
            store_points(block_ref, r, pair)

    def ends(step, block_ref):
        weight = ends_ref[:, block_rows(step)]
        for piece in range(wide_ref.shape[1]):
            block = block_ref[piece]
            wide_ref[step, piece] = block
            done = jnp.dot(weight, block, preferred_element_type=F32)
            end_ref[step, piece] = done.astype(BF16)
        results.copy(step).start()
        end_results.copy(step).start()

    wait()
    in_turn(pieces, along_x, ends, even_ref, odd_ref)
    results.wait()
    end_results.wait()


def y_carries(y_ref, arrived_ref, f_ref):
    devices = arrived_ref.shape[0]
    lanes = arrived_ref.shape[2]
    width = arrived_ref.shape[1] // 3
    mine = lax.axis_index("ty")
    mixed = [
        [
            y_ref[3 + 3 * q + k, pl.ds(mine, 1), :] * y_ref[12 + k, pl.ds(0, 1), :]
            for k in range(3)
        ]
        for q in range(3)
    ]
    for at in range(0, width, 2 * GROUP):
        ahead = [jnp.zeros((2 * GROUP, lanes), F32) for _ in range(3)]
        back = list(ahead)
        for u in range(devices):
            for q in range(3):
                came = arrived_ref[u, pl.ds(q * width + at, 2 * GROUP), :].astype(F32)
                ahead[q] += jnp.where(u < mine, came, 0.0)
                back[q] += jnp.where(u < mine, 0.0, came)
        states = list(ahead)
        for q in range(3):
            total = back[q]
            for k in range(3):
                total += mixed[q][k] * ahead[k]
            states.append(total)
        for half in range(2):
            for k in range(6):
                part = states[k][half * GROUP : (half + 1) * GROUP]
                place = pl.ds(k * GROUP, GROUP)
                f_ref[at // (2 * GROUP), place, half * lanes : (half + 1) * lanes] = part


def scan_blocks(scan_ref, end_ref, f_ref, ahead_ref, state_ref):
    steps, count, _, _ = end_ref.shape

    def at(k):
        return pl.ds(k * GROUP, GROUP)

    def factor(step, plane):
        row = scan_ref[step, pl.ds(plane, 1), :]
        return jnp.concatenate([row, row], axis=1)

    def two(step, piece, k):
        pair = end_ref[step, piece, pl.ds(k * GROUP, 2 * GROUP), :].astype(F32)
        return pair[:GROUP], pair[GROUP:]

    def ends_of(step, piece):
        return [part for k in range(0, 6, 2) for part in two(step, piece, k)]

    def forward(step, _):
        for piece in range(count):
            ends = ends_of(step, piece)
            for k in range(3):
                state = f_ref[piece, at(k), :]
                ahead_ref[step, piece, at(k), :] = state
                f_ref[piece, at(k), :] = factor(step, k) * state + ends[k]
        return 0

    def backward(i, _):
        step = steps - 1 - i
        for piece in range(count):
            ends = ends_of(step, piece)
            states = [ahead_ref[step, piece, at(k), :] for k in range(3)]
            for q in range(3):
                state = f_ref[piece, at(3 + q), :]
                states.append(state)
                total = factor(step, q) * state + ends[3 + q]
                for k in range(3):
                    total += factor(step, 3 + 3 * q + k) * states[k]
                f_ref[piece, at(3 + q), :] = total
            for k in range(0, 6, 2):
                pair = jnp.concatenate([states[k], states[k + 1]], axis=0)
                state_ref[step, piece, pl.ds(k * GROUP, 2 * GROUP), :] = pair.astype(BF16)
        return 0

    lax.fori_loop(0, steps, forward, 0)
    lax.fori_loop(0, steps, backward, 0)


def fill_held(owner, held_ref):
    slabs = owner.shape[1]
    across = jnp.broadcast_to(owner, (slabs, slabs))
    down = across.T
    row, lane = iota((slabs, slabs), 0), iota((slabs, slabs), 1)
    earlier = jnp.where((across == down) & (row < lane), 1.0, 0.0)
    rank = jnp.sum(earlier, axis=0, keepdims=True)
    for slot in range(MOST):
        held_ref[slot] = jnp.where((across == row.astype(F32)) & (rank == slot), 1.0, 0.0)


def whole_rows(left_ref, wide_ref, state_ref, step, sigma, take):
    _, count, lines, lanes = wide_ref.shape
    lanes //= 2
    left = left_ref[block_rows(step), :][:, : lines + 12 * GROUP]
    for piece in range(count):
        states = state_ref[step, piece]
        right = jnp.concatenate([wide_ref[step, piece], states, states], axis=0)
        result = jnp.dot(left, right, preferred_element_type=F32)
        here = pl.ds(piece * 2 * GROUP, 2 * GROUP)
        for r in range(BLOCK):
            part = result[r * GROUP : (r + 1) * GROUP]
            part = jnp.concatenate([part[:, :lanes], part[:, lanes:]], axis=0)
            take(step * BLOCK + r, here, part * sigma)


def final_kernel(
    y_far, wide_far, end_far, local_far, scan_far, owner_ref, sigma_ref, arrived_ref,
    out_ref, peak_ref, wide_ref, arrived, end_ref, y_ref, local_ref, scan_ref, fetched, fetched_small,
    held_ref, f_ref, ahead_ref, state_ref, done_ref, sent, left_ref,
):
    steps = wide_far.shape[0]
    lanes = peak_ref.shape[1]
    pieces = Pieces(wide_far, wide_ref, arrived, TURNS)
    results = Pieces(done_ref, out_ref, sent, TURNS * BLOCK)
    wait_small = start_all([local_far, y_far, scan_far], [local_ref, y_ref, scan_ref], fetched_small)
    wait = start_all([end_far], [end_ref], fetched)
    pieces.start()
    fill_held(owner_ref[...], held_ref)
    wait_small()
    lines = BLOCK * GROUP
    for step in range(steps):
        whole = each_point(local_ref[pl.ds(step * BLOCK, BLOCK), :])
        left_ref[pl.ds(step * lines, lines), :] = whole
    y_carries(y_ref, arrived_ref, f_ref)
    wait()
    scan_blocks(scan_ref, end_ref, f_ref, ahead_ref, state_ref)
    sigma = jnp.broadcast_to(sigma_ref[...], (2 * GROUP, lanes))

    def run(i, most):
        most = list(most)

        def take(row, here, scaled):
            at = len(taken) % 2
            taken.append(row)
            most[at] = jnp.maximum(most[at], jnp.abs(scaled))
            done_ref[row, here, :] = scaled.astype(BF16)

        taken = []
        pieces.copy(i).wait()
        for step in range(TURNS):
            whole_rows(left_ref, wide_ref, state_ref, TURNS * i + step, sigma, take)
        results.copy(i).start()
        return tuple(most)

    start = tuple(jnp.zeros((2 * GROUP, lanes), F32) for _ in range(2))
    most = lax.fori_loop(0, steps // TURNS, run, start)
    peaks = jnp.max(jnp.maximum(*most), axis=0, keepdims=True)
    lane = iota(peak_ref.shape, 1)
    rows = jnp.zeros(peak_ref.shape, F32)
    for slot in range(MOST):
        held = jnp.sum(held_ref[slot] * peaks, axis=1, keepdims=True)
        rows = jnp.where(lane == slot, held, rows)
    peak_ref[...] = rows
    results.wait()


SMEM = pl.BlockSpec(memory_space=pltpu.SMEM)
VMEM = pl.BlockSpec(memory_space=pltpu.VMEM)
HBM = pl.BlockSpec(memory_space=pltpu.HBM)
MIB = 1024 * 1024
FULL = 61
LAST = 55


def call(kernel, name, ins, outs, scratch, mib, us):
    return pl.pallas_call(
        kernel,
        in_specs=ins,
        out_specs=[spec for spec, _ in outs],
        out_shape=[array for _, array in outs],
        scratch_shapes=scratch,
        compiler_params=pltpu.CompilerParams(vmem_limit_bytes=mib * MIB),
        cost_estimate=pl.CostEstimate(flops=0, bytes_accessed=int(us * 3e6), transcendentals=0),
        name=name,
    )


def shape(*dims, kind=BF16):
    return jax.ShapeDtypeStruct(dims, kind)


def copies(count):
    return pltpu.SemaphoreType.DMA((count,))


def x_ends(lat_class, lengths, increments):
    height, width, lanes = increments.shape
    return call(
        ends_kernel,
        "x_ends",
        [SMEM, SMEM, HBM],
        [(VMEM, shape(height * GROUP, lanes))],
        [
            pltpu.VMEM((NCLASS * NCLASS, 2 * GROUP, width), BF16),
            pltpu.VMEM((height, width, lanes), BF16),
            copies(height // LONG),
        ],
        FULL,
        4,
    )(lat_class, lengths, increments)[0]


def tables(lengths, lat_class, count, width, lanes):
    height = lat_class.shape[0] // count
    return call(
        tables_kernel,
        "tables",
        [SMEM, VMEM],
        [
            (VMEM, shape(2 * NCLASS, width, width + 2 * GROUP)),
            (VMEM, shape(width, NCLASS * GROUP)),
            (VMEM, shape(15, count, lanes, kind=F32)),
            (VMEM, shape(GROUP, height * GROUP, kind=F32)),
            (VMEM, shape(6 * GROUP, height * GROUP)),
            (VMEM, shape(6 * GROUP, height * GROUP)),
            (VMEM, shape(height, 2 * lanes)),
            (VMEM, shape(height // BLOCK, 16, lanes, kind=F32)),
        ],
        [],
        FULL,
        6,
    )(lengths, lat_class.reshape(-1, lanes))


def own_y_ends(lat_class, increments, m_table, weights):
    height, width, lanes = increments.shape
    pieces = width // (2 * GROUP)
    block = pltpu.VMEM((pieces, BLOCK * GROUP, 2 * lanes), BF16)
    return call(
        own_ends_kernel,
        "own_y_ends",
        [SMEM, HBM, HBM, HBM],
        [(VMEM, shape(6, width, lanes, kind=F32))],
        [
            pltpu.VMEM((pieces, 6 * GROUP, 2 * lanes), F32),
            block,
            block,
            pltpu.VMEM((height, width, lanes), BF16),
            copies(height // (2 * BLOCK)),
            pltpu.VMEM(m_table.shape, m_table.dtype),
            pltpu.VMEM(weights.shape, weights.dtype),
            copies(2),
        ],
        FULL,
        6,
    )(lat_class, increments, m_table, weights)[0]


def x_scan(lat_class, lengths, ends, width, height):
    _, lines, lanes = ends.shape
    return call(
        functools.partial(scan_kernel, width, height),
        "x_scan",
        [SMEM, SMEM, VMEM],
        [(VMEM, shape(*ends.shape))],
        [pltpu.VMEM((lines, lanes), F32), pltpu.VMEM((lines, lanes), BF16), pltpu.VMEM(ends.shape, F32)],
        8,
        1,
    )(lat_class, lengths, ends)[0]


def y_ends(corner, states, x_table, own, y_table):
    _, width, lanes = own.shape
    return call(
        corner_kernel,
        "y_ends",
        [VMEM] * 5,
        [(VMEM, shape(y_table.shape[1], 3 * width, lanes))],
        [pltpu.VMEM((6, width, lanes), F32)],
        8,
        1,
    )(corner, states, x_table, own, y_table)[0]


def x_filter(lat_class, increments, states, m_table, ends, after):
    height, width, lanes = increments.shape
    pieces = width // (2 * GROUP)
    steps = height // BLOCK
    wide = (steps, pieces, BLOCK * GROUP, 2 * lanes)
    end = (steps, pieces, 6 * GROUP, 2 * lanes)
    return call(
        filter_kernel,
        "x_filter",
        [SMEM] + [HBM] * 5,
        [(HBM, shape(*wide)), (HBM, shape(*end))],
        [pltpu.VMEM(array.shape, array.dtype) for array in (states, m_table, ends)]
        + [
            copies(3),
            pltpu.VMEM(wide[1:], BF16),
            pltpu.VMEM(wide[1:], BF16),
            pltpu.VMEM(wide, BF16),
            pltpu.VMEM(end, BF16),
            pltpu.VMEM((height, width, lanes), BF16),
            copies(steps // 2),
            copies(steps),
            copies(steps),
        ],
        FULL,
        8,
    )(lat_class, increments, states, m_table, ends, after)


def tile_output(y_table, wide, ends, local, scan, owner, sigma, arrived, height, width):
    steps, pieces, lines, lanes = ends.shape
    half = lanes // 2
    return call(
        final_kernel,
        "tile_output",
        [HBM] * 5 + [VMEM] * 3,
        [(HBM, shape(height, width, half)), (VMEM, shape(half, half, kind=F32))],
        [
            pltpu.VMEM(wide.shape, wide.dtype),
            copies(steps // TURNS),
            pltpu.VMEM(ends.shape, ends.dtype),
            pltpu.VMEM(y_table.shape, y_table.dtype),
            pltpu.VMEM(local.shape, local.dtype),
            pltpu.VMEM(scan.shape, scan.dtype),
            copies(1),
            copies(3),
            pltpu.VMEM((MOST, half, half), F32),
            pltpu.VMEM((pieces, lines, lanes), F32),
            pltpu.VMEM((steps, pieces, lines // 2, lanes), F32),
            pltpu.VMEM(ends.shape, BF16),
            pltpu.VMEM((height, width, half), BF16),
            copies(steps // TURNS),
            pltpu.VMEM((height * GROUP, lanes), BF16),
        ],
        LAST,
        8,
    )(y_table, wide, ends, local, scan, owner, sigma, arrived)


def local(increments, lengths, lat_class, slab_owner, level_sigma):
    count_x = lax.axis_size("tx")
    count_y = lax.axis_size("ty")
    height, width, lanes = increments.shape
    lines = height // count_x * GROUP

    ends = x_ends(lat_class, lengths, increments)
    ends, lengths, lat_class = lax.optimization_barrier((ends, lengths, lat_class))
    with jax.named_scope("x_ends_to_scanners"):
        ends = lax.all_to_all(ends.reshape(count_x, lines, lanes), "tx", 0, 0, tiled=True)

    sigma = level_sigma.reshape(1, lanes)
    owner = slab_owner.astype(F32).reshape(1, lanes)
    (
        m_table, x_table, y_table, corner,
        weights, block_ends, block_local, block_scan,
    ) = tables(lengths, lat_class, count_y, width, lanes)

    ends, m_table = lax.optimization_barrier((ends, m_table))
    states = x_scan(lat_class, lengths, ends, width, height)
    with jax.named_scope("x_states_to_tiles"):
        states = lax.all_to_all(states, "tx", 0, 0, tiled=True).reshape(height * GROUP, lanes)
    own = own_y_ends(lat_class, increments, m_table, weights)

    sent = y_ends(corner, states, x_table, own, y_table)
    with jax.named_scope("y_ends_to_column"):
        arrived = lax.all_to_all(sent, "ty", 0, 0, tiled=True)
    wide, ends = x_filter(lat_class, increments, states, m_table, block_ends, sent)

    tile_out, peak_rows = tile_output(
        y_table, wide, ends, block_local, block_scan, owner, sigma, arrived, height, width
    )
    with jax.named_scope("peaks_to_owners"):
        peaks = lax.all_to_all(peak_rows, ("tx", "ty"), 0, 0, tiled=True)
    peak_table = jnp.max(peaks, axis=0, keepdims=True)[:, :MOST]
    return (tile_out, peak_table)


def solution(mesh):
    placed = (P("ty", "tx", None), P(), P(), P(), P())
    return jax.shard_map(
        local,
        mesh=mesh,
        in_specs=placed,
        out_specs=(P("ty", "tx", None), P(("tx", "ty"), None)),
        check_vma=False,
    )
```

```python
import functools

import jax
import jax.numpy as jnp
from jax import lax
from jax.experimental import pallas as pl
from jax.experimental.pallas import tpu as pltpu
from jax.sharding import PartitionSpec as P

NCLASS = 4
MOST = 2
SCALE_WEIGHTS = (0.5, 0.35, 0.25)
LOG, RATE, FWD, BWD, INV = 0, 3, 6, 9, 12
GROUP = 8
BLOCK = 16
LONG = 48
TURNS = 6
CHUNK = 48
F32, BF16 = jnp.float32, jnp.bfloat16


def iota(shape, axis):
    return lax.broadcasted_iota(jnp.int32, shape, axis)


def class_rows(lengths_ref, lanes):
    rows = []
    for c in range(NCLASS):
        log = [-1.0 / jnp.full((1, lanes), lengths_ref[c, k], F32) for k in range(3)]
        rate = [jnp.exp(log[k]) for k in range(3)]
        forward = [SCALE_WEIGHTS[k] * jnp.sqrt(1.0 - rate[k] * rate[k]) for k in range(3)]
        backward = [SCALE_WEIGHTS[k] * (1.0 - rate[k]) for k in range(3)]
        inverse = [1.0 / (1.0 - rate[k] * rate[q]) for q in range(3) for k in range(3)]
        rows.append(log + rate + forward + backward + inverse)
    return rows


class Pieces:
    def __init__(self, source, target, done, rows):
        self.source, self.target, self.done, self.rows = source, target, done, rows
        self.count = source.shape[0] // rows

    def copy(self, piece):
        rows = pl.ds(pl.multiple_of(piece * self.rows, self.rows), self.rows)
        return pltpu.make_async_copy(self.source.at[rows], self.target.at[rows], self.done.at[piece])

    def start(self, order=None):
        for piece in range(self.count) if order is None else order:
            self.copy(piece).start()

    def wait(self):
        for piece in range(self.count):
            self.copy(piece).wait()


def start_all(sources, targets, done):
    copies = [
        pltpu.make_async_copy(source, target, done.at[i])
        for i, (source, target) in enumerate(zip(sources, targets))
    ]
    for copy in copies:
        copy.start()

    def wait():
        for copy in copies:
            copy.wait()

    return wait


def class_reader(rows, c, lanes):
    return lambda at: rows[c][at][:, :lanes]


def ends_kernel(lat_ref, lengths_ref, v_ref, e_ref, w_ref, here_ref, arrived):
    height, width, lanes = v_ref.shape
    tile = lax.axis_index("ty") * height
    pieces = Pieces(v_ref, here_ref, arrived, LONG)
    pieces.start()
    shape = (GROUP, width)
    row = iota(shape, 0)
    at = iota(shape, 1).astype(F32)
    totals = []
    for c in range(NCLASS):
        log = [-1.0 / jnp.full(shape, lengths_ref[c, k], F32) for k in range(3)]
        rate = [jnp.exp(log[k]) for k in range(3)]
        fwd = [SCALE_WEIGHTS[k] * jnp.sqrt(1.0 - rate[k] * rate[k]) for k in range(3)]
        rest = [jnp.exp(log[k] * (width - at)) for k in range(3)]
        total = jnp.zeros(shape, F32)
        for k in range(3):
            fwd_end = fwd[k] * jnp.exp(log[k] * (width - 1 - at))
            total = jnp.where(row == k, fwd_end, total)
        for q in range(3):
            back = jnp.zeros(shape, F32)
            for k in range(3):
                back += fwd[k] * (1.0 - rest[k] * rest[q]) / (1.0 - rate[k] * rate[q])
            back = back * (SCALE_WEIGHTS[q] * (1.0 - rate[q])) * jnp.exp(log[q] * at)
            total = jnp.where(row == 3 + q, back, total)
        totals.append(total)
    for c in range(NCLASS):
        for d in range(NCLASS):
            w_ref[NCLASS * c + d] = jnp.concatenate([totals[c], totals[d]], axis=0).astype(BF16)

    def run(step, _):
        pieces.copy(step).wait()
        for r in range(0, LONG, 2):
            row = step * LONG + r
            pair = NCLASS * lat_ref[tile + row] + lat_ref[tile + row + 1]
            both = jnp.concatenate([here_ref[row], here_ref[row + 1]], axis=1)
            done = jnp.dot(w_ref[pair], both, preferred_element_type=F32)
            own = jnp.concatenate([done[:GROUP, :lanes], done[GROUP:, lanes:]], axis=0)
            at = pl.multiple_of(row * GROUP, 2 * GROUP)
            e_ref[pl.ds(at, 2 * GROUP), :] = own.astype(BF16)
        return 0

    lax.fori_loop(0, pieces.count, run, 0)


def scan_kernel(width, height, lat_ref, lengths_ref, e_ref, c_ref, decay_ref, cross_ref, f_ref):
    devices, lines, lanes = e_ref.shape
    fill_scan_tables(lat_ref, lengths_ref, width, height, decay_ref, cross_ref)
    decay = decay_ref[...]
    cross = cross_ref[:, :lines]
    state = jnp.zeros((lines, lanes), F32)
    for t in range(devices):
        f_ref[t] = state
        state = decay * state + e_ref[t].astype(F32)
    kind = iota((lines, lanes), 0) % GROUP
    state = jnp.zeros((lines, lanes), F32)
    for t in range(devices - 1, -1, -1):
        ahead = f_ref[t]
        c_ref[t] = jnp.where(kind < 3, ahead, jnp.where(kind < 6, state, 0.0)).astype(BF16)
        if t > 0:
            turned = jnp.dot(cross, ahead.astype(BF16), preferred_element_type=F32)
            state = decay * state + e_ref[t].astype(F32) + turned


def fill_scan_tables(lat_ref, lengths_ref, width, height, decay_ref, cross_ref):
    lines, lanes = decay_ref.shape
    rows = lines // GROUP
    first = lax.axis_index("ty") * height + lax.axis_index("tx") * rows
    row = iota((GROUP, lanes), 0)
    lane = iota((GROUP, lanes), 1)
    decay, cross = [], []
    for c in range(NCLASS):
        logs = [-1.0 / jnp.full((GROUP, lanes), lengths_ref[c, k], F32) for k in range(3)]
        rate = [jnp.exp(logs[k]) for k in range(3)]
        far = [jnp.exp(logs[k] * width) for k in range(3)]
        hold = jnp.zeros((GROUP, lanes), F32)
        mix = jnp.zeros((GROUP, lanes), F32)
        for k in range(3):
            hold = jnp.where((row == k) | (row == 3 + k), far[k], hold)
            for q in range(3):
                value = (SCALE_WEIGHTS[q] * (1.0 - rate[q])) * rate[k] * (
                    (1.0 - far[k] * far[q]) / (1.0 - rate[k] * rate[q])
                )
                mix = jnp.where((row == 3 + q) & (lane % GROUP == k), value, mix)
        decay.append(hold)
        cross.append(mix)
    for r in range(0, rows, 2):
        mixes = []
        for at in (r, r + 1):
            c = lat_ref[first + at]
            d, m = decay[0], cross[0]
            for other in range(1, NCLASS):
                d = jnp.where(c == other, decay[other], d)
                m = jnp.where(c == other, cross[other], m)
            decay_ref[pl.ds(at * GROUP, GROUP), :] = d
            mixes.append(jnp.where(lane // GROUP == at, m, 0.0))
        cross_ref[pl.ds(r * GROUP, 2 * GROUP), :] = jnp.concatenate(mixes, axis=0).astype(BF16)


def x_table_parts(rows, c, width, depth):
    get = class_reader(rows, c, depth)
    out_at = iota((width, depth), 0).astype(F32)
    lane = iota((width, depth), 1)
    in_at = lane.astype(F32)
    far = jnp.maximum(out_at, in_at)
    later = out_at >= in_at
    gap = jnp.abs(out_at - in_at)
    near_power = [jnp.exp(get(LOG + k) * gap) for k in range(3)]
    rest_power = [jnp.exp(get(LOG + k) * jnp.maximum(width - far, 0.0)) for k in range(3)]
    own_rest = [jnp.exp(get(LOG + k) * (width - out_at)) for k in range(3)]
    inner = jnp.zeros((width, depth), F32)
    carried = [jnp.zeros((width, depth), F32) for _ in range(3)]
    for q in range(3):
        for k in range(3):
            inverse = get(INV + 3 * q + k)
            inner += (get(FWD + k) * get(BWD + q) * inverse) * (
                jnp.where(later, near_power[k], near_power[q])
                * (1.0 - rest_power[k] * rest_power[q])
            )
            carried[k] += (get(BWD + q) * inverse) * (1.0 - own_rest[k] * own_rest[q])
    inner = jnp.where(lane < width, inner, 0.0)
    for k in range(3):
        carried[k] = carried[k] * jnp.exp(get(LOG + k) * (out_at + 1.0))
    return lane, inner, carried + own_rest


EXACT = dict(precision=lax.Precision.HIGHEST, preferred_element_type=F32)


def of_class(rows, lat, at):
    lanes = lat.shape[1]
    value = jnp.broadcast_to(rows[0][at][:, :lanes], lat.shape)
    for c in range(1, NCLASS):
        value = jnp.where(lat == c, rows[c][at][:, :lanes], value)
    return value


def over_points(rows):
    height = rows.shape[1]
    long = height * GROUP
    wider = (iota((height, long), 1) // GROUP == iota((height, long), 0)).astype(BF16)
    wide = jnp.dot(rows.astype(BF16), wider, preferred_element_type=F32)
    same = iota((GROUP, long), 1) % GROUP == iota((GROUP, long), 0)
    spread = [jnp.where(same, wide[q : q + 1], 0.0) for q in range(6)]
    return wide, jnp.concatenate(spread, axis=0).astype(BF16)


def tables_kernel(
    lengths_ref, lat_ref, m_ref, x_ref, y_ref, corner_ref,
    own_ref, ends_ref, local_ref, scan_ref,
):
    _, width, depth = m_ref.shape
    lanes = y_ref.shape[2]
    devices = y_ref.shape[1]
    height = lat_ref.shape[0] * lat_ref.shape[1] // devices
    rows = class_rows(lengths_ref, 2 * lanes)
    flat = lat_ref[...].astype(F32)
    flat = jnp.concatenate([flat[i : i + 1] for i in range(lat_ref.shape[0])], axis=1)
    lat = [flat[:, u * height : (u + 1) * height] for u in range(devices)]
    lat = jnp.concatenate(lat, axis=0)
    spread = jnp.zeros((width, depth), F32)
    for c in range(NCLASS):
        lane, inner, states = x_table_parts(rows, c, width, depth)
        for parity in range(2):
            table = inner
            for k in range(6):
                table = jnp.where(lane == width + GROUP * parity + k, states[k], table)
            m_ref[2 * c + parity] = table.astype(BF16)
        for k in range(6):
            spread = jnp.where(lane == c * GROUP + k, states[k], spread)
    x_ref[...] = spread[:, : x_ref.shape[1]].astype(BF16)

    def by_class(lat, at):
        return of_class(rows, lat, at)

    row, column = iota((height, height), 0), iota((height, height), 1)
    upto = (row <= column).astype(F32)
    logs = [by_class(lat, LOG + k) for k in range(3)]
    level = jnp.dot(jnp.concatenate(logs, axis=0), upto, **EXACT)
    levels = [level[k * devices : (k + 1) * devices] for k in range(3)]
    reach = [jnp.exp(levels[k]) for k in range(3)]
    cross = []
    for q in range(3):
        gain = by_class(lat, BWD + q) * jnp.exp(levels[q] - logs[q])
        for k in range(3):
            mixed = jnp.sum(gain * reach[k], axis=1, keepdims=True)
            cross.append(jnp.broadcast_to(mixed, (devices, lanes)))
    fill_y_tables(levels, cross, y_ref)

    mine = iota(lat.shape, 0) == lax.axis_index("ty")
    own = jnp.sum(jnp.where(mine, lat, 0.0), axis=0, keepdims=True)
    own = jnp.broadcast_to(own, (GROUP, height))
    fill_block_tables(rows, own, ends_ref, local_ref, scan_ref)
    _, _, ends, _, _, _, _ = two_passes(rows, own, row >= 0)
    total, own_ref[...] = over_points(ends)
    corner_ref[...] = total


def two_passes(rows, lat, same):
    height = lat.shape[1]
    lanes = 128
    kind = iota((GROUP, height), 0)
    row, column = iota((height, height), 0), iota((height, height), 1)
    log = jnp.zeros((GROUP, height), F32)
    forward = jnp.zeros((GROUP, height), F32)
    backward = jnp.zeros((GROUP, height), F32)
    for k in range(3):
        log = jnp.where(kind == k, of_class(rows, lat, LOG + k), log)
        forward = jnp.where(kind == k, of_class(rows, lat, FWD + k), forward)
        backward = jnp.where(kind == k, of_class(rows, lat, BWD + k), backward)
    turn = (((1,), (1,)), ((), ()))
    upto = jnp.dot(log, (same & (row <= column)).astype(F32), **EXACT)
    every = jnp.dot(log, same.astype(F32), **EXACT)
    before = upto - log
    upto_down = lax.dot_general((same & (column <= row)).astype(F32), log, turn, **EXACT)
    before_down = lax.dot_general((same & (column < row)).astype(F32), log, turn, **EXACT)
    every_down = lax.dot_general(same.astype(F32), log, turn, **EXACT)
    ahead = jnp.zeros((height, height), F32)
    back = jnp.zeros((height, height), F32)
    for k in range(3):
        gap = jnp.minimum(upto_down[:, k : k + 1] - upto[k : k + 1], 0.0)
        ahead += jnp.exp(gap) * forward[k : k + 1]
        gap = jnp.minimum(before[k : k + 1] - before_down[:, k : k + 1], 0.0)
        back += jnp.exp(gap) * backward[k : k + 1]
    ahead = jnp.where(same & (row >= column), ahead, 0.0)
    back = jnp.where(same & (row <= column), back, 0.0)

    gain = backward * jnp.exp(before)
    turned = jnp.dot(gain, ahead, **EXACT)
    ends = [(forward * jnp.exp(every - upto))[:3], turned[:3], lat[:1].astype(F32), lat[:1].astype(F32)]
    from_ahead = jnp.dot(back, jnp.exp(upto_down), **EXACT)
    from_back = jnp.exp(every_down - before_down)
    lane = iota((height, lanes), 1)
    entering = jnp.zeros((height, lanes), F32)
    for k in range(3):
        entering = jnp.where(lane % 48 // GROUP == k, from_ahead[:, k : k + 1], entering)
        entering = jnp.where(lane % 48 // GROUP == 3 + k, from_back[:, k : k + 1], entering)
    rest = entering - entering.astype(BF16).astype(F32)
    entering = jnp.where(lane < 48, entering, jnp.where(lane < 96, rest, 0.0)).astype(BF16)
    return ahead, back, jnp.concatenate(ends, axis=0), entering, gain, upto, every


def fill_block_tables(rows, lat, ends_ref, local_ref, scan_ref):
    height = lat.shape[1]
    blocks, _, lanes = scan_ref.shape
    same = iota((height, height), 0) // BLOCK == iota((height, height), 1) // BLOCK
    ahead, back, ends, entering, gain, upto, every = two_passes(rows, lat, same)
    _, ends_ref[...] = over_points(ends)

    reach = jnp.exp(upto)
    steps = [jnp.exp(every)[:3]]
    for q in range(3):
        steps.append(jnp.dot(gain[q : q + 1] * reach, same.astype(F32), **EXACT)[:3])
    steps = jnp.concatenate(steps + [jnp.zeros((4, height), F32)], axis=0)
    pick = (iota((height, lanes), 0) == iota((height, lanes), 1) * BLOCK).astype(F32)
    steps = jnp.dot(steps, pick, **EXACT)
    for block in range(blocks):
        scan_ref[block] = jnp.broadcast_to(steps[:, block : block + 1], steps.shape)

    inner = jnp.dot(back, ahead, **EXACT)
    fold = (iota((height, lanes), 0) % BLOCK == iota((height, lanes), 1) // GROUP).astype(BF16)
    inner = jnp.dot(inner.astype(BF16), fold, preferred_element_type=F32).astype(BF16)
    local_ref[...] = jnp.concatenate([inner, entering], axis=1)


def each_point(rows):
    count = rows.shape[0]
    long = count * GROUP
    taller = (iota((long, count), 0) // GROUP == iota((long, count), 1)).astype(BF16)
    whole = jnp.dot(taller, rows, preferred_element_type=F32)
    same_point = iota(whole.shape, 0) % GROUP == iota(whole.shape, 1) % GROUP
    return jnp.where(same_point, whole, 0.0).astype(BF16)


def fill_y_tables(levels, cross, y_ref):
    _, devices, lanes = y_ref.shape
    mine = lax.axis_index("ty")
    row = iota((devices, lanes), 0)
    before, upto, my_before, my_upto = [], [], [], []
    for k in range(3):
        level = jnp.broadcast_to(levels[k][:, -1:], (devices, lanes))
        total = jnp.zeros((devices, lanes), F32)
        for u in range(devices - 1):
            total += jnp.where(row > u, level[u : u + 1], 0.0)
        before.append(total)
        upto.append(total + level)
        my_before.append(jnp.sum(jnp.where(row == mine, total, 0.0), axis=0, keepdims=True))
        my_upto.append(jnp.sum(jnp.where(row == mine, total + level, 0.0), axis=0, keepdims=True))
        y_ref[12 + k] = jnp.broadcast_to(jnp.exp(my_upto[k] - my_before[k]), (devices, lanes))

    def decay(gap):
        return jnp.exp(jnp.minimum(gap, 0.0))

    for q in range(3):
        y_ref[q] = jnp.where(row < mine, decay(my_before[q] - upto[q]), 0.0)
        back = [decay(before[q][u : u + 1] - upto[q]) for u in range(devices)]
        for k in range(3):
            turned = jnp.zeros((devices, lanes), F32)
            for u in range(1, devices):
                ahead = decay(before[k][u : u + 1] - my_upto[k]) * cross[3 * q + k][u : u + 1]
                turned += jnp.where(mine < u, back[u] * ahead, 0.0)
            straight = decay(before[k] - my_upto[k]) if q == k else 0.0
            y_ref[3 + 3 * q + k] = jnp.where(row > mine, straight, turned)


def block_rows(step):
    lines = BLOCK * GROUP
    return pl.ds(pl.multiple_of(step * lines, lines), lines)


def store_points(wide_ref, row, pair):
    width, lanes = pair[0].shape
    at = pl.multiple_of(row * GROUP, 2 * GROUP)
    for piece in range(width // (2 * GROUP)):
        for half in range(2):
            rows = slice((2 * piece + half) * GROUP, (2 * piece + half + 1) * GROUP)
            both = jnp.concatenate([pair[0][rows], pair[1][rows]], axis=0)
            here = slice(half * lanes, (half + 1) * lanes)
            wide_ref[piece, pl.ds(at, 2 * GROUP), here] = both.astype(BF16)


def own_ends_kernel(
    lat_ref, v_ref, m_far, weight_far,
    e_ref, sum_ref, even_ref, odd_ref, here_ref, arrived, m_ref, weight_ref, fetched,
):
    height, width, lanes = v_ref.shape
    pieces = Pieces(v_ref, here_ref, arrived, 2 * BLOCK)
    wait = start_all([m_far, weight_far], [m_ref, weight_ref], fetched)
    pieces.start()
    tile = lax.axis_index("ty") * height
    sum_ref[...] = jnp.zeros_like(sum_ref)

    def along_x(step, block_ref):
        for r in range(0, BLOCK, 2):
            pair = []
            for at in (r, r + 1):
                row = step * BLOCK + at
                table = m_ref[2 * lat_ref[tile + row]][:, :width]
                pair.append(jnp.dot(table, here_ref[row], preferred_element_type=F32))
            store_points(block_ref, r, pair)

    def along_y(step, block_ref):
        weight = weight_ref[:, block_rows(step)]
        for piece in range(sum_ref.shape[0]):
            sum_ref[piece] += jnp.dot(weight, block_ref[piece], preferred_element_type=F32)

    wait()
    in_turn(pieces, along_x, along_y, even_ref, odd_ref)
    for piece in range(sum_ref.shape[0]):
        for half in range(2):
            for q in range(6):
                here = pl.ds((2 * piece + half) * GROUP, GROUP)
                part = sum_ref[piece, pl.ds(q * GROUP, GROUP), half * lanes : (half + 1) * lanes]
                e_ref[q, here, :] = part


def corner_kernel(corner_ref, c_ref, x_ref, own_ref, y_ref, send_ref, e_ref):
    group = x_ref.shape[1]
    devices = send_ref.shape[0]
    _, width, _ = own_ref.shape
    long = corner_ref.shape[1]
    pick = iota((group, long), 0)
    chosen = (corner_ref[pl.ds(6, 1), :] == (pick // GROUP).astype(F32)) & (
        iota((group, long), 1) % GROUP == pick % GROUP
    )
    corner = [jnp.where(chosen, corner_ref[pl.ds(q, 1), :], 0.0).astype(BF16) for q in range(6)]
    corner = jnp.concatenate(corner, axis=0)
    sums = jnp.dot(corner, c_ref[...], preferred_element_type=F32).astype(BF16)
    for q in range(6):
        part = sums[q * group : (q + 1) * group]
        e_ref[q] = own_ref[q] + jnp.dot(x_ref[...], part, preferred_element_type=F32)
    for at in range(0, width, CHUNK):
        ends = [e_ref[q, pl.ds(at, CHUNK), :] for q in range(6)]
        for u in range(devices):
            for q in range(3):
                total = y_ref[q, pl.ds(u, 1), :] * ends[3 + q]
                for k in range(3):
                    total += y_ref[3 + 3 * q + k, pl.ds(u, 1), :] * ends[k]
                send_ref[u, pl.ds(q * width + at, CHUNK), :] = total.astype(BF16)


def in_turn(pieces, produce, use, even_ref, odd_ref):
    steps = 2 * pieces.count
    pieces.copy(0).wait()
    produce(0, even_ref)

    def pair(i, _):
        pieces.copy(i + 1).wait()
        produce(2 * i + 1, odd_ref)
        use(2 * i, even_ref)
        produce(2 * i + 2, even_ref)
        use(2 * i + 1, odd_ref)
        return 0

    lax.fori_loop(0, pieces.count - 1, pair, 0)
    produce(steps - 1, odd_ref)
    use(steps - 2, even_ref)
    use(steps - 1, odd_ref)


def filter_kernel(
    lat_ref, v_ref, c_far, m_far, ends_far, after_ref,
    wide_far, end_far, c_ref, m_ref, ends_ref, fetched, even_ref, odd_ref, wide_ref, end_ref,
    here_ref, arrived, sent, end_sent,
):
    del after_ref
    height, width, lanes = v_ref.shape
    pieces = Pieces(v_ref, here_ref, arrived, 2 * BLOCK)
    results = Pieces(wide_ref, wide_far, sent, 1)
    end_results = Pieces(end_ref, end_far, end_sent, 1)
    wait = start_all([c_far, m_far, ends_far], [c_ref, m_ref, ends_ref], fetched)
    pieces.start()
    tile = lax.axis_index("ty") * height

    def along_x(step, block_ref):
        for r in range(0, BLOCK, 2):
            pair = []
            at = pl.multiple_of((step * BLOCK + r) * GROUP, 2 * GROUP)
            states = c_ref[pl.ds(at, 2 * GROUP), :]
            for parity in range(2):
                row = step * BLOCK + r + parity
                right = jnp.concatenate([here_ref[row], states], axis=0)
                table = m_ref[2 * lat_ref[tile + row] + parity]
                pair.append(jnp.dot(table, right, preferred_element_type=F32))
            store_points(block_ref, r, pair)

    def ends(step, block_ref):
        weight = ends_ref[:, block_rows(step)]
        for piece in range(wide_ref.shape[1]):
            block = block_ref[piece]
            wide_ref[step, piece] = block
            done = jnp.dot(weight, block, preferred_element_type=F32)
            end_ref[step, piece] = done.astype(BF16)
        results.copy(step).start()
        end_results.copy(step).start()

    wait()
    in_turn(pieces, along_x, ends, even_ref, odd_ref)
    results.wait()
    end_results.wait()


def y_carries(y_ref, arrived_ref, f_ref):
    devices = arrived_ref.shape[0]
    lanes = arrived_ref.shape[2]
    width = arrived_ref.shape[1] // 3
    mine = lax.axis_index("ty")
    mixed = [
        [
            y_ref[3 + 3 * q + k, pl.ds(mine, 1), :] * y_ref[12 + k, pl.ds(0, 1), :]
            for k in range(3)
        ]
        for q in range(3)
    ]
    for at in range(0, width, 2 * GROUP):
        ahead = [jnp.zeros((2 * GROUP, lanes), F32) for _ in range(3)]
        back = list(ahead)
        for u in range(devices):
            for q in range(3):
                came = arrived_ref[u, pl.ds(q * width + at, 2 * GROUP), :].astype(F32)
                ahead[q] += jnp.where(u < mine, came, 0.0)
                back[q] += jnp.where(u < mine, 0.0, came)
        states = list(ahead)
        for q in range(3):
            total = back[q]
            for k in range(3):
                total += mixed[q][k] * ahead[k]
            states.append(total)
        for half in range(2):
            for k in range(6):
                part = states[k][half * GROUP : (half + 1) * GROUP]
                place = pl.ds(k * GROUP, GROUP)
                f_ref[at // (2 * GROUP), place, half * lanes : (half + 1) * lanes] = part


def scan_blocks(scan_ref, end_ref, f_ref, ahead_ref, state_ref):
    steps, count, _, _ = end_ref.shape

    def at(k):
        return pl.ds(k * GROUP, GROUP)

    def factor(step, plane):
        row = scan_ref[step, pl.ds(plane, 1), :]
        return jnp.concatenate([row, row], axis=1)

    def two(step, piece, k):
        pair = end_ref[step, piece, pl.ds(k * GROUP, 2 * GROUP), :].astype(F32)
        return pair[:GROUP], pair[GROUP:]

    def ends_of(step, piece):
        return [part for k in range(0, 6, 2) for part in two(step, piece, k)]

    def forward(step, _):
        for piece in range(count):
            ends = ends_of(step, piece)
            for k in range(3):
                state = f_ref[piece, at(k), :]
                ahead_ref[step, piece, at(k), :] = state
                f_ref[piece, at(k), :] = factor(step, k) * state + ends[k]
        return 0

    def backward(i, _):
        step = steps - 1 - i
        for piece in range(count):
            ends = ends_of(step, piece)
            states = [ahead_ref[step, piece, at(k), :] for k in range(3)]
            for q in range(3):
                state = f_ref[piece, at(3 + q), :]
                states.append(state)
                total = factor(step, q) * state + ends[3 + q]
                for k in range(3):
                    total += factor(step, 3 + 3 * q + k) * states[k]
                f_ref[piece, at(3 + q), :] = total
            for k in range(0, 6, 2):
                pair = jnp.concatenate([states[k], states[k + 1]], axis=0)
                state_ref[step, piece, pl.ds(k * GROUP, 2 * GROUP), :] = pair.astype(BF16)
        return 0

    lax.fori_loop(0, steps, forward, 0)
    lax.fori_loop(0, steps, backward, 0)


def fill_held(owner, held_ref):
    slabs = owner.shape[1]
    across = jnp.broadcast_to(owner, (slabs, slabs))
    down = across.T
    row, lane = iota((slabs, slabs), 0), iota((slabs, slabs), 1)
    earlier = jnp.where((across == down) & (row < lane), 1.0, 0.0)
    rank = jnp.sum(earlier, axis=0, keepdims=True)
    for slot in range(MOST):
        held_ref[slot] = jnp.where((across == row.astype(F32)) & (rank == slot), 1.0, 0.0)


def whole_rows(left_ref, wide_ref, state_ref, step, sigma, take):
    _, count, lines, lanes = wide_ref.shape
    lanes //= 2
    left = left_ref[block_rows(step), :][:, : lines + 12 * GROUP]
    for piece in range(count):
        states = state_ref[step, piece]
        right = jnp.concatenate([wide_ref[step, piece], states, states], axis=0)
        result = jnp.dot(left, right, preferred_element_type=F32)
        here = pl.ds(piece * 2 * GROUP, 2 * GROUP)
        for r in range(BLOCK):
            part = result[r * GROUP : (r + 1) * GROUP]
            part = jnp.concatenate([part[:, :lanes], part[:, lanes:]], axis=0)
            take(step * BLOCK + r, here, part * sigma)


def final_kernel(
    y_far, wide_far, end_far, local_far, scan_far, owner_ref, sigma_ref, arrived_ref,
    out_ref, peak_ref, wide_ref, arrived, end_ref, y_ref, local_ref, scan_ref, fetched, fetched_small,
    held_ref, f_ref, ahead_ref, state_ref, done_ref, sent, left_ref,
):
    steps = wide_far.shape[0]
    lanes = peak_ref.shape[1]
    pieces = Pieces(wide_far, wide_ref, arrived, TURNS)
    results = Pieces(done_ref, out_ref, sent, TURNS // 2 * BLOCK)
    wait_small = start_all([local_far, y_far, scan_far], [local_ref, y_ref, scan_ref], fetched_small)
    wait = start_all([end_far], [end_ref], fetched)
    pieces.start()
    fill_held(owner_ref[...], held_ref)
    wait_small()
    lines = BLOCK * GROUP
    for step in range(steps):
        whole = each_point(local_ref[pl.ds(step * BLOCK, BLOCK), :])
        left_ref[pl.ds(step * lines, lines), :] = whole
    y_carries(y_ref, arrived_ref, f_ref)
    wait()
    scan_blocks(scan_ref, end_ref, f_ref, ahead_ref, state_ref)
    sigma = jnp.broadcast_to(sigma_ref[...], (2 * GROUP, lanes))

    def run(i, most):
        most = list(most)

        def take(row, here, scaled):
            at = len(taken) % 2
            taken.append(row)
            most[at] = jnp.maximum(most[at], jnp.abs(scaled))
            done_ref[row, here, :] = scaled.astype(BF16)

        taken = []
        pieces.copy(i).wait()
        for step in range(TURNS):
            whole_rows(left_ref, wide_ref, state_ref, TURNS * i + step, sigma, take)
            if step % (TURNS // 2) == TURNS // 2 - 1:
                results.copy(2 * i + step // (TURNS // 2)).start()
        return tuple(most)

    start = tuple(jnp.zeros((2 * GROUP, lanes), F32) for _ in range(2))
    most = lax.fori_loop(0, steps // TURNS, run, start)
    peaks = jnp.max(jnp.maximum(*most), axis=0, keepdims=True)
    lane = iota(peak_ref.shape, 1)
    rows = jnp.zeros(peak_ref.shape, F32)
    for slot in range(MOST):
        held = jnp.sum(held_ref[slot] * peaks, axis=1, keepdims=True)
        rows = jnp.where(lane == slot, held, rows)
    peak_ref[...] = rows
    results.wait()


SMEM = pl.BlockSpec(memory_space=pltpu.SMEM)
VMEM = pl.BlockSpec(memory_space=pltpu.VMEM)
HBM = pl.BlockSpec(memory_space=pltpu.HBM)
MIB = 1024 * 1024
FULL = 61
LAST = 55


def call(kernel, name, ins, outs, scratch, mib, us):
    return pl.pallas_call(
        kernel,
        in_specs=ins,
        out_specs=[spec for spec, _ in outs],
        out_shape=[array for _, array in outs],
        scratch_shapes=scratch,
        compiler_params=pltpu.CompilerParams(vmem_limit_bytes=mib * MIB),
        cost_estimate=pl.CostEstimate(flops=0, bytes_accessed=int(us * 3e6), transcendentals=0),
        name=name,
    )


def shape(*dims, kind=BF16):
    return jax.ShapeDtypeStruct(dims, kind)


def copies(count):
    return pltpu.SemaphoreType.DMA((count,))


def x_ends(lat_class, lengths, increments):
    height, width, lanes = increments.shape
    return call(
        ends_kernel,
        "x_ends",
        [SMEM, SMEM, HBM],
        [(VMEM, shape(height * GROUP, lanes))],
        [
            pltpu.VMEM((NCLASS * NCLASS, 2 * GROUP, width), BF16),
            pltpu.VMEM((height, width, lanes), BF16),
            copies(height // LONG),
        ],
        FULL,
        4,
    )(lat_class, lengths, increments)[0]


def tables(lengths, lat_class, count, width, lanes):
    height = lat_class.shape[0] // count
    return call(
        tables_kernel,
        "tables",
        [SMEM, VMEM],
        [
            (VMEM, shape(2 * NCLASS, width, width + 2 * GROUP)),
            (VMEM, shape(width, NCLASS * GROUP)),
            (VMEM, shape(15, count, lanes, kind=F32)),
            (VMEM, shape(GROUP, height * GROUP, kind=F32)),
            (VMEM, shape(6 * GROUP, height * GROUP)),
            (VMEM, shape(6 * GROUP, height * GROUP)),
            (VMEM, shape(height, 2 * lanes)),
            (VMEM, shape(height // BLOCK, 16, lanes, kind=F32)),
        ],
        [],
        FULL,
        6,
    )(lengths, lat_class.reshape(-1, lanes))


def own_y_ends(lat_class, increments, m_table, weights):
    height, width, lanes = increments.shape
    pieces = width // (2 * GROUP)
    block = pltpu.VMEM((pieces, BLOCK * GROUP, 2 * lanes), BF16)
    return call(
        own_ends_kernel,
        "own_y_ends",
        [SMEM, HBM, HBM, HBM],
        [(VMEM, shape(6, width, lanes, kind=F32))],
        [
            pltpu.VMEM((pieces, 6 * GROUP, 2 * lanes), F32),
            block,
            block,
            pltpu.VMEM((height, width, lanes), BF16),
            copies(height // (2 * BLOCK)),
            pltpu.VMEM(m_table.shape, m_table.dtype),
            pltpu.VMEM(weights.shape, weights.dtype),
            copies(2),
        ],
        FULL,
        6,
    )(lat_class, increments, m_table, weights)[0]


def x_scan(lat_class, lengths, ends, width, height):
    _, lines, lanes = ends.shape
    return call(
        functools.partial(scan_kernel, width, height),
        "x_scan",
        [SMEM, SMEM, VMEM],
        [(VMEM, shape(*ends.shape))],
        [pltpu.VMEM((lines, lanes), F32), pltpu.VMEM((lines, lanes), BF16), pltpu.VMEM(ends.shape, F32)],
        8,
        1,
    )(lat_class, lengths, ends)[0]


def y_ends(corner, states, x_table, own, y_table):
    _, width, lanes = own.shape
    return call(
        corner_kernel,
        "y_ends",
        [VMEM] * 5,
        [(VMEM, shape(y_table.shape[1], 3 * width, lanes))],
        [pltpu.VMEM((6, width, lanes), F32)],
        8,
        1,
    )(corner, states, x_table, own, y_table)[0]


def x_filter(lat_class, increments, states, m_table, ends, after):
    height, width, lanes = increments.shape
    pieces = width // (2 * GROUP)
    steps = height // BLOCK
    wide = (steps, pieces, BLOCK * GROUP, 2 * lanes)
    end = (steps, pieces, 6 * GROUP, 2 * lanes)
    return call(
        filter_kernel,
        "x_filter",
        [SMEM] + [HBM] * 5,
        [(HBM, shape(*wide)), (HBM, shape(*end))],
        [pltpu.VMEM(array.shape, array.dtype) for array in (states, m_table, ends)]
        + [
            copies(3),
            pltpu.VMEM(wide[1:], BF16),
            pltpu.VMEM(wide[1:], BF16),
            pltpu.VMEM(wide, BF16),
            pltpu.VMEM(end, BF16),
            pltpu.VMEM((height, width, lanes), BF16),
            copies(steps // 2),
            copies(steps),
            copies(steps),
        ],
        FULL,
        8,
    )(lat_class, increments, states, m_table, ends, after)


def tile_output(y_table, wide, ends, local, scan, owner, sigma, arrived, height, width):
    steps, pieces, lines, lanes = ends.shape
    half = lanes // 2
    return call(
        final_kernel,
        "tile_output",
        [HBM] * 5 + [VMEM] * 3,
        [(HBM, shape(height, width, half)), (VMEM, shape(half, half, kind=F32))],
        [
            pltpu.VMEM(wide.shape, wide.dtype),
            copies(steps // TURNS),
            pltpu.VMEM(ends.shape, ends.dtype),
            pltpu.VMEM(y_table.shape, y_table.dtype),
            pltpu.VMEM(local.shape, local.dtype),
            pltpu.VMEM(scan.shape, scan.dtype),
            copies(1),
            copies(3),
            pltpu.VMEM((MOST, half, half), F32),
            pltpu.VMEM((pieces, lines, lanes), F32),
            pltpu.VMEM((steps, pieces, lines // 2, lanes), F32),
            pltpu.VMEM(ends.shape, BF16),
            pltpu.VMEM((height, width, half), BF16),
            copies(2 * steps // TURNS),
            pltpu.VMEM((height * GROUP, lanes), BF16),
        ],
        LAST,
        8,
    )(y_table, wide, ends, local, scan, owner, sigma, arrived)


def local(increments, lengths, lat_class, slab_owner, level_sigma):
    count_x = lax.axis_size("tx")
    count_y = lax.axis_size("ty")
    height, width, lanes = increments.shape
    lines = height // count_x * GROUP

    ends = x_ends(lat_class, lengths, increments)
    ends, lengths, lat_class = lax.optimization_barrier((ends, lengths, lat_class))
    with jax.named_scope("x_ends_to_scanners"):
        ends = lax.all_to_all(ends.reshape(count_x, lines, lanes), "tx", 0, 0, tiled=True)

    sigma = level_sigma.reshape(1, lanes)
    owner = slab_owner.astype(F32).reshape(1, lanes)
    (
        m_table, x_table, y_table, corner,
        weights, block_ends, block_local, block_scan,
    ) = tables(lengths, lat_class, count_y, width, lanes)

    ends, m_table = lax.optimization_barrier((ends, m_table))
    states = x_scan(lat_class, lengths, ends, width, height)
    with jax.named_scope("x_states_to_tiles"):
        states = lax.all_to_all(states, "tx", 0, 0, tiled=True).reshape(height * GROUP, lanes)
    own = own_y_ends(lat_class, increments, m_table, weights)

    sent = y_ends(corner, states, x_table, own, y_table)
    with jax.named_scope("y_ends_to_column"):
        arrived = lax.all_to_all(sent, "ty", 0, 0, tiled=True)
    wide, ends = x_filter(lat_class, increments, states, m_table, block_ends, sent)

    tile_out, peak_rows = tile_output(
        y_table, wide, ends, block_local, block_scan, owner, sigma, arrived, height, width
    )
    with jax.named_scope("peaks_to_owners"):
        peaks = lax.all_to_all(peak_rows, ("tx", "ty"), 0, 0, tiled=True)
    peak_table = jnp.max(peaks, axis=0, keepdims=True)[:, :MOST]
    return (tile_out, peak_table)


def solution(mesh):
    placed = (P("ty", "tx", None), P(), P(), P(), P())
    return jax.shard_map(
        local,
        mesh=mesh,
        in_specs=placed,
        out_specs=(P("ty", "tx", None), P(("tx", "ty"), None)),
        check_vma=False,
    )
```
